32 devices in a mesh: groups: 2 (over x), rows: 16 (over z, y, core).
Axes of the slice: x: 2, y: 2, z: 4, core: 2. Of those that a mesh axis runs over, the one named last changes fastest.
Arguments:
- genotypes: bfloat16 [32768, 4096], P(('groups', 'rows')), parts along dimension 0, may hold values from -6 to 6
- sample_factors: float32 [32768, 64], P(('groups', 'rows')), parts along dimension 0, may hold values from -2.1213203 to 2.1213203
- snp_factors: float32 [20480, 64], P(('groups', 'rows')), parts along dimension 0, may hold values from -2.1213203 to 2.1213203
- coverage: int32 [32, 64], P('groups'), parts along dimension 0, may hold values from 0 to 159, as said below
Outputs:
- new_samples: float32 [32768, 64], P(('groups', 'rows')), parts along dimension 0
- new_snps: float32 [20480, 64], P(('groups', 'rows')), parts along dimension 0
The draws below stay inside these ranges and needn't reach their ends.
There are 2 independent parts, one for each index of `groups`. The reference program is written for one: setup_inputs(seed, part) draws one part's arguments, and reference() takes and returns one part's arrays. A program takes and returns all parts, laid end to end along the dimension named above; each array names one. Nothing has to cross between parts.
Inputs may be any that keep to these rules, and one draw needn't show every extreme that they name: `coverage`: each row lists 64 distinct SNP blocks in ascending order, exactly 4 of them among blocks o * 10 to (o + 1) * 10 - 1 for every o; every SNP block is listed by at least one batch.
All inputs are finite; a program needn't handle non-finite values.
Results may differ from the reference program's by a relative error of at most 0.0067.
Values may be sent and summed in bfloat16 or wider, within the bound.
No kernel may reach another device: no remote copies, remote signals or barrier semaphores. Data moves between devices by JAX's collectives and lax.ppermute only.
A program may use at most 128 MiB of HBM per device.

```python
import math
import jax
import jax.numpy as jnp
from jax import lax

R = 64
TILE = 64
SAMP_DEV = 1024
SNP_BLK_DEV = 10
PER_OWNER = 4
ROUNDS = 2
BATCHES = 16
SAMPLES = 16384
SNPS = 10240
COVER = 64


signal_terms = 4


def cover_rows(key):
    random_part = jax.random.randint(key, (BATCHES, BATCHES, SNP_BLK_DEV), 0, 65536)
    popular = jax.random.randint(jax.random.fold_in(key, 7), (1, BATCHES, SNP_BLK_DEV), 0, 3)
    shifted = jax.random.randint(jax.random.fold_in(key, 11), (1, BATCHES, 1), 0, SNP_BLK_DEV)
    batch_ids = jnp.arange(BATCHES, dtype=jnp.int32)[:, None, None]
    block_ids = jnp.arange(SNP_BLK_DEV, dtype=jnp.int32)[None, None, :]
    forced = ((batch_ids + shifted) % SNP_BLK_DEV == block_ids).astype(jnp.int32)
    scores = (random_part + popular * 65536 + forced * 1048576) * SNP_BLK_DEV + block_ids
    order = jnp.argsort(-scores, axis=-1)
    chosen = jnp.sort(order[:, :, :PER_OWNER], axis=-1).astype(jnp.int32)
    owners = jnp.arange(BATCHES, dtype=jnp.int32)[None, :, None] * SNP_BLK_DEV
    return (chosen + owners).reshape(BATCHES, BATCHES * PER_OWNER).astype(jnp.int32)


def sample_scores(key):
    return jax.random.normal(jax.random.fold_in(key, 201), (SAMPLES, signal_terms), jnp.float32)


def snp_loads(key):
    return jax.random.normal(jax.random.fold_in(key, 202), (SNPS, signal_terms), jnp.float32)


def rough_field(key, shape):
    return jax.random.normal(key, shape, jnp.float32)


def mixed_terms(left_side, right_side):
    summed = left_side[:, 0:1] * right_side[0:1, :]
    for which_term in range(1, signal_terms):
        summed = summed + left_side[:, which_term:which_term + 1] * right_side[which_term:which_term + 1, :]
    return summed * 0.5


def draw_coverage(key, part):
    return cover_rows(key)


def draw_genotypes(key, part):
    listed = cover_rows(key)
    shared_amp, block_amp, rough_amp = (0.7, 0.4, 0.59)
    scores = sample_scores(key).reshape(BATCHES, SAMP_DEV, signal_terms)
    loads = snp_loads(key)
    columns = (listed[:, :, None] * TILE + jnp.arange(TILE, dtype=jnp.int32)[None, None, :]).reshape(BATCHES, COVER * TILE)
    picked = loads[columns]
    shared = scores[:, :, 0:1] * picked[:, None, :, 0]
    for which_term in range(1, signal_terms):
        shared = shared + scores[:, :, which_term:which_term + 1] * picked[:, None, :, which_term]
    shared = shared * 0.5
    block_load = jax.random.normal(jax.random.fold_in(key, 205), (SNPS,), jnp.float32)[columns]
    block_score = jax.random.normal(jax.random.fold_in(key, 206), (BATCHES, SAMP_DEV, COVER), jnp.float32)
    haplotype = jnp.repeat(block_score, TILE, axis=2) * block_load[:, None, :]
    scatter = rough_field(jax.random.fold_in(key, 207), (BATCHES, SAMP_DEV, COVER * TILE))
    values = shared_amp * shared + block_amp * haplotype + rough_amp * scatter
    return jnp.clip(values, -6.0, 6.0).reshape(SAMPLES, COVER * TILE).astype(jnp.bfloat16)


def draw_sample_factors(key, part):
    scores = sample_scores(key)
    mixing = jax.random.normal(jax.random.fold_in(key, 203), (signal_terms, R), jnp.float32)
    scatter = rough_field(jax.random.fold_in(key, 209), (SAMPLES, R))
    values = R ** (-0.25) * (0.22 * mixed_terms(scores, mixing) + 0.97 * scatter)
    limit = 6.0 * R ** (-0.25)
    return jnp.clip(values, -limit, limit).astype(jnp.float32)


def draw_snp_factors(key, part):
    loads = snp_loads(key)
    mixing = jax.random.normal(jax.random.fold_in(key, 204), (signal_terms, R), jnp.float32)
    scatter = rough_field(jax.random.fold_in(key, 210), (SNPS, R))
    values = R ** (-0.25) * (0.25 * mixed_terms(loads, mixing) + 0.97 * scatter)
    limit = 6.0 * R ** (-0.25)
    return jnp.clip(values, -limit, limit).astype(jnp.float32)


def setup_inputs(seed: int = 0, part: int = 0) -> dict:
    streams_of = jax.random.split(jax.random.key(seed), 5)
    own_keys = jax.random.split(jax.random.fold_in(streams_of[4], part), 5)
    return {
        "genotypes": draw_genotypes(jax.random.fold_in(jax.random.fold_in(streams_of[4], part), 71), part),
        "sample_factors": draw_sample_factors(jax.random.fold_in(jax.random.fold_in(streams_of[4], part), 71), part),
        "snp_factors": draw_snp_factors(jax.random.fold_in(jax.random.fold_in(streams_of[4], part), 71), part),
        "coverage": draw_coverage(jax.random.fold_in(jax.random.fold_in(streams_of[4], part), 71), part),
    }


weight_decay = 0.02

def reference(genotypes, sample_factors, snp_factors, coverage):
    blocks_total = SNP_BLK_DEV * BATCHES
    listed_all = coverage.reshape(-1)
    observers = lax.optimization_barrier(jnp.sum((listed_all[:, None] == jnp.arange(blocks_total, dtype=jnp.int32)[None, :]).astype(jnp.float32), axis=0))
    snp_step = 0.5 * math.sqrt(R) / (SAMP_DEV * observers)
    sample_step = 0.5 * math.sqrt(R) / (COVER * TILE)
    geno = genotypes.reshape(BATCHES, SAMP_DEV, COVER * TILE)
    samples = sample_factors.reshape(BATCHES, SAMP_DEV, R)
    snps = snp_factors
    for iteration in range(ROUNDS):
        snp_bf16 = snps.astype(jnp.bfloat16).reshape(blocks_total, TILE, R)

        def update_rows(inputs):
            g_rows, factor_rows, listed = inputs
            panels = snp_bf16[listed.astype(jnp.int32)].reshape(COVER * TILE, R)
            predicted = lax.dot_general(factor_rows.astype(jnp.bfloat16), panels, (((1,), (1,)), ((), ())), preferred_element_type=jnp.float32)
            residual = (g_rows.astype(jnp.float32) - predicted).astype(jnp.bfloat16)
            gradient = jnp.dot(residual, panels, preferred_element_type=jnp.float32)
            return (1.0 - weight_decay) * factor_rows + sample_step * gradient
        samples = lax.map(update_rows, (geno, samples, coverage))
        sample_bf16 = samples.astype(jnp.bfloat16)

        def add_batch(total, inputs):
            g_rows, factor_bf16, listed = inputs
            panels = snp_bf16[listed.astype(jnp.int32)].reshape(COVER * TILE, R)
            predicted = lax.dot_general(factor_bf16, panels, (((1,), (1,)), ((), ())), preferred_element_type=jnp.float32)
            residual = (g_rows.astype(jnp.float32) - predicted).astype(jnp.bfloat16)
            contribution = lax.dot_general(residual, factor_bf16, (((0,), (0,)), ((), ())), preferred_element_type=jnp.float32)
            total = total.at[listed.astype(jnp.int32)].add(contribution.reshape(COVER, TILE, R))
            return (total, None)
        summed, unused = lax.scan(add_batch, jnp.zeros((blocks_total, TILE, R), jnp.float32), (geno, sample_bf16, coverage))
        snps = (1.0 - weight_decay) * snps + (snp_step[:, None, None] * summed).reshape(blocks_total * TILE, R)
    return (samples.reshape(SAMPLES, R), snps)
```

```python
import functools
import math

import jax
import jax.numpy as jnp
from jax import lax
from jax.experimental import pallas as pl
from jax.experimental.pallas import tpu as pltpu
from jax.sharding import PartitionSpec as P

ROUNDS = 2

weight_decay = 0.02

NT = (((1,), (1,)), ((), ()))
NN = (((1,), (0,)), ((), ()))
VMEM_LIMIT = 48 * 1024 * 1024


def dot(a, b, dims):
    return lax.dot_general(a, b, dims, preferred_element_type=jnp.float32)


def split3(x):
    hi = x.astype(jnp.bfloat16)
    rest = x - hi.astype(jnp.float32)
    mid = rest.astype(jnp.bfloat16)
    lo = (rest - mid.astype(jnp.float32)).astype(jnp.bfloat16)
    return hi, mid, lo


def low_half(rows):
    return lax.broadcasted_iota(jnp.int32, (rows, 128), 1) < 64


def double(x, low):
    turned = pltpu.roll(x, 64, 1)
    return jnp.where(low, x, turned), jnp.where(low, turned, x)


def write_sends(cov, pos, blocks, send, per_owner, own_blocks):
    batches, rank = send.shape[0], send.shape[1]
    low = low_half(rank)

    def batch(b, carry):
        for q in range(per_owner // 2):
            first = cov[b, pos * per_owner + 2 * q] - pos * own_blocks
            second = cov[b, pos * per_owner + 2 * q + 1] - pos * own_blocks
            pair = jnp.where(low, blocks[first], blocks[second])
            send[b, :, 128 * q:128 * (q + 1)] = pair.astype(send.dtype)
        return carry

    lax.fori_loop(0, batches, batch, 0, unroll=4)


def pack_kernel(per_owner, pos_ref, cov, snps, send, blocks):
    pos = pos_ref[0]
    own_blocks = blocks.shape[0]
    low = low_half(snps.shape[0])
    for j in range(own_blocks // 2):
        blocks[2 * j], blocks[2 * j + 1] = double(snps[:, 128 * j:128 * (j + 1)], low)
    write_sends(cov, pos, blocks, send, per_owner, own_blocks)


def owner_kernel(per_owner, last, pos_ref, cov, steps, incoming, snps, new_snps, *rest):
    pos = pos_ref[0]
    total = rest[-1]
    own_blocks = total.shape[0]
    batches, rank = incoming.shape[0], incoming.shape[1]
    low = low_half(rank)
    total[...] = jnp.zeros_like(total)

    def batch(b, carry):
        for q in range(per_owner // 2):
            first = cov[b, pos * per_owner + 2 * q] - pos * own_blocks
            second = cov[b, pos * per_owner + 2 * q + 1] - pos * own_blocks
            pair = incoming[b, :, 128 * q:128 * (q + 1)].astype(jnp.float32)
            total[first] += jnp.where(low, pair, 0.0)
            total[second] += jnp.where(low, 0.0, pair)
        return carry

    lax.fori_loop(0, batches, batch, 0, unroll=4)
    for j in range(own_blocks // 2):
        first, second = total[2 * j], total[2 * j + 1]
        first = (first + pltpu.roll(first, 64, 1)) * steps[2 * j]
        second = (second + pltpu.roll(second, 64, 1)) * steps[2 * j + 1]
        columns = slice(128 * j, 128 * (j + 1))
        updated = (1.0 - weight_decay) * snps[:, columns] + jnp.where(low, first, second)
        new_snps[:, columns] = updated
        if not last:
            total[2 * j], total[2 * j + 1] = double(updated, low)
    if not last:
        write_sends(cov, pos, total, rest[0], per_owner, own_blocks)


def batch_kernel(sample_step, geno, panels, samples, new_samples, terms, sums, panel_gram, sample_gram):
    step = pl.program_id(0)
    owners, rank, width = panels.shape

    @pl.when(step == 0)
    def _():
        gram = jnp.zeros((rank, rank), jnp.float32)
        for o in range(owners):
            gram += dot(panels[o], panels[o], NT)
        panel_gram[...] = gram
        sample_gram[...] = jnp.zeros_like(sample_gram)

    old = samples[...]
    old_bf16 = old.astype(jnp.bfloat16)
    gradient = jnp.zeros(old.shape, jnp.float32)
    for o in range(owners):
        gradient += dot(panels[o], geno[:, o * width:(o + 1) * width], NT)
    for part in split3(panel_gram[...]):
        gradient -= dot(part, old_bf16, NN)
    new = (1.0 - weight_decay) * old + sample_step * gradient
    new_samples[...] = new
    new_bf16 = new.astype(jnp.bfloat16)
    sample_gram[...] += dot(new_bf16, new_bf16, NT)

    @pl.when(step == 0)
    def _():
        for o in range(owners):
            sums[o] = dot(new_bf16, geno[:, o * width:(o + 1) * width], NN)

    @pl.when(step > 0)
    def _():
        for o in range(owners):
            sums[o] += dot(new_bf16, geno[:, o * width:(o + 1) * width], NN)

    @pl.when(step == pl.num_programs(0) - 1)
    def _():
        parts = split3(sample_gram[...])
        for o in range(owners):
            term = sums[o]
            for part in parts:
                term -= dot(part, panels[o], NN)
            terms[o] = term.astype(terms.dtype)


def on_device(genotypes, sample_factors, snp_factors, coverage):
    devices = lax.axis_size("rows")
    position = lax.axis_index("rows").astype(jnp.int32)
    samples_here = genotypes.shape[0]
    rank = sample_factors.shape[1]
    covered = coverage.shape[1]
    tile_size = genotypes.shape[1] // covered
    per_owner = covered // devices
    own_snps = snp_factors.shape[0]
    own_blocks = own_snps // tile_size
    width = per_owner * tile_size
    assert tile_size == 64 and per_owner % 2 == 0 and own_blocks % 2 == 0

    local_list = (
        lax.dynamic_slice_in_dim(coverage, position * per_owner, per_owner, 1)
        - position * own_blocks
    )
    one_hot = local_list[:, :, None] == jnp.arange(own_blocks, dtype=jnp.int32)[None, None, :]
    observers = jnp.sum(one_hot.astype(jnp.float32), axis=(0, 1))
    snp_step = 0.5 * math.sqrt(rank) / (samples_here * observers)
    sample_step = 0.5 * math.sqrt(rank) / (covered * tile_size)

    smem = pl.BlockSpec(memory_space=pltpu.SMEM)
    vmem = pl.BlockSpec(memory_space=pltpu.VMEM)
    params = pltpu.CompilerParams(vmem_limit_bytes=VMEM_LIMIT)
    pos = position.reshape(1)
    sends = jax.ShapeDtypeStruct((devices, rank, width), jnp.bfloat16)
    blocks = pltpu.VMEM((own_blocks, rank, 2 * tile_size), jnp.float32)

    pack = pl.pallas_call(
        functools.partial(pack_kernel, per_owner),
        out_shape=sends,
        in_specs=[smem, smem, vmem],
        out_specs=vmem,
        scratch_shapes=[blocks],
        compiler_params=params,
        name="pack_panels",
    )
    snps_shape = jax.ShapeDtypeStruct((rank, own_snps), jnp.float32)

    def owner_step(last):
        return pl.pallas_call(
            functools.partial(owner_kernel, per_owner, last),
            out_shape=snps_shape if last else (snps_shape, sends),
            in_specs=[smem, smem, smem, vmem, vmem],
            out_specs=vmem if last else (vmem, vmem),
            scratch_shapes=[blocks],
            compiler_params=params,
            name="owner_update_last" if last else "owner_update",
        )

    rows = 256
    batch_step = pl.pallas_call(
        functools.partial(batch_kernel, sample_step),
        grid=(samples_here // rows,),
        out_shape=(jax.ShapeDtypeStruct((rank, samples_here), jnp.float32), sends),
        in_specs=[
            pl.BlockSpec((rows, covered * tile_size), lambda i: (i, 0)),
            pl.BlockSpec((devices, rank, width), lambda i: (0, 0, 0)),
            pl.BlockSpec((rank, rows), lambda i: (0, i)),
        ],
        out_specs=(
            pl.BlockSpec((rank, rows), lambda i: (0, i)),
            pl.BlockSpec((devices, rank, width), lambda i: (0, 0, 0)),
        ),
        scratch_shapes=[
            pltpu.VMEM((devices, rank, width), jnp.float32),
            pltpu.VMEM((rank, rank), jnp.float32),
            pltpu.VMEM((rank, rank), jnp.float32),
        ],
        compiler_params=params,
        name="batch_step",
    )

    def exchange(x):
        return lax.all_to_all(x, "rows", split_axis=0, concat_axis=0, tiled=True)

    samples = sample_factors.T
    snps = snp_factors.T
    outgoing = pack(pos, coverage, snps)
    for iteration in range(ROUNDS):
        panels = exchange(outgoing)
        samples, terms = batch_step(genotypes, panels, samples)
        incoming = exchange(terms)
        if iteration == ROUNDS - 1:
            snps = owner_step(True)(pos, coverage, snp_step, incoming, snps)
        else:
            snps, outgoing = owner_step(False)(pos, coverage, snp_step, incoming, snps)
    return (samples.T, snps.T)


def solution(mesh):
    placed = (
        P(("groups", "rows"), None),
        P(("groups", "rows"), None),
        P(("groups", "rows"), None),
        P("groups", None),
    )
    return jax.shard_map(
        on_device,
        mesh=mesh,
        in_specs=placed,
        out_specs=(P(("groups", "rows"), None), P(("groups", "rows"), None)),
        check_vma=False,
    )
```

```python
import functools
import math

import jax
import jax.numpy as jnp
from jax import lax
from jax.experimental import pallas as pl
from jax.experimental.pallas import tpu as pltpu
from jax.sharding import PartitionSpec as P

ROUNDS = 2

weight_decay = 0.02

PLANE = 4
NT = (((1,), (1,)), ((), ()))
NN = (((1,), (0,)), ((), ()))
VMEM_LIMIT = 32 * 1024 * 1024


def dot(a, b, dims):
    return lax.dot_general(a, b, dims, preferred_element_type=jnp.float32)


def split3(x):
    hi = x.astype(jnp.bfloat16)
    rest = x - hi.astype(jnp.float32)
    mid = rest.astype(jnp.bfloat16)
    lo = (rest - mid.astype(jnp.float32)).astype(jnp.bfloat16)
    return hi, mid, lo


def low_half(rows):
    return lax.broadcasted_iota(jnp.int32, (rows, 128), 1) < 64


def double(x, low):
    turned = pltpu.roll(x, 64, 1)
    return jnp.where(low, x, turned), jnp.where(low, turned, x)


def owner_at(pos, planes, ahead, mate):
    plane = lax.rem(lax.shift_right_logical(pos, 2) + ahead, planes)
    return plane * PLANE + lax.bitwise_xor(lax.bitwise_and(pos, 3), mate)


def pick_kernel(planes, shifts, per_owner, own_blocks, pos_ref, cov, *refs):
    held, sends, blocks = refs[:len(shifts)], refs[len(shifts):-1], refs[-1]
    pos = pos_ref[0]
    rank = held[0].shape[0]
    low = low_half(rank)
    for i, shift in enumerate(shifts):
        for j in range(own_blocks // 2):
            x = held[i][:, 128 * j:128 * (j + 1)].astype(jnp.float32)
            blocks[i, 2 * j], blocks[i, 2 * j + 1] = double(x, low)
    for i, shift in enumerate(shifts):
        owner = owner_at(pos, planes, planes - shift, 0)
        for mate in range(PLANE):
            batch = owner_at(pos, planes, 0, mate)
            for q in range(per_owner // 2):
                first = cov[batch, owner * per_owner + 2 * q] - owner * own_blocks
                second = cov[batch, owner * per_owner + 2 * q + 1] - owner * own_blocks
                pair = jnp.where(low, blocks[i, first], blocks[i, second])
                sends[mate][i, :, 128 * q:128 * (q + 1)] = pair.astype(jnp.bfloat16)


def plane_sum_kernel(planes, shifts, per_owner, own_blocks, pos_ref, cov, *refs):
    terms, sums, total = refs[:PLANE], refs[PLANE:-1], refs[-1]
    pos = pos_ref[0]
    rank = terms[0].shape[1]
    low = low_half(rank)
    total[...] = jnp.zeros_like(total)
    for i, shift in enumerate(shifts):
        owner = owner_at(pos, planes, shift, 0)
        for mate in range(PLANE):
            batch = owner_at(pos, planes, 0, mate)
            for q in range(per_owner // 2):
                first = cov[batch, owner * per_owner + 2 * q] - owner * own_blocks
                second = cov[batch, owner * per_owner + 2 * q + 1] - owner * own_blocks
                pair = terms[mate][i, :, 128 * q:128 * (q + 1)].astype(jnp.float32)
                total[i, first] += jnp.where(low, pair, 0.0)
                total[i, second] += jnp.where(low, 0.0, pair)
    for i, shift in enumerate(shifts):
        for j in range(own_blocks // 2):
            first, second = total[i, 2 * j], total[i, 2 * j + 1]
            both = jnp.where(low, first, second) + pltpu.roll(jnp.where(low, second, first), 64, 1)
            sums[i][:, 128 * j:128 * (j + 1)] = both.astype(sums[i].dtype)


def batch_kernel(sample_step, planes, panel_at, term_at, pos_ref, geno, samples, *refs):
    step = pl.program_id(0)
    n_panels = 1 + max(ref for ref, _ in panel_at.values())
    panel_refs = refs[:n_panels]
    new_samples = refs[n_panels]
    terms = refs[n_panels + 1:-3]
    sums, panel_gram, sample_gram = refs[-3:]
    rank, width = panel_refs[0].shape[1], panel_refs[0].shape[2]
    pos = pos_ref[0]
    places = [(ahead, mate) for ahead in range(planes) for mate in range(PLANE)]

    def panel(place):
        ref, i = panel_at[place]
        return panel_refs[ref][i]

    def columns(place):
        start = owner_at(pos, planes, *place) * width
        return geno[:, pl.ds(pl.multiple_of(start, width), width)]

    @pl.when(step == 0)
    def _():
        gram = jnp.zeros((rank, rank), jnp.float32)
        for place in places:
            gram += dot(panel(place), panel(place), NT)
        panel_gram[...] = gram
        sample_gram[...] = jnp.zeros_like(sample_gram)

    old = samples[...]
    old_bf16 = old.astype(jnp.bfloat16)
    gradient = jnp.zeros(old.shape, jnp.float32)
    for place in places:
        gradient += dot(panel(place), columns(place), NT)
    for part in split3(panel_gram[...]):
        gradient -= dot(part, old_bf16, NN)
    new = (1.0 - weight_decay) * old + sample_step * gradient
    new_samples[...] = new
    new_bf16 = new.astype(jnp.bfloat16)
    sample_gram[...] += dot(new_bf16, new_bf16, NT)

    @pl.when(step == 0)
    def _():
        for o, place in enumerate(places):
            sums[o] = dot(new_bf16, columns(place), NN)

    @pl.when(step > 0)
    def _():
        for o, place in enumerate(places):
            sums[o] += dot(new_bf16, columns(place), NN)

    @pl.when(step == pl.num_programs(0) - 1)
    def _():
        parts = split3(sample_gram[...])
        for o, place in enumerate(places):
            term = sums[o]
            for part in parts:
                term -= dot(part, panel(place), NN)
            ref, i = term_at[place]
            terms[ref][i] = term.astype(jnp.bfloat16)


def on_device(genotypes, sample_factors, snp_factors, coverage):
    devices = lax.axis_size("rows")
    planes = devices // PLANE
    position = lax.axis_index("rows").astype(jnp.int32)
    samples_here = genotypes.shape[0]
    rank = sample_factors.shape[1]
    covered = coverage.shape[1]
    tile_size = genotypes.shape[1] // covered
    per_owner = covered // devices
    own_snps = snp_factors.shape[0]
    own_blocks = own_snps // tile_size
    width = per_owner * tile_size
    assert tile_size == 64 and per_owner % 2 == 0 and own_blocks % 2 == 0
    assert devices % PLANE == 0 and planes % 2 == 0

    local_list = (
        lax.dynamic_slice_in_dim(coverage, position * per_owner, per_owner, 1)
        - position * own_blocks
    )
    one_hot = local_list[:, :, None] == jnp.arange(own_blocks, dtype=jnp.int32)[None, None, :]
    observers = jnp.sum(one_hot.astype(jnp.float32), axis=(0, 1))
    snp_step = 0.5 * math.sqrt(rank) / (samples_here * observers)
    snp_step = jnp.broadcast_to(snp_step[:, None], (own_blocks, tile_size)).reshape(1, own_snps)
    sample_step = 0.5 * math.sqrt(rank) / (covered * tile_size)

    smem = pl.BlockSpec(memory_space=pltpu.SMEM)
    vmem = pl.BlockSpec(memory_space=pltpu.VMEM)
    params = pltpu.CompilerParams(vmem_limit_bytes=VMEM_LIMIT)
    pos = position.reshape(1)
    half = planes // 2
    out_groups = [list(range(half)), list(range(half, planes))]
    back_groups = [list(range(1, half + 1)), [0] + list(range(half + 1, planes))]
    packet = jax.ShapeDtypeStruct((half, rank, width), jnp.bfloat16)

    panel_at, term_at = {}, {}
    for g in range(2):
        for i in range(half):
            for mate in range(PLANE):
                panel_at[(planes - out_groups[g][i]) % planes, mate] = (g * PLANE + mate, i)
                term_at[back_groups[g][i], mate] = (g * PLANE + mate, i)

    def pick(shifts, held):
        return pl.pallas_call(
            functools.partial(pick_kernel, planes, shifts, per_owner, own_blocks),
            out_shape=(packet,) * PLANE,
            in_specs=[smem, smem] + [vmem] * half,
            out_specs=(vmem,) * PLANE,
            scratch_shapes=[pltpu.VMEM((half, own_blocks, rank, 128), jnp.float32)],
            compiler_params=params,
            name="pick_blocks",
        )(pos, coverage, *held)

    def plane_sum(shifts, terms):
        return pl.pallas_call(
            functools.partial(plane_sum_kernel, planes, shifts, per_owner, own_blocks),
            out_shape=tuple(
                jax.ShapeDtypeStruct((rank, own_snps), jnp.bfloat16 if shift else jnp.float32)
                for shift in shifts
            ),
            in_specs=[smem, smem] + [vmem] * PLANE,
            out_specs=(vmem,) * half,
            scratch_shapes=[pltpu.VMEM((half, own_blocks, rank, 128), jnp.float32)],
            compiler_params=params,
            name="plane_sum",
        )(pos, coverage, *terms)

    rows = 256
    whole_packet = pl.BlockSpec((half, rank, width), lambda i: (0, 0, 0))
    batch_step = pl.pallas_call(
        functools.partial(batch_kernel, sample_step, planes, panel_at, term_at),
        grid=(samples_here // rows,),
        out_shape=(jax.ShapeDtypeStruct((rank, samples_here), jnp.float32),) + (packet,) * (2 * PLANE),
        in_specs=[
            smem,
            pl.BlockSpec((rows, covered * tile_size), lambda i: (i, 0)),
            pl.BlockSpec((rank, rows), lambda i: (0, i)),
        ] + [whole_packet] * (2 * PLANE),
        out_specs=(pl.BlockSpec((rank, rows), lambda i: (0, i)),) + (whole_packet,) * (2 * PLANE),
        scratch_shapes=[
            pltpu.VMEM((devices, rank, width), jnp.float32),
            pltpu.VMEM((rank, rank), jnp.float32),
            pltpu.VMEM((rank, rank), jnp.float32),
        ],
        compiler_params=params,
        name="batch_step",
    )

    def along(x, shift):
        if shift == 0:
            return x
        pairs = [(r, ((r // PLANE + shift) % planes) * PLANE + r % PLANE) for r in range(devices)]
        return lax.ppermute(x, "rows", pairs)

    def to_mates(packets):
        return [packets[0]] + [
            lax.ppermute(packets[mate], "rows", [(r, r ^ mate) for r in range(devices)])
            for mate in range(1, PLANE)
        ]

    samples = sample_factors.T
    snps = snp_factors.T
    for iteration in range(ROUNDS):
        own = snps.astype(jnp.bfloat16)
        held = [along(own, shift) for shift in range(planes)]
        panels = []
        for group in out_groups:
            panels += to_mates(pick(group, [held[shift] for shift in group]))
        results = batch_step(pos, genotypes, samples, *panels)
        samples, terms = results[0], results[1:]
        summed = {}
        for g, group in enumerate(back_groups):
            sums = plane_sum(group, to_mates(terms[g * PLANE:(g + 1) * PLANE]))
            for shift, plane in zip(group, sums):
                summed[shift] = along(plane, shift)
        total = summed[0]
        for shift in range(1, planes):
            total = total + summed[shift].astype(jnp.float32)
        snps = (1.0 - weight_decay) * snps + snp_step * total
    return (samples.T, snps.T)


def solution(mesh):
    placed = (
        P(("groups", "rows"), None),
        P(("groups", "rows"), None),
        P(("groups", "rows"), None),
        P("groups", None),
    )
    return jax.shard_map(
        on_device,
        mesh=mesh,
        in_specs=placed,
        out_specs=(P(("groups", "rows"), None), P(("groups", "rows"), None)),
        check_vma=False,
    )
```

```python
import functools
import math

import jax
import jax.numpy as jnp
from jax import lax
from jax.experimental import pallas as pl
from jax.experimental.pallas import tpu as pltpu
from jax.sharding import PartitionSpec as P

ROUNDS = 2

weight_decay = 0.02

PLANE = 4
NT = (((1,), (1,)), ((), ()))
NN = (((1,), (0,)), ((), ()))
VMEM_LIMIT = 24 * 1024 * 1024


def dot(a, b, dims):
    return lax.dot_general(a, b, dims, preferred_element_type=jnp.float32)


def split3(x):
    hi = x.astype(jnp.bfloat16)
    rest = x - hi.astype(jnp.float32)
    mid = rest.astype(jnp.bfloat16)
    lo = (rest - mid.astype(jnp.float32)).astype(jnp.bfloat16)
    return hi, mid, lo


def low_half(rows):
    return lax.broadcasted_iota(jnp.int32, (rows, 128), 1) < 64


def double(x, low):
    turned = pltpu.roll(x, 64, 1)
    return jnp.where(low, x, turned), jnp.where(low, turned, x)


def owner_at(pos, planes, ahead, mate):
    plane = lax.rem(lax.shift_right_logical(pos, 2) + ahead, planes)
    return plane * PLANE + lax.bitwise_xor(lax.bitwise_and(pos, 3), mate)


def load_kernel(geno, samples, geno_out, samples_out, sems):
    copies = [
        pltpu.make_async_copy(samples, samples_out, sems.at[0]),
        pltpu.make_async_copy(geno, geno_out, sems.at[1]),
    ]
    for copy in copies:
        copy.start()
    for copy in copies:
        copy.wait()


def table_kernel(planes, per_owner, own_blocks, pos_ref, cov, table):
    pos = pos_ref[0]
    for mate in range(PLANE):
        batch = owner_at(pos, planes, 0, mate)
        for ahead in range(planes):
            owner = owner_at(pos, planes, ahead, 0)
            for p in range(per_owner):
                table[mate * planes + ahead, p] = cov[batch, owner * per_owner + p] - owner * own_blocks


def pick_kernel(planes, per_owner, own_blocks, table, *refs):
    held, packets, blocks = refs[:planes], refs[planes:-1], refs[-1]
    low = low_half(held[0].shape[0])
    for ahead in range(planes):
        for j in range(own_blocks // 2):
            x = held[ahead][:, 128 * j:128 * (j + 1)].astype(jnp.float32)
            blocks[ahead, 2 * j], blocks[ahead, 2 * j + 1] = double(x, low)
    for ahead in range(planes):
        for mate in range(PLANE):
            for q in range(per_owner // 2):
                first = table[mate * planes + ahead, 2 * q]
                second = table[mate * planes + ahead, 2 * q + 1]
                pair = jnp.where(low, blocks[ahead, first], blocks[ahead, second])
                packets[mate][ahead, :, 128 * q:128 * (q + 1)] = pair.astype(jnp.bfloat16)


def plane_sum_kernel(planes, per_owner, own_blocks, table, *refs):
    terms, sums, total = refs[:PLANE], refs[PLANE:-1], refs[-1]
    low = low_half(terms[0].shape[1])
    total[...] = jnp.zeros_like(total)
    for ahead in range(planes):
        for mate in range(PLANE):
            for q in range(per_owner // 2):
                first = table[mate * planes + ahead, 2 * q]
                second = table[mate * planes + ahead, 2 * q + 1]
                pair = terms[mate][ahead, :, 128 * q:128 * (q + 1)].astype(jnp.float32)
                total[ahead, first] += jnp.where(low, pair, 0.0)
                total[ahead, second] += jnp.where(low, 0.0, pair)
    for ahead in range(planes):
        for j in range(own_blocks // 2):
            first, second = total[ahead, 2 * j], total[ahead, 2 * j + 1]
            both = jnp.where(low, first, second) + pltpu.roll(jnp.where(low, second, first), 64, 1)
            sums[ahead][:, 128 * j:128 * (j + 1)] = both.astype(sums[ahead].dtype)


def columns_of(pos, planes, ahead, mate, width):
    return pl.ds(pl.multiple_of(owner_at(pos, planes, ahead, mate) * width, width), width)


def product_kernel(planes, mates, first, rows, pos_ref, geno, *refs):
    refs = list(refs)
    packets = [refs.pop(0) for _ in mates]
    before = None if first else (refs.pop(0), refs.pop(0))
    gradient, gram = refs
    pos = pos_ref[0]
    width = packets[0].shape[2]
    total = None if first else before[1][...]
    for packet in packets:
        for ahead in range(planes):
            term = dot(packet[ahead], packet[ahead], NT)
            total = term if total is None else total + term
    gram[...] = total
    for i in range(geno.shape[0] // rows):
        here = slice(i * rows, (i + 1) * rows)
        total = None if first else before[0][:, here]
        for mate, packet in zip(mates, packets):
            for ahead in range(planes):
                term = dot(packet[ahead], geno[here, columns_of(pos, planes, ahead, mate, width)], NT)
                total = term if total is None else total + term
        gradient[:, here] = total


def sample_kernel(sample_step, samples, gradient, gram, new_samples, new_bf16, new_gram):
    old = samples[...]
    old_bf16 = old.astype(jnp.bfloat16)
    total = gradient[...]
    for part in split3(gram[...]):
        total -= dot(part, old_bf16, NN)
    new = (1.0 - weight_decay) * old + sample_step * total
    new_samples[...] = new
    rounded = new.astype(jnp.bfloat16)
    new_bf16[...] = rounded
    new_gram[...] = dot(rounded, rounded, NT)


def term_kernel(planes, mate, pos_ref, geno, samples, gram, packet, terms):
    pos = pos_ref[0]
    width = packet.shape[2]
    parts = split3(gram[...])
    for ahead in range(planes):
        term = dot(samples[...], geno[:, columns_of(pos, planes, ahead, mate, width)], NN)
        for part in parts:
            term -= dot(part, packet[ahead], NN)
        terms[ahead] = term.astype(jnp.bfloat16)


def on_device(genotypes, sample_factors, snp_factors, coverage):
    devices = lax.axis_size("rows")
    planes = devices // PLANE
    position = lax.axis_index("rows").astype(jnp.int32)
    samples_here, snps_here = genotypes.shape
    rank = sample_factors.shape[1]
    covered = coverage.shape[1]
    tile_size = snps_here // covered
    per_owner = covered // devices
    own_snps = snp_factors.shape[0]
    own_blocks = own_snps // tile_size
    width = per_owner * tile_size
    assert tile_size == 64 and per_owner % 2 == 0 and own_blocks % 2 == 0
    assert devices % PLANE == 0

    local_list = (
        lax.dynamic_slice_in_dim(coverage, position * per_owner, per_owner, 1)
        - position * own_blocks
    )
    one_hot = local_list[:, :, None] == jnp.arange(own_blocks, dtype=jnp.int32)[None, None, :]
    observers = jnp.sum(one_hot.astype(jnp.float32), axis=(0, 1))
    snp_step = 0.5 * math.sqrt(rank) / (samples_here * observers)
    snp_step = jnp.broadcast_to(snp_step[:, None], (own_blocks, tile_size)).reshape(1, own_snps)
    sample_step = 0.5 * math.sqrt(rank) / (covered * tile_size)

    smem = pl.BlockSpec(memory_space=pltpu.SMEM)
    vmem = pl.BlockSpec(memory_space=pltpu.VMEM)
    hbm = pl.BlockSpec(memory_space=pltpu.HBM)
    params = pltpu.CompilerParams(vmem_limit_bytes=VMEM_LIMIT)
    pos = position.reshape(1)
    packet = jax.ShapeDtypeStruct((planes, rank, width), jnp.bfloat16)
    dense_blocks = pltpu.VMEM((planes, own_blocks, rank, 128), jnp.float32)
    by_samples = jax.ShapeDtypeStruct((rank, samples_here), jnp.float32)
    square = jax.ShapeDtypeStruct((rank, rank), jnp.float32)
    sizes = (planes, per_owner, own_blocks)

    def cost(flops, bytes_accessed):
        return pl.CostEstimate(flops=flops, bytes_accessed=bytes_accessed, transcendentals=0)

    table = pl.pallas_call(
        functools.partial(table_kernel, *sizes),
        out_shape=jax.ShapeDtypeStruct((PLANE * planes, per_owner), jnp.int32),
        in_specs=[smem, smem],
        out_specs=smem,
        compiler_params=params,
        name="block_table",
    )(pos, coverage)
    geno, samples = pl.pallas_call(
        load_kernel,
        out_shape=(
            pltpu.VMEM((samples_here, snps_here), jnp.bfloat16),
            pltpu.VMEM((rank, samples_here), jnp.float32),
        ),
        in_specs=[hbm, hbm],
        out_specs=(vmem, vmem),
        scratch_shapes=[pltpu.SemaphoreType.DMA((2,))],
        compiler_params=pltpu.CompilerParams(
            vmem_limit_bytes=58 * 1024 * 1024 - 2 * samples_here * snps_here
        ),
        cost_estimate=cost(0, 2 * samples_here * snps_here),
        name="load_batch",
    )(genotypes, sample_factors.T)

    def pick(held):
        return pl.pallas_call(
            functools.partial(pick_kernel, *sizes),
            out_shape=(packet,) * PLANE,
            in_specs=[smem] + [vmem] * planes,
            out_specs=(vmem,) * PLANE,
            scratch_shapes=[dense_blocks],
            compiler_params=params,
            name="pick_blocks",
        )(table, *held)

    def plane_sum(terms):
        return pl.pallas_call(
            functools.partial(plane_sum_kernel, *sizes),
            out_shape=tuple(
                jax.ShapeDtypeStruct((rank, own_snps), jnp.bfloat16 if ahead else jnp.float32)
                for ahead in range(planes)
            ),
            in_specs=[smem] + [vmem] * PLANE,
            out_specs=(vmem,) * planes,
            scratch_shapes=[dense_blocks],
            compiler_params=params,
            name="plane_sum",
        )(table, *terms)

    def product(mates, panels, before):
        share = len(mates) * samples_here * snps_here // PLANE
        return pl.pallas_call(
            functools.partial(product_kernel, planes, mates, before is None, 256),
            out_shape=(by_samples, square),
            in_specs=[smem] + [vmem] * (1 + len(mates) + (0 if before is None else 2)),
            out_specs=(vmem, vmem),
            compiler_params=params,
            cost_estimate=cost(8 * rank * share, 2 * share),
            name="panel_product",
        )(pos, geno, *[panels[mate] for mate in mates], *(before or ()))

    def sample_update(samples, gradient, gram):
        return pl.pallas_call(
            functools.partial(sample_kernel, sample_step),
            out_shape=(by_samples, jax.ShapeDtypeStruct((rank, samples_here), jnp.bfloat16), square),
            in_specs=[vmem] * 3,
            out_specs=(vmem,) * 3,
            compiler_params=params,
            name="sample_update",
        )(samples, gradient, gram)

    def terms_for(mate, samples_bf16, gram, panel):
        share = samples_here * snps_here // PLANE
        return pl.pallas_call(
            functools.partial(term_kernel, planes, mate),
            out_shape=packet,
            in_specs=[smem] + [vmem] * 4,
            out_specs=vmem,
            compiler_params=params,
            cost_estimate=cost(8 * rank * share, 2 * share),
            name="mate_terms",
        )(pos, geno, samples_bf16, gram, panel)

    def along(x, shift):
        if shift % planes == 0:
            return x
        pairs = [(r, ((r // PLANE + shift) % planes) * PLANE + r % PLANE) for r in range(devices)]
        return lax.ppermute(x, "rows", pairs)

    def to_mate(x, mate):
        if mate == 0:
            return x
        return lax.ppermute(x, "rows", [(r, r ^ mate) for r in range(devices)])

    snps = snp_factors.T
    for iteration in range(ROUNDS):
        own = snps.astype(jnp.bfloat16)
        held = [along(own, planes - ahead) for ahead in range(planes)]
        packets = pick(held)
        panels = [to_mate(packets[mate], mate) for mate in range(PLANE)]
        partial = product([0], panels, None)
        partial = product([1], panels, partial)
        partial = product([2, 3], panels, partial)
        samples, samples_bf16, sample_gram = sample_update(samples, *partial)
        terms = [None] * PLANE
        for mate in (2, 3, 1, 0):
            terms[mate] = to_mate(terms_for(mate, samples_bf16, sample_gram, panels[mate]), mate)
        sums = plane_sum(terms)
        total = sums[0]
        for ahead in range(1, planes):
            total = total + along(sums[ahead], ahead).astype(jnp.float32)
        snps = (1.0 - weight_decay) * snps + snp_step * total
    return (samples.T, snps.T)


def solution(mesh):
    placed = (
        P(("groups", "rows"), None),
        P(("groups", "rows"), None),
        P(("groups", "rows"), None),
        P("groups", None),
    )
    return jax.shard_map(
        on_device,
        mesh=mesh,
        in_specs=placed,
        out_specs=(P(("groups", "rows"), None), P(("groups", "rows"), None)),
        check_vma=False,
    )
```

```python
import functools
import math

import jax
import jax.numpy as jnp
from jax import lax
from jax.experimental import pallas as pl
from jax.experimental.pallas import tpu as pltpu
from jax.sharding import PartitionSpec as P

ROUNDS = 2

weight_decay = 0.02

PLANE = 4
NT = (((1,), (1,)), ((), ()))
NN = (((1,), (0,)), ((), ()))
VMEM_LIMIT = 24 * 1024 * 1024


def dot(a, b, dims):
    return lax.dot_general(a, b, dims, preferred_element_type=jnp.float32)


def split3(x):
    hi = x.astype(jnp.bfloat16)
    rest = x - hi.astype(jnp.float32)
    mid = rest.astype(jnp.bfloat16)
    lo = (rest - mid.astype(jnp.float32)).astype(jnp.bfloat16)
    return hi, mid, lo


def low_half(rows):
    return lax.broadcasted_iota(jnp.int32, (rows, 128), 1) < 64


def double(x, low):
    turned = pltpu.roll(x, 64, 1)
    return jnp.where(low, x, turned), jnp.where(low, turned, x)


def owner_at(pos, planes, ahead, mate):
    plane = lax.rem(lax.shift_right_logical(pos, 2) + ahead, planes)
    return plane * PLANE + lax.bitwise_xor(lax.bitwise_and(pos, 3), mate)


def load_kernel(geno, samples, geno_out, samples_out, sems):
    copies = [
        pltpu.make_async_copy(samples, samples_out, sems.at[0]),
        pltpu.make_async_copy(geno, geno_out, sems.at[1]),
    ]
    for copy in copies:
        copy.start()
    for copy in copies:
        copy.wait()


def table_kernel(planes, per_owner, own_blocks, pos_ref, cov, table):
    pos = pos_ref[0]
    for mate in range(PLANE):
        batch = owner_at(pos, planes, 0, mate)
        for ahead in range(planes):
            owner = owner_at(pos, planes, ahead, 0)
            for p in range(per_owner):
                table[mate * planes + ahead, p] = cov[batch, owner * per_owner + p] - owner * own_blocks


def write_sends(cov, pos, blocks, send, per_owner):
    own_blocks = blocks.shape[0]
    low = low_half(blocks.shape[1])

    def batch(b, carry):
        for q in range(per_owner // 2):
            first = cov[b, pos * per_owner + 2 * q] - pos * own_blocks
            second = cov[b, pos * per_owner + 2 * q + 1] - pos * own_blocks
            pair = jnp.where(low, blocks[first], blocks[second])
            send[b, :, 128 * q:128 * (q + 1)] = pair.astype(send.dtype)
        return carry

    lax.fori_loop(0, send.shape[0], batch, 0, unroll=4)


def pack_kernel(per_owner, pos_ref, cov, snps, send, upper, blocks):
    own_blocks, rows = blocks.shape[0], blocks.shape[1]
    low = low_half(rows)
    upper[...] = snps[rows:, :]
    for j in range(own_blocks // 2):
        blocks[2 * j], blocks[2 * j + 1] = double(snps[rows:, 128 * j:128 * (j + 1)], low)
    write_sends(cov, pos_ref[0], blocks, send, per_owner)


def owner_kernel(per_owner, last, pos_ref, cov, steps, incoming, snps, new_snps, *rest):
    pos = pos_ref[0]
    total = rest[-1]
    own_blocks = total.shape[0]
    low = low_half(total.shape[1])
    total[...] = jnp.zeros_like(total)

    def batch(b, carry):
        for q in range(per_owner // 2):
            first = cov[b, pos * per_owner + 2 * q] - pos * own_blocks
            second = cov[b, pos * per_owner + 2 * q + 1] - pos * own_blocks
            pair = incoming[b, :, 128 * q:128 * (q + 1)].astype(jnp.float32)
            total[first] += jnp.where(low, pair, 0.0)
            total[second] += jnp.where(low, 0.0, pair)
        return carry

    lax.fori_loop(0, incoming.shape[0], batch, 0, unroll=4)
    for j in range(own_blocks // 2):
        first, second = total[2 * j], total[2 * j + 1]
        first = (first + pltpu.roll(first, 64, 1)) * steps[2 * j]
        second = (second + pltpu.roll(second, 64, 1)) * steps[2 * j + 1]
        columns = slice(128 * j, 128 * (j + 1))
        updated = (1.0 - weight_decay) * snps[:, columns] + jnp.where(low, first, second)
        new_snps[:, columns] = updated
        if not last:
            total[2 * j], total[2 * j + 1] = double(updated, low)
    if not last:
        write_sends(cov, pos, total, rest[0], per_owner)


def pick_kernel(planes, per_owner, own_blocks, table, *refs):
    held, packets, blocks = refs[:planes], refs[planes:-1], refs[-1]
    low = low_half(held[0].shape[0])
    for ahead in range(planes):
        for j in range(own_blocks // 2):
            x = held[ahead][:, 128 * j:128 * (j + 1)].astype(jnp.float32)
            blocks[ahead, 2 * j], blocks[ahead, 2 * j + 1] = double(x, low)
    for ahead in range(planes):
        for mate in range(PLANE):
            for q in range(per_owner // 2):
                first = table[mate * planes + ahead, 2 * q]
                second = table[mate * planes + ahead, 2 * q + 1]
                pair = jnp.where(low, blocks[ahead, first], blocks[ahead, second])
                packets[mate][ahead, :, 128 * q:128 * (q + 1)] = pair.astype(jnp.bfloat16)


def plane_sum_kernel(planes, per_owner, own_blocks, table, *refs):
    terms, sums, total = refs[:PLANE], refs[PLANE:-1], refs[-1]
    low = low_half(terms[0].shape[1])
    total[...] = jnp.zeros_like(total)
    for ahead in range(planes):
        for mate in range(PLANE):
            for q in range(per_owner // 2):
                first = table[mate * planes + ahead, 2 * q]
                second = table[mate * planes + ahead, 2 * q + 1]
                pair = terms[mate][ahead, :, 128 * q:128 * (q + 1)].astype(jnp.float32)
                total[ahead, first] += jnp.where(low, pair, 0.0)
                total[ahead, second] += jnp.where(low, 0.0, pair)
    for ahead in range(planes):
        for j in range(own_blocks // 2):
            first, second = total[ahead, 2 * j], total[ahead, 2 * j + 1]
            both = jnp.where(low, first, second) + pltpu.roll(jnp.where(low, second, first), 64, 1)
            sums[ahead][:, 128 * j:128 * (j + 1)] = both.astype(sums[ahead].dtype)


def columns_of(pos, planes, ahead, mate, width):
    return pl.ds(pl.multiple_of(owner_at(pos, planes, ahead, mate) * width, width), width)


def panel_of(pos, planes, ahead, mate, packet, upper):
    return jnp.concatenate([packet[ahead], upper[owner_at(pos, planes, ahead, mate)]], axis=0)


def product_kernel(planes, mates, first, rows, pos_ref, geno, upper, *refs):
    refs = list(refs)
    packets = [refs.pop(0) for _ in mates]
    before = None if first else (refs.pop(0), refs.pop(0))
    gradient, gram = refs
    pos = pos_ref[0]
    width = packets[0].shape[2]
    places = [(mate, packet, ahead) for mate, packet in zip(mates, packets) for ahead in range(planes)]
    panels = [panel_of(pos, planes, ahead, mate, packet, upper) for mate, packet, ahead in places]
    total = None if first else before[1][...]
    for panel in panels:
        term = dot(panel, panel, NT)
        total = term if total is None else total + term
    gram[...] = total
    for i in range(geno.shape[0] // rows):
        here = slice(i * rows, (i + 1) * rows)
        total = None if first else before[0][:, here]
        for (mate, packet, ahead), panel in zip(places, panels):
            term = dot(panel, geno[here, columns_of(pos, planes, ahead, mate, width)], NT)
            total = term if total is None else total + term
        gradient[:, here] = total


def sample_kernel(sample_step, samples, gradient, gram, new_samples, new_bf16, new_gram):
    old = samples[...]
    old_bf16 = old.astype(jnp.bfloat16)
    total = gradient[...]
    for part in split3(gram[...]):
        total -= dot(part, old_bf16, NN)
    new = (1.0 - weight_decay) * old + sample_step * total
    new_samples[...] = new
    rounded = new.astype(jnp.bfloat16)
    new_bf16[...] = rounded
    new_gram[...] = dot(rounded, rounded, NT)


def term_kernel(planes, mate, others, pos_ref, geno, samples, gram, packet, upper, *refs):
    terms, direct = refs[-2:]
    pos = pos_ref[0]
    half, width = packet.shape[1], packet.shape[2]
    parts = split3(gram[...])
    for ahead in range(planes):
        panel = panel_of(pos, planes, ahead, mate, packet, upper)
        term = dot(samples[...], geno[:, columns_of(pos, planes, ahead, mate, width)], NN)
        for part in parts:
            term -= dot(part, panel, NN)
        term = term.astype(jnp.bfloat16)
        terms[ahead] = term[:half]
        if others:
            direct[owner_at(pos, planes, ahead, mate)] = term[half:]
            for other, piece in zip(others, refs):
                direct[owner_at(pos, planes, ahead, other)] = piece[ahead]
        else:
            direct[ahead] = term[half:]


def on_device(genotypes, sample_factors, snp_factors, coverage):
    devices = lax.axis_size("rows")
    planes = devices // PLANE
    position = lax.axis_index("rows").astype(jnp.int32)
    samples_here, snps_here = genotypes.shape
    rank = sample_factors.shape[1]
    covered = coverage.shape[1]
    tile_size = snps_here // covered
    per_owner = covered // devices
    own_snps = snp_factors.shape[0]
    own_blocks = own_snps // tile_size
    width = per_owner * tile_size
    assert tile_size == 64 and per_owner % 2 == 0 and own_blocks % 2 == 0
    assert devices % PLANE == 0
    half = rank // 2

    local_list = (
        lax.dynamic_slice_in_dim(coverage, position * per_owner, per_owner, 1)
        - position * own_blocks
    )
    one_hot = local_list[:, :, None] == jnp.arange(own_blocks, dtype=jnp.int32)[None, None, :]
    observers = jnp.sum(one_hot.astype(jnp.float32), axis=(0, 1))
    snp_step = 0.5 * math.sqrt(rank) / (samples_here * observers)
    snp_steps = jnp.broadcast_to(snp_step[:, None], (own_blocks, tile_size)).reshape(1, own_snps)
    sample_step = 0.5 * math.sqrt(rank) / (covered * tile_size)

    smem = pl.BlockSpec(memory_space=pltpu.SMEM)
    vmem = pl.BlockSpec(memory_space=pltpu.VMEM)
    hbm = pl.BlockSpec(memory_space=pltpu.HBM)
    params = pltpu.CompilerParams(vmem_limit_bytes=VMEM_LIMIT)
    pos = position.reshape(1)
    packet = jax.ShapeDtypeStruct((planes, half, width), jnp.bfloat16)
    direct = jax.ShapeDtypeStruct((devices, half, width), jnp.bfloat16)
    dense_blocks = pltpu.VMEM((planes, own_blocks, half, 128), jnp.float32)
    owner_blocks = pltpu.VMEM((own_blocks, half, 128), jnp.float32)
    half_snps = jax.ShapeDtypeStruct((half, own_snps), jnp.float32)
    by_samples = jax.ShapeDtypeStruct((rank, samples_here), jnp.float32)
    square = jax.ShapeDtypeStruct((rank, rank), jnp.float32)
    sizes = (planes, per_owner, own_blocks)

    def cost(flops, bytes_accessed):
        return pl.CostEstimate(flops=flops, bytes_accessed=bytes_accessed, transcendentals=0)

    table = pl.pallas_call(
        functools.partial(table_kernel, *sizes),
        out_shape=jax.ShapeDtypeStruct((PLANE * planes, per_owner), jnp.int32),
        in_specs=[smem, smem],
        out_specs=smem,
        compiler_params=params,
        name="block_table",
    )(pos, coverage)
    geno, samples = pl.pallas_call(
        load_kernel,
        out_shape=(
            pltpu.VMEM((samples_here, snps_here), jnp.bfloat16),
            pltpu.VMEM((rank, samples_here), jnp.float32),
        ),
        in_specs=[hbm, hbm],
        out_specs=(vmem, vmem),
        scratch_shapes=[pltpu.SemaphoreType.DMA((2,))],
        compiler_params=pltpu.CompilerParams(
            vmem_limit_bytes=58 * 1024 * 1024 - 2 * samples_here * snps_here
        ),
        cost_estimate=cost(0, 2 * samples_here * snps_here),
        name="load_batch",
    )(genotypes, sample_factors.T)

    def pick(held):
        return pl.pallas_call(
            functools.partial(pick_kernel, *sizes),
            out_shape=(packet,) * PLANE,
            in_specs=[smem] + [vmem] * planes,
            out_specs=(vmem,) * PLANE,
            scratch_shapes=[dense_blocks],
            compiler_params=params,
            name="pick_blocks",
        )(table, *held)

    def plane_sum(terms):
        return pl.pallas_call(
            functools.partial(plane_sum_kernel, *sizes),
            out_shape=tuple(
                jax.ShapeDtypeStruct((half, own_snps), jnp.bfloat16 if ahead else jnp.float32)
                for ahead in range(planes)
            ),
            in_specs=[smem] + [vmem] * PLANE,
            out_specs=(vmem,) * planes,
            scratch_shapes=[dense_blocks],
            compiler_params=params,
            name="plane_sum",
        )(table, *terms)

    def pack(snps):
        return pl.pallas_call(
            functools.partial(pack_kernel, per_owner),
            out_shape=(direct, half_snps),
            in_specs=[smem, smem, vmem],
            out_specs=(vmem, vmem),
            scratch_shapes=[owner_blocks],
            compiler_params=params,
            name="pack_blocks",
        )(pos, coverage, snps)

    def owner_update(incoming, snps, last):
        results = pl.pallas_call(
            functools.partial(owner_kernel, per_owner, last),
            out_shape=(half_snps,) if last else (half_snps, direct),
            in_specs=[smem, smem, smem, vmem, vmem],
            out_specs=(vmem,) if last else (vmem, vmem),
            scratch_shapes=[owner_blocks],
            compiler_params=params,
            name="owner_update",
        )(pos, coverage, snp_step, incoming, snps)
        return results[0], None if last else results[1]

    def resident():
        return pltpu.with_memory_space_constraint(geno, pltpu.VMEM)

    def product(mates, panels, upper, before):
        share = len(mates) * samples_here * snps_here // PLANE
        return pl.pallas_call(
            functools.partial(product_kernel, planes, mates, before is None, 256),
            out_shape=(by_samples, square),
            in_specs=[smem] + [vmem] * (2 + len(mates) + (0 if before is None else 2)),
            out_specs=(vmem, vmem),
            compiler_params=params,
            cost_estimate=cost(8 * rank * share, 2 * share),
            name="panel_product",
        )(pos, resident(), upper, *[panels[mate] for mate in mates], *(before or ()))

    def sample_update(samples, gradient, gram):
        return pl.pallas_call(
            functools.partial(sample_kernel, sample_step),
            out_shape=(by_samples, jax.ShapeDtypeStruct((rank, samples_here), jnp.bfloat16), square),
            in_specs=[vmem] * 3,
            out_specs=(vmem,) * 3,
            compiler_params=params,
            name="sample_update",
        )(samples, gradient, gram)

    def terms_for(mate, samples_bf16, gram, panel, upper, others, pieces):
        share = samples_here * snps_here // PLANE
        return pl.pallas_call(
            functools.partial(term_kernel, planes, mate, others),
            out_shape=(packet, direct if others else packet),
            in_specs=[smem] + [vmem] * (5 + len(pieces)),
            out_specs=(vmem, vmem),
            compiler_params=params,
            cost_estimate=cost(8 * rank * share, 2 * share),
            name="mate_terms",
        )(pos, resident(), samples_bf16, gram, panel, upper, *pieces)

    def exchange(x):
        return lax.all_to_all(x, "rows", split_axis=0, concat_axis=0, tiled=True)

    def along(x, shift):
        if shift % planes == 0:
            return x
        pairs = [(r, ((r // PLANE + shift) % planes) * PLANE + r % PLANE) for r in range(devices)]
        return lax.ppermute(x, "rows", pairs)

    def to_mate(x, mate):
        if mate == 0:
            return x
        return lax.ppermute(x, "rows", [(r, r ^ mate) for r in range(devices)])

    lower = snp_factors.T[:half]
    outgoing, upper = pack(snp_factors.T)
    for iteration in range(ROUNDS):
        own = lower.astype(jnp.bfloat16)
        held = [along(own, planes - ahead) for ahead in range(planes)]
        upper_panels = exchange(outgoing)
        packets = pick(held)
        panels = [to_mate(packets[mate], mate) for mate in range(PLANE)]
        partial = product([0], panels, upper_panels, None)
        partial = product([1], panels, upper_panels, partial)
        partial = product([2, 3], panels, upper_panels, partial)
        samples, samples_bf16, sample_gram = sample_update(samples, *partial)
        terms, pieces = {}, []
        order = (2, 3, 1, 0)
        for mate in order:
            last = mate == order[-1]
            own_terms, piece = terms_for(
                mate, samples_bf16, sample_gram, panels[mate], upper_panels,
                order[:-1] if last else (), pieces if last else [],
            )
            terms[mate] = to_mate(own_terms, mate)
            pieces.append(piece)
        outgoing = pieces[-1]
        incoming = exchange(outgoing)
        sums = plane_sum([terms[mate] for mate in range(PLANE)])
        total = sums[0]
        for ahead in range(1, planes):
            total = total + along(sums[ahead], ahead).astype(jnp.float32)
        lower = (1.0 - weight_decay) * lower + snp_steps * total
        upper, outgoing = owner_update(incoming, upper, iteration == ROUNDS - 1)
    return (samples.T, jnp.concatenate([lower, upper], axis=0).T)


def solution(mesh):
    placed = (
        P(("groups", "rows"), None),
        P(("groups", "rows"), None),
        P(("groups", "rows"), None),
        P("groups", None),
    )
    return jax.shard_map(
        on_device,
        mesh=mesh,
        in_specs=placed,
        out_specs=(P(("groups", "rows"), None), P(("groups", "rows"), None)),
        check_vma=False,
    )
```

```python
import functools
import math

import jax
import jax.numpy as jnp
from jax import lax
from jax.experimental import pallas as pl
from jax.experimental.pallas import tpu as pltpu
from jax.sharding import PartitionSpec as P

ROUNDS = 2

weight_decay = 0.02

PLANE = 4
NT = (((1,), (1,)), ((), ()))
NN = (((1,), (0,)), ((), ()))
VMEM_LIMIT = 24 * 1024 * 1024


def dot(a, b, dims):
    return lax.dot_general(a, b, dims, preferred_element_type=jnp.float32)


def split3(x):
    hi = x.astype(jnp.bfloat16)
    rest = x - hi.astype(jnp.float32)
    mid = rest.astype(jnp.bfloat16)
    lo = (rest - mid.astype(jnp.float32)).astype(jnp.bfloat16)
    return hi, mid, lo


def low_half(rows):
    return lax.broadcasted_iota(jnp.int32, (rows, 128), 1) < 64


def double(x, low):
    turned = pltpu.roll(x, 64, 1)
    return jnp.where(low, x, turned), jnp.where(low, turned, x)


def load_kernel(geno, samples, geno_out, samples_out, sems):
    copies = [
        pltpu.make_async_copy(samples, samples_out, sems.at[0]),
        pltpu.make_async_copy(geno, geno_out, sems.at[1]),
    ]
    for copy in copies:
        copy.start()
    for copy in copies:
        copy.wait()


def table_kernel(planes, per_owner, own_blocks, pos_ref, cov, table):
    place = lax.bitwise_and(pos_ref[0], PLANE - 1)
    for mate in range(PLANE):
        batch = lax.bitwise_xor(pos_ref[0], mate)
        for plane in range(planes):
            owner = plane * PLANE + place
            for p in range(per_owner):
                table[mate * planes + plane, p] = cov[batch, owner * per_owner + p] - owner * own_blocks


def pick_kernel(planes, per_owner, own_blocks, pos_ref, table, held, packets, blocks):
    place = lax.bitwise_and(pos_ref[0], PLANE - 1)
    low = low_half(held.shape[1])
    for plane in range(planes):
        for j in range(own_blocks // 2):
            x = held[plane, :, 128 * j:128 * (j + 1)].astype(jnp.float32)
            blocks[plane, 2 * j], blocks[plane, 2 * j + 1] = double(x, low)
    for plane in range(planes):
        for mate in range(PLANE):
            for q in range(per_owner // 2):
                first = table[mate * planes + plane, 2 * q]
                second = table[mate * planes + plane, 2 * q + 1]
                pair = jnp.where(low, blocks[plane, first], blocks[plane, second])
                to = lax.bitwise_xor(place, mate)
                packets[to, plane, :, 128 * q:128 * (q + 1)] = pair.astype(jnp.bfloat16)


def plane_sum_kernel(planes, per_owner, own_blocks, table, *refs):
    terms, sums, total = refs[:PLANE], refs[PLANE], refs[-1]
    low = low_half(terms[0].shape[1])
    total[...] = jnp.zeros_like(total)
    for plane in range(planes):
        for mate in range(PLANE):
            for q in range(per_owner // 2):
                first = table[mate * planes + plane, 2 * q]
                second = table[mate * planes + plane, 2 * q + 1]
                pair = terms[mate][plane, :, 128 * q:128 * (q + 1)].astype(jnp.float32)
                total[plane, first] += jnp.where(low, pair, 0.0)
                total[plane, second] += jnp.where(low, 0.0, pair)
    for plane in range(planes):
        for j in range(own_blocks // 2):
            first, second = total[plane, 2 * j], total[plane, 2 * j + 1]
            both = jnp.where(low, first, second) + pltpu.roll(jnp.where(low, second, first), 64, 1)
            sums[plane, :, 128 * j:128 * (j + 1)] = both.astype(jnp.bfloat16)


def columns_of(plane, place, width):
    return pl.ds(pl.multiple_of((plane * PLANE + place) * width, width), width)


def product_kernel(mates, first, rows, pos_ref, geno, packets, *refs):
    before, (geno_out, gradient, gram) = refs[:-3], refs[-3:]
    place = lax.bitwise_and(pos_ref[0], PLANE - 1)
    planes, width = packets.shape[1], packets.shape[3]
    places = [(plane, lax.bitwise_xor(place, mate)) for mate in mates for plane in range(planes)]
    total = None if first else before[1][...]
    for plane, at in places:
        term = dot(packets[at, plane], packets[at, plane], NT)
        total = term if total is None else total + term
    gram[...] = total
    for i in range(geno.shape[0] // rows):
        here = slice(i * rows, (i + 1) * rows)
        total = None if first else before[0][:, here]
        for plane, at in places:
            term = dot(packets[at, plane], geno[here, columns_of(plane, at, width)], NT)
            total = term if total is None else total + term
        gradient[:, here] = total


def sample_kernel(sample_step, samples, gradient, gram, new_samples, new_bf16, new_gram):
    old = samples[...]
    old_bf16 = old.astype(jnp.bfloat16)
    total = gradient[...]
    for part in split3(gram[...]):
        total -= dot(part, old_bf16, NN)
    new = (1.0 - weight_decay) * old + sample_step * total
    new_samples[...] = new
    rounded = new.astype(jnp.bfloat16)
    new_bf16[...] = rounded
    new_gram[...] = dot(rounded, rounded, NT)


def term_kernel(mate, pos_ref, geno, samples, gram, packets, geno_out, terms):
    place = lax.bitwise_and(pos_ref[0], PLANE - 1)
    at = lax.bitwise_xor(place, mate)
    planes, width = packets.shape[1], packets.shape[3]
    parts = split3(gram[...])
    for plane in range(planes):
        term = dot(samples[...], geno[:, columns_of(plane, at, width)], NN)
        for part in parts:
            term -= dot(part, packets[at, plane], NN)
        terms[plane] = term.astype(jnp.bfloat16)


def on_device(genotypes, sample_factors, snp_factors, coverage):
    devices = lax.axis_size("rows")
    planes = devices // PLANE
    position = lax.axis_index("rows").astype(jnp.int32)
    samples_here, snps_here = genotypes.shape
    rank = sample_factors.shape[1]
    covered = coverage.shape[1]
    tile_size = snps_here // covered
    per_owner = covered // devices
    own_snps = snp_factors.shape[0]
    own_blocks = own_snps // tile_size
    width = per_owner * tile_size
    assert tile_size == 64 and per_owner % 2 == 0 and own_blocks % 2 == 0
    assert devices % PLANE == 0

    local_list = (
        lax.dynamic_slice_in_dim(coverage, position * per_owner, per_owner, 1)
        - position * own_blocks
    )
    one_hot = local_list[:, :, None] == jnp.arange(own_blocks, dtype=jnp.int32)[None, None, :]
    observers = jnp.sum(one_hot.astype(jnp.float32), axis=(0, 1))
    snp_step = 0.5 * math.sqrt(rank) / (samples_here * observers)
    snp_step = jnp.broadcast_to(snp_step[:, None], (own_blocks, tile_size)).reshape(1, own_snps)
    sample_step = 0.5 * math.sqrt(rank) / (covered * tile_size)

    smem = pl.BlockSpec(memory_space=pltpu.SMEM)
    vmem = pl.BlockSpec(memory_space=pltpu.VMEM)
    hbm = pl.BlockSpec(memory_space=pltpu.HBM)
    params = pltpu.CompilerParams(vmem_limit_bytes=VMEM_LIMIT)
    pos = position.reshape(1)
    packet = jax.ShapeDtypeStruct((planes, rank, width), jnp.bfloat16)
    packets_shape = jax.ShapeDtypeStruct((PLANE, planes, rank, width), jnp.bfloat16)
    dense_blocks = pltpu.VMEM((planes, own_blocks, rank, 128), jnp.float32)
    by_samples = jax.ShapeDtypeStruct((rank, samples_here), jnp.float32)
    square = jax.ShapeDtypeStruct((rank, rank), jnp.float32)
    sizes = (planes, per_owner, own_blocks)

    def cost(flops, bytes_accessed):
        return pl.CostEstimate(flops=flops, bytes_accessed=bytes_accessed, transcendentals=0)

    table = pl.pallas_call(
        functools.partial(table_kernel, *sizes),
        out_shape=jax.ShapeDtypeStruct((PLANE * planes, per_owner), jnp.int32),
        in_specs=[smem, smem],
        out_specs=smem,
        compiler_params=params,
        name="block_table",
    )(pos, coverage)
    geno, samples = pl.pallas_call(
        load_kernel,
        out_shape=(
            pltpu.VMEM((samples_here, snps_here), jnp.bfloat16),
            pltpu.VMEM((rank, samples_here), jnp.float32),
        ),
        in_specs=[hbm, hbm],
        out_specs=(vmem, vmem),
        scratch_shapes=[pltpu.SemaphoreType.DMA((2,))],
        compiler_params=pltpu.CompilerParams(
            vmem_limit_bytes=58 * 1024 * 1024 - 2 * samples_here * snps_here
        ),
        cost_estimate=cost(0, 2 * samples_here * snps_here),
        name="load_batch",
    )(genotypes, sample_factors.T)

    resident = pltpu.VMEM((samples_here, snps_here), jnp.bfloat16)

    def pick(held):
        return pl.pallas_call(
            functools.partial(pick_kernel, *sizes),
            out_shape=packets_shape,
            in_specs=[smem, smem, vmem],
            out_specs=vmem,
            scratch_shapes=[dense_blocks],
            compiler_params=params,
            name="pick_blocks",
        )(pos, table, held)

    def plane_sum(terms):
        return pl.pallas_call(
            functools.partial(plane_sum_kernel, *sizes),
            out_shape=jax.ShapeDtypeStruct((planes, rank, own_snps), jnp.bfloat16),
            in_specs=[smem] + [vmem] * PLANE,
            out_specs=vmem,
            scratch_shapes=[dense_blocks],
            compiler_params=params,
            name="plane_sum",
        )(table, *terms)

    def product(mates, geno, packets, before):
        share = len(mates) * samples_here * snps_here // PLANE
        return pl.pallas_call(
            functools.partial(product_kernel, mates, not before, 256),
            out_shape=(resident, by_samples, square),
            in_specs=[smem] + [vmem] * (2 + len(before)),
            out_specs=(vmem,) * 3,
            input_output_aliases={1: 0},
            compiler_params=params,
            cost_estimate=cost(8 * rank * share, 2 * share),
            name="panel_product",
        )(pos, geno, packets, *before)

    def sample_update(samples, gradient, gram):
        return pl.pallas_call(
            functools.partial(sample_kernel, sample_step),
            out_shape=(by_samples, jax.ShapeDtypeStruct((rank, samples_here), jnp.bfloat16), square),
            in_specs=[vmem] * 3,
            out_specs=(vmem,) * 3,
            compiler_params=params,
            name="sample_update",
        )(samples, gradient, gram)

    def terms_for(mate, geno, samples_bf16, gram, packets):
        share = samples_here * snps_here // PLANE
        return pl.pallas_call(
            functools.partial(term_kernel, mate),
            out_shape=(resident, packet),
            in_specs=[smem] + [vmem] * 4,
            out_specs=(vmem, vmem),
            input_output_aliases={1: 0},
            compiler_params=params,
            cost_estimate=cost(8 * rank * share, 2 * share),
            name="mate_terms",
        )(pos, geno, samples_bf16, gram, packets)

    def across_planes(x):
        groups = [[plane * PLANE + place for plane in range(planes)] for place in range(PLANE)]
        return lax.all_to_all(x, "rows", 0, 0, axis_index_groups=groups, tiled=True)

    def across_mates(x):
        groups = [[plane * PLANE + place for place in range(PLANE)] for plane in range(planes)]
        return lax.all_to_all(x, "rows", 0, 0, axis_index_groups=groups, tiled=True)

    def to_mate(x, mate):
        if mate == 0:
            return x
        return lax.ppermute(x, "rows", [(r, r ^ mate) for r in range(devices)])

    snps = snp_factors.T
    for iteration in range(ROUNDS):
        own = jnp.broadcast_to(snps.astype(jnp.bfloat16), (planes, rank, own_snps))
        packets = pick(across_planes(own))
        panels = across_mates(packets)
        geno, *partial = product([0], geno, packets, ())
        geno, *partial = product([1, 2, 3], geno, panels, partial)
        samples, samples_bf16, sample_gram = sample_update(samples, *partial)
        terms = [None] * PLANE
        for mate in (2, 3, 1, 0):
            geno, own_terms = terms_for(mate, geno, samples_bf16, sample_gram, panels)
            terms[mate] = to_mate(own_terms, mate)
        sums = across_planes(plane_sum(terms))
        total = jnp.sum(sums.astype(jnp.float32), axis=0)
        snps = (1.0 - weight_decay) * snps + snp_step * total
    return (samples.T, snps.T)


def solution(mesh):
    placed = (
        P(("groups", "rows"), None),
        P(("groups", "rows"), None),
        P(("groups", "rows"), None),
        P("groups", None),
    )
    return jax.shard_map(
        on_device,
        mesh=mesh,
        in_specs=placed,
        out_specs=(P(("groups", "rows"), None), P(("groups", "rows"), None)),
        check_vma=False,
    )
```

```python
import functools
import math

import jax
import jax.numpy as jnp
from jax import lax
from jax.experimental import pallas as pl
from jax.experimental.pallas import tpu as pltpu
from jax.sharding import PartitionSpec as P

ROUNDS = 2

weight_decay = 0.02

PLANE = 4
NT = (((1,), (1,)), ((), ()))
NN = (((1,), (0,)), ((), ()))
VMEM_LIMIT = 24 * 1024 * 1024


def dot(a, b, dims):
    return lax.dot_general(a, b, dims, preferred_element_type=jnp.float32)


def split3(x):
    hi = x.astype(jnp.bfloat16)
    rest = x - hi.astype(jnp.float32)
    mid = rest.astype(jnp.bfloat16)
    lo = (rest - mid.astype(jnp.float32)).astype(jnp.bfloat16)
    return hi, mid, lo


def low_half(rows):
    return lax.broadcasted_iota(jnp.int32, (rows, 128), 1) < 64


def double(x, low):
    turned = pltpu.roll(x, 64, 1)
    return jnp.where(low, x, turned), jnp.where(low, turned, x)


def load_kernel(geno, samples, geno_out, samples_out, sems):
    copies = [
        pltpu.make_async_copy(samples, samples_out, sems.at[0]),
        pltpu.make_async_copy(geno, geno_out, sems.at[1]),
    ]
    for copy in copies:
        copy.start()
    for copy in copies:
        copy.wait()


def table_kernel(planes, per_owner, own_blocks, pos_ref, cov, table):
    for mate in range(PLANE):
        batch = lax.bitwise_xor(pos_ref[0], mate)
        for turn in range(planes):
            owner = lax.bitwise_xor(pos_ref[0], turn * PLANE)
            for p in range(per_owner):
                table[mate * planes + turn, p] = cov[batch, owner * per_owner + p] - owner * own_blocks


def steps_kernel(scale, own_blocks, pos_ref, cov, steps):
    def step_of(block):
        seen = (cov[...] == pos_ref[0] * own_blocks + block).astype(jnp.float32)
        return scale / jnp.sum(jnp.sum(seen, axis=1, keepdims=True), axis=0, keepdims=True)

    low = low_half(steps.shape[0])
    for j in range(own_blocks // 2):
        steps[:, 128 * j:128 * (j + 1)] = jnp.where(low, step_of(2 * j), step_of(2 * j + 1))


def pick_kernel(planes, turns, per_owner, own_blocks, table, *refs):
    held, packets, blocks = refs[:len(turns)], refs[len(turns):-1], refs[-1]
    low = low_half(held[0].shape[0])
    for i in range(len(turns)):
        for j in range(own_blocks // 2):
            x = held[i][:, 128 * j:128 * (j + 1)].astype(jnp.float32)
            blocks[i, 2 * j], blocks[i, 2 * j + 1] = double(x, low)
    for mate in range(PLANE):
        for i, turn in enumerate(turns):
            for q in range(per_owner // 2):
                first = table[mate * planes + turn, 2 * q]
                second = table[mate * planes + turn, 2 * q + 1]
                pair = jnp.where(low, blocks[i, first], blocks[i, second])
                packets[mate][i, :, 128 * q:128 * (q + 1)] = pair.astype(jnp.bfloat16)


def plane_sum_kernel(planes, turns, per_owner, own_blocks, table, *refs):
    terms, sums, total = refs[:PLANE], refs[PLANE:-1], refs[-1]
    low = low_half(terms[0].shape[1])
    total[...] = jnp.zeros_like(total)
    for i, turn in enumerate(turns):
        for mate in range(PLANE):
            for q in range(per_owner // 2):
                first = table[mate * planes + turn, 2 * q]
                second = table[mate * planes + turn, 2 * q + 1]
                pair = terms[mate][i, :, 128 * q:128 * (q + 1)].astype(jnp.float32)
                total[i, first] += jnp.where(low, pair, 0.0)
                total[i, second] += jnp.where(low, 0.0, pair)
    for i in range(len(turns)):
        for j in range(own_blocks // 2):
            first, second = total[i, 2 * j], total[i, 2 * j + 1]
            both = jnp.where(low, first, second) + pltpu.roll(jnp.where(low, second, first), 64, 1)
            sums[i][:, 128 * j:128 * (j + 1)] = both.astype(sums[i].dtype)


def columns_of(pos, turn, mate, width):
    owner = lax.bitwise_xor(pos, turn * PLANE + mate)
    return pl.ds(pl.multiple_of(owner * width, width), width)


def product_kernel(turns, mates, first, rows, pos_ref, geno, *refs):
    packets, before, (gradient, gram) = refs[:len(mates)], refs[len(mates):-2], refs[-2:]
    pos = pos_ref[0]
    width = packets[0].shape[2]
    places = [(i, turn, m, mate) for m, mate in enumerate(mates) for i, turn in enumerate(turns)]
    total = None if first else before[1][...]
    for i, turn, m, mate in places:
        term = dot(packets[m][i], packets[m][i], NT)
        total = term if total is None else total + term
    gram[...] = total
    for r in range(geno.shape[0] // rows):
        here = slice(r * rows, (r + 1) * rows)
        total = None if first else before[0][:, here]
        for i, turn, m, mate in places:
            term = dot(packets[m][i], geno[here, columns_of(pos, turn, mate, width)], NT)
            total = term if total is None else total + term
        gradient[:, here] = total


def sample_kernel(sample_step, samples, gradient, gram, new_samples, new_bf16, new_gram):
    old = samples[...]
    old_bf16 = old.astype(jnp.bfloat16)
    total = gradient[...]
    for part in split3(gram[...]):
        total -= dot(part, old_bf16, NN)
    new = (1.0 - weight_decay) * old + sample_step * total
    new_samples[...] = new
    rounded = new.astype(jnp.bfloat16)
    new_bf16[...] = rounded
    new_gram[...] = dot(rounded, rounded, NT)


def term_kernel(turns, mate, pos_ref, geno, samples, gram, packet, terms):
    pos = pos_ref[0]
    width = packet.shape[2]
    parts = split3(gram[...])
    for i, turn in enumerate(turns):
        term = dot(samples[...], geno[:, columns_of(pos, turn, mate, width)], NN)
        for part in parts:
            term -= dot(part, packet[i], NN)
        terms[i] = term.astype(jnp.bfloat16)


def on_device(genotypes, sample_factors, snp_factors, coverage):
    devices = lax.axis_size("rows")
    planes = devices // PLANE
    position = lax.axis_index("rows").astype(jnp.int32)
    samples_here, snps_here = genotypes.shape
    rank = sample_factors.shape[1]
    covered = coverage.shape[1]
    tile_size = snps_here // covered
    per_owner = covered // devices
    own_snps = snp_factors.shape[0]
    own_blocks = own_snps // tile_size
    width = per_owner * tile_size
    assert tile_size == 64 and per_owner % 2 == 0 and own_blocks % 2 == 0
    assert devices % PLANE == 0 and planes % 2 == 0 and planes & (planes - 1) == 0

    sample_step = 0.5 * math.sqrt(rank) / (covered * tile_size)

    smem = pl.BlockSpec(memory_space=pltpu.SMEM)
    vmem = pl.BlockSpec(memory_space=pltpu.VMEM)
    hbm = pl.BlockSpec(memory_space=pltpu.HBM)
    params = pltpu.CompilerParams(vmem_limit_bytes=VMEM_LIMIT)
    pos = position.reshape(1)
    half = planes // 2
    near, far = tuple(range(half)), tuple(range(half, planes))
    packet = jax.ShapeDtypeStruct((half, rank, width), jnp.bfloat16)
    dense_blocks = pltpu.VMEM((half, own_blocks, rank, 128), jnp.float32)
    by_samples = jax.ShapeDtypeStruct((rank, samples_here), jnp.float32)
    square = jax.ShapeDtypeStruct((rank, rank), jnp.float32)
    sizes = (planes, per_owner, own_blocks)

    def cost(flops, bytes_accessed):
        return pl.CostEstimate(flops=flops, bytes_accessed=bytes_accessed, transcendentals=0)

    table = pl.pallas_call(
        functools.partial(table_kernel, *sizes),
        out_shape=jax.ShapeDtypeStruct((PLANE * planes, per_owner), jnp.int32),
        in_specs=[smem, smem],
        out_specs=smem,
        compiler_params=params,
        name="block_table",
    )(pos, coverage)
    geno, samples = pl.pallas_call(
        load_kernel,
        out_shape=(
            pltpu.VMEM((samples_here, snps_here), jnp.bfloat16),
            pltpu.VMEM((rank, samples_here), jnp.float32),
        ),
        in_specs=[hbm, hbm],
        out_specs=(vmem, vmem),
        scratch_shapes=[pltpu.SemaphoreType.DMA((2,))],
        compiler_params=pltpu.CompilerParams(
            vmem_limit_bytes=58 * 1024 * 1024 - 2 * samples_here * snps_here
        ),
        cost_estimate=cost(0, 2 * samples_here * snps_here),
        name="load_batch",
    )(genotypes, sample_factors.T)

    snp_step = pl.pallas_call(
        functools.partial(steps_kernel, 0.5 * math.sqrt(rank) / samples_here, own_blocks),
        out_shape=jax.ShapeDtypeStruct((rank, own_snps), jnp.float32),
        in_specs=[smem, vmem],
        out_specs=vmem,
        compiler_params=params,
        name="snp_steps",
    )(pos, coverage)
    small = cost(0, 2 * 1024 * 1024)

    def pick(turns, held):
        return pl.pallas_call(
            functools.partial(pick_kernel, planes, turns, per_owner, own_blocks),
            out_shape=(packet,) * PLANE,
            in_specs=[smem] + [vmem] * half,
            out_specs=(vmem,) * PLANE,
            scratch_shapes=[dense_blocks],
            compiler_params=params,
            cost_estimate=small,
            name="pick_blocks",
        )(table, *[held[turn] for turn in turns])

    def plane_sum(turns, terms):
        sums = pl.pallas_call(
            functools.partial(plane_sum_kernel, planes, turns, per_owner, own_blocks),
            out_shape=tuple(
                jax.ShapeDtypeStruct((rank, own_snps), jnp.bfloat16 if turn % 2 else jnp.float32)
                for turn in turns
            ),
            in_specs=[smem] + [vmem] * PLANE,
            out_specs=(vmem,) * half,
            scratch_shapes=[dense_blocks],
            compiler_params=params,
            cost_estimate=small,
            name="plane_sum",
        )(table, *terms)
        return dict(zip(turns, sums))

    def product(turns, mates, panels, before):
        share = len(turns) * len(mates) * samples_here * snps_here // devices
        return pl.pallas_call(
            functools.partial(product_kernel, turns, mates, not before, 256),
            out_shape=(by_samples, square),
            in_specs=[smem] + [vmem] * (1 + len(mates) + len(before)),
            out_specs=(vmem, vmem),
            compiler_params=params,
            cost_estimate=cost(8 * rank * share, 2 * share),
            name="panel_product",
        )(pos, geno, *[panels[turns][mate] for mate in mates], *before)

    def sample_update(samples, gradient, gram):
        return pl.pallas_call(
            functools.partial(sample_kernel, sample_step),
            out_shape=(by_samples, jax.ShapeDtypeStruct((rank, samples_here), jnp.bfloat16), square),
            in_specs=[vmem] * 3,
            out_specs=(vmem,) * 3,
            compiler_params=params,
            name="sample_update",
        )(samples, gradient, gram)

    def terms_for(turns, mate, samples_bf16, gram, panels):
        share = len(turns) * samples_here * snps_here // devices
        return pl.pallas_call(
            functools.partial(term_kernel, turns, mate),
            out_shape=packet,
            in_specs=[smem] + [vmem] * 4,
            out_specs=vmem,
            compiler_params=params,
            cost_estimate=cost(8 * rank * share, 2 * share),
            name="mate_terms",
        )(pos, geno, samples_bf16, gram, panels[turns][mate])

    def swap(x, turn):
        return lax.ppermute(x, "rows", [(r, r ^ turn) for r in range(devices)])

    def to_mate(x, mate):
        return swap(x, mate) if mate else x

    snps = snp_factors.T
    for iteration in range(ROUNDS):
        held = {0: snps.astype(jnp.bfloat16)}
        for turn in sorted(range(1, planes), key=lambda turn: (turn & (turn - 1), -turn)):
            bit = turn & -turn
            held[turn] = swap(held[turn ^ bit], bit * PLANE)
        panels = {}
        for turns in (near, far):
            packets = pick(turns, held)
            panels[turns] = [to_mate(packets[mate], mate) for mate in range(PLANE)]
        partial = ()
        for turns, mates in (
            (near, (0,)), (far, (0,)), (near, (1,)), (near, (2, 3)), (far, (1,)), (far, (2,)), (far, (3,))
        ):
            partial = product(turns, mates, panels, partial)
        samples, samples_bf16, sample_gram = sample_update(samples, *partial)
        sums = {}
        for turns in (far, near):
            terms = {}
            for mate in (2, 3, 1, 0):
                terms[mate] = to_mate(terms_for(turns, mate, samples_bf16, sample_gram, panels), mate)
            sums.update(plane_sum(turns, [terms[mate] for mate in range(PLANE)]))
        for turn in range(planes - 1, 0, -1):
            bit = turn & -turn
            arrived = swap(sums[turn].astype(jnp.bfloat16), bit * PLANE)
            sums[turn ^ bit] = sums[turn ^ bit] + arrived.astype(jnp.float32)
        snps = (1.0 - weight_decay) * snps + snp_step * sums[0]
    return (samples.T, snps.T)


def solution(mesh):
    placed = (
        P(("groups", "rows"), None),
        P(("groups", "rows"), None),
        P(("groups", "rows"), None),
        P("groups", None),
    )
    return jax.shard_map(
        on_device,
        mesh=mesh,
        in_specs=placed,
        out_specs=(P(("groups", "rows"), None), P(("groups", "rows"), None)),
        check_vma=False,
    )
```

```python
import functools
import math

import jax
import jax.numpy as jnp
from jax import lax
from jax.experimental import pallas as pl
from jax.experimental.pallas import tpu as pltpu
from jax.sharding import PartitionSpec as P

ROUNDS = 2

weight_decay = 0.02

PLANE = 4
NT = (((1,), (1,)), ((), ()))
NN = (((1,), (0,)), ((), ()))
VMEM_LIMIT = 24 * 1024 * 1024


def dot(a, b, dims):
    return lax.dot_general(a, b, dims, preferred_element_type=jnp.float32)


def split3(x):
    hi = x.astype(jnp.bfloat16)
    rest = x - hi.astype(jnp.float32)
    mid = rest.astype(jnp.bfloat16)
    lo = (rest - mid.astype(jnp.float32)).astype(jnp.bfloat16)
    return hi, mid, lo


def low_half(rows):
    return lax.broadcasted_iota(jnp.int32, (rows, 128), 1) < 64


def double(x, low):
    turned = pltpu.roll(x, 64, 1)
    return jnp.where(low, x, turned), jnp.where(low, turned, x)


def load_kernel(planes, per_owner, own_blocks, pos_ref, cov, geno, samples, geno_out, samples_out, table, listed, sems):
    copies = [
        pltpu.make_async_copy(cov, listed, sems.at[0]),
        pltpu.make_async_copy(samples, samples_out, sems.at[1]),
        pltpu.make_async_copy(geno, geno_out, sems.at[2]),
    ]
    for copy in copies:
        copy.start()
    copies[0].wait()
    for mate in range(PLANE):
        batch = lax.bitwise_xor(pos_ref[0], mate)
        for turn in range(planes):
            owner = lax.bitwise_xor(pos_ref[0], turn * PLANE)
            for p in range(per_owner):
                table[mate * planes + turn, p] = listed[batch, owner * per_owner + p] - owner * own_blocks
    for copy in copies[1:]:
        copy.wait()


def steps_kernel(scale, own_blocks, pos_ref, cov, steps):
    def step_of(block):
        seen = (cov[...] == pos_ref[0] * own_blocks + block).astype(jnp.float32)
        return scale / jnp.sum(jnp.sum(seen, axis=1, keepdims=True), axis=0, keepdims=True)

    low = low_half(steps.shape[0])
    for j in range(own_blocks // 2):
        steps[:, 128 * j:128 * (j + 1)] = jnp.where(low, step_of(2 * j), step_of(2 * j + 1))


def pick_kernel(planes, turns, per_owner, own_blocks, table, *refs):
    held, packets, blocks = refs[:len(turns)], refs[len(turns):-1], refs[-1]
    low = low_half(held[0].shape[0])
    for i in range(len(turns)):
        for j in range(own_blocks // 2):
            x = held[i][:, 128 * j:128 * (j + 1)].astype(jnp.float32)
            blocks[i, 2 * j], blocks[i, 2 * j + 1] = double(x, low)
    for mate in range(PLANE):
        for i, turn in enumerate(turns):
            for q in range(per_owner // 2):
                first = table[mate * planes + turn, 2 * q]
                second = table[mate * planes + turn, 2 * q + 1]
                pair = jnp.where(low, blocks[i, first], blocks[i, second])
                packets[mate][i, :, 128 * q:128 * (q + 1)] = pair.astype(jnp.bfloat16)


def plane_sum_kernel(planes, turns, per_owner, own_blocks, table, *refs):
    terms, sums, total = refs[:PLANE], refs[-1 - len(turns):-1], refs[-1]
    low = low_half(terms[0].shape[1])
    total[...] = jnp.zeros_like(total)
    for i, turn in enumerate(turns):
        for mate in range(PLANE):
            for q in range(per_owner // 2):
                first = table[mate * planes + turn, 2 * q]
                second = table[mate * planes + turn, 2 * q + 1]
                pair = terms[mate][i, :, 128 * q:128 * (q + 1)].astype(jnp.float32)
                total[i, first] += jnp.where(low, pair, 0.0)
                total[i, second] += jnp.where(low, 0.0, pair)
    for i in range(len(turns)):
        for j in range(own_blocks // 2):
            first, second = total[i, 2 * j], total[i, 2 * j + 1]
            both = jnp.where(low, first, second) + pltpu.roll(jnp.where(low, second, first), 64, 1)
            sums[i][:, 128 * j:128 * (j + 1)] = both.astype(sums[i].dtype)


def columns_of(pos, turn, mate, width):
    owner = lax.bitwise_xor(pos, turn * PLANE + mate)
    return pl.ds(pl.multiple_of(owner * width, width), width)


def product_kernel(turns, mates, first, rows, pos_ref, geno, *refs):
    packets, before, (gradient, gram) = refs[:len(mates)], refs[len(mates):-2], refs[-2:]
    pos = pos_ref[0]
    width = packets[0].shape[2]
    places = [(i, turn, m, mate) for m, mate in enumerate(mates) for i, turn in enumerate(turns)]
    total = None if first else before[1][...]
    for i, turn, m, mate in places:
        term = dot(packets[m][i], packets[m][i], NT)
        total = term if total is None else total + term
    gram[...] = total
    for r in range(geno.shape[0] // rows):
        here = slice(r * rows, (r + 1) * rows)
        total = None if first else before[0][:, here]
        for i, turn, m, mate in places:
            term = dot(packets[m][i], geno[here, columns_of(pos, turn, mate, width)], NT)
            total = term if total is None else total + term
        gradient[:, here] = total


def sample_kernel(sample_step, samples, gradient, gram, new_samples, new_bf16, new_gram):
    old = samples[...]
    old_bf16 = old.astype(jnp.bfloat16)
    total = gradient[...]
    for part in split3(gram[...]):
        total -= dot(part, old_bf16, NN)
    new = (1.0 - weight_decay) * old + sample_step * total
    new_samples[...] = new
    rounded = new.astype(jnp.bfloat16)
    new_bf16[...] = rounded
    new_gram[...] = dot(rounded, rounded, NT)


def term_kernel(turns, mate, pos_ref, geno, samples, gram, packet, terms):
    pos = pos_ref[0]
    width = packet.shape[2]
    parts = split3(gram[...])
    for i, turn in enumerate(turns):
        term = dot(samples[...], geno[:, columns_of(pos, turn, mate, width)], NN)
        for part in parts:
            term -= dot(part, packet[i], NN)
        terms[i] = term.astype(jnp.bfloat16)


def on_device(genotypes, sample_factors, snp_factors, coverage):
    devices = lax.axis_size("rows")
    planes = devices // PLANE
    position = lax.axis_index("rows").astype(jnp.int32)
    samples_here, snps_here = genotypes.shape
    rank = sample_factors.shape[1]
    covered = coverage.shape[1]
    tile_size = snps_here // covered
    per_owner = covered // devices
    own_snps = snp_factors.shape[0]
    own_blocks = own_snps // tile_size
    width = per_owner * tile_size
    assert tile_size == 64 and per_owner % 2 == 0 and own_blocks % 2 == 0
    assert devices % PLANE == 0 and planes % 2 == 0 and planes & (planes - 1) == 0

    sample_step = 0.5 * math.sqrt(rank) / (covered * tile_size)

    smem = pl.BlockSpec(memory_space=pltpu.SMEM)
    vmem = pl.BlockSpec(memory_space=pltpu.VMEM)
    hbm = pl.BlockSpec(memory_space=pltpu.HBM)
    anywhere = pl.BlockSpec(memory_space=pl.ANY)
    params = pltpu.CompilerParams(vmem_limit_bytes=VMEM_LIMIT)
    pos = position.reshape(1)
    half = planes // 2
    near, far = tuple(range(half)), tuple(range(half, planes))
    packet = jax.ShapeDtypeStruct((half, rank, width), jnp.bfloat16)
    dense_blocks = pltpu.VMEM((half, own_blocks, rank, 128), jnp.float32)
    by_samples = jax.ShapeDtypeStruct((rank, samples_here), jnp.float32)
    square = jax.ShapeDtypeStruct((rank, rank), jnp.float32)

    def cost(flops, bytes_accessed):
        return pl.CostEstimate(flops=flops, bytes_accessed=bytes_accessed, transcendentals=0)

    geno, samples, table = pl.pallas_call(
        functools.partial(load_kernel, planes, per_owner, own_blocks),
        out_shape=(
            pltpu.VMEM((samples_here, snps_here), jnp.bfloat16),
            pltpu.VMEM((rank, samples_here), jnp.float32),
            pltpu.SMEM((PLANE * planes, per_owner), jnp.int32),
        ),
        in_specs=[smem, hbm, hbm, hbm],
        out_specs=(vmem, vmem, smem),
        scratch_shapes=[pltpu.SMEM(coverage.shape, jnp.int32), pltpu.SemaphoreType.DMA((3,))],
        compiler_params=pltpu.CompilerParams(
            vmem_limit_bytes=58 * 1024 * 1024 - 2 * samples_here * snps_here
        ),
        cost_estimate=cost(0, 2 * samples_here * snps_here),
        name="load_batch",
    )(pos, coverage, genotypes, sample_factors.T)

    snp_step = pl.pallas_call(
        functools.partial(steps_kernel, 0.5 * math.sqrt(rank) / samples_here, own_blocks),
        out_shape=jax.ShapeDtypeStruct((rank, own_snps), jnp.float32),
        in_specs=[smem, vmem],
        out_specs=vmem,
        compiler_params=params,
        name="snp_steps",
    )(pos, coverage)
    small = cost(0, 2 * 1024 * 1024)

    def pick(turns, held):
        return pl.pallas_call(
            functools.partial(pick_kernel, planes, turns, per_owner, own_blocks),
            out_shape=(packet,) * PLANE,
            in_specs=[smem] + [vmem] * half,
            out_specs=(vmem,) * PLANE,
            scratch_shapes=[dense_blocks],
            compiler_params=params,
            cost_estimate=small,
            name="pick_blocks",
        )(table, *[held[turn] for turn in turns])

    def plane_sum(turns, terms, after):
        sums = pl.pallas_call(
            functools.partial(plane_sum_kernel, planes, turns, per_owner, own_blocks),
            out_shape=tuple(
                jax.ShapeDtypeStruct((rank, own_snps), jnp.bfloat16 if turn % 2 else jnp.float32)
                for turn in turns
            ),
            in_specs=[smem] + [vmem] * PLANE + [anywhere] * len(after),
            out_specs=(vmem,) * half,
            scratch_shapes=[dense_blocks],
            compiler_params=params,
            cost_estimate=small,
            name="plane_sum",
        )(table, *terms, *after)
        return dict(zip(turns, sums))

    def product(turns, mates, panels, before):
        share = len(turns) * len(mates) * samples_here * snps_here // devices
        return pl.pallas_call(
            functools.partial(product_kernel, turns, mates, not before, 256),
            out_shape=(by_samples, square),
            in_specs=[smem] + [vmem] * (1 + len(mates) + len(before)),
            out_specs=(vmem, vmem),
            compiler_params=params,
            cost_estimate=cost(8 * rank * share, 2 * share),
            name="panel_product",
        )(pos, geno, *[panels[turns][mate] for mate in mates], *before)

    def sample_update(samples, gradient, gram):
        return pl.pallas_call(
            functools.partial(sample_kernel, sample_step),
            out_shape=(by_samples, jax.ShapeDtypeStruct((rank, samples_here), jnp.bfloat16), square),
            in_specs=[vmem] * 3,
            out_specs=(vmem,) * 3,
            compiler_params=params,
            name="sample_update",
        )(samples, gradient, gram)

    def terms_for(turns, mate, samples_bf16, gram, panels):
        share = len(turns) * samples_here * snps_here // devices
        return pl.pallas_call(
            functools.partial(term_kernel, turns, mate),
            out_shape=packet,
            in_specs=[smem] + [vmem] * 4,
            out_specs=vmem,
            compiler_params=params,
            cost_estimate=cost(8 * rank * share, 2 * share),
            name="mate_terms",
        )(pos, geno, samples_bf16, gram, panels[turns][mate])

    def swap(x, turn):
        return lax.ppermute(x, "rows", [(r, r ^ turn) for r in range(devices)])

    def to_mate(x, mate):
        return swap(x, mate) if mate else x

    snps = snp_factors.T
    for iteration in range(ROUNDS):
        held = {0: snps.astype(jnp.bfloat16)}
        for turn in sorted(range(1, planes), key=lambda turn: (turn & (turn - 1), -turn)):
            bit = turn & -turn
            source = held[turn ^ bit]
            if iteration == 0 and turn != bit:
                source, _ = lax.optimization_barrier((source, samples))
            held[turn] = swap(source, bit * PLANE)
        panels = {}
        for turns in (near, far):
            packets = pick(turns, held)
            panels[turns] = [to_mate(packets[mate], mate) for mate in range(PLANE)]
        partial = ()
        for turns, mates in (
            (near, (0,)), (far, (0,)), (near, (1,)), (near, (2, 3)), (far, (1,)), (far, (2,)), (far, (3,))
        ):
            partial = product(turns, mates, panels, partial)
        samples, samples_bf16, sample_gram = sample_update(samples, *partial)
        terms, sent = {}, {}
        for turns in (far, near):
            for mate in (2, 3, 1, 0):
                terms[turns, mate] = terms_for(turns, mate, samples_bf16, sample_gram, panels)
                sent[turns, mate] = to_mate(terms[turns, mate], mate)
        sums = plane_sum(far, [sent[far, mate] for mate in range(PLANE)], [terms[near, mate] for mate in range(PLANE)])
        sums.update(plane_sum(near, [sent[near, mate] for mate in range(PLANE)], []))
        for turn in range(planes - 1, 0, -1):
            bit = turn & -turn
            arrived = swap(sums[turn].astype(jnp.bfloat16), bit * PLANE)
            sums[turn ^ bit] = sums[turn ^ bit] + arrived.astype(jnp.float32)
        snps = (1.0 - weight_decay) * snps + snp_step * sums[0]
    return (samples.T, snps.T)


def solution(mesh):
    placed = (
        P(("groups", "rows"), None),
        P(("groups", "rows"), None),
        P(("groups", "rows"), None),
        P("groups", None),
    )
    return jax.shard_map(
        on_device,
        mesh=mesh,
        in_specs=placed,
        out_specs=(P(("groups", "rows"), None), P(("groups", "rows"), None)),
        check_vma=False,
    )
```

```python
import functools
import math

import jax
import jax.numpy as jnp
from jax import lax
from jax.experimental import pallas as pl
from jax.experimental.pallas import tpu as pltpu
from jax.sharding import PartitionSpec as P

ROUNDS = 2

weight_decay = 0.02

PLANE = 4
NT = (((1,), (1,)), ((), ()))
NN = (((1,), (0,)), ((), ()))
VMEM_LIMIT = 24 * 1024 * 1024


def dot(a, b, dims):
    return lax.dot_general(a, b, dims, preferred_element_type=jnp.float32)


def split3(x):
    hi = x.astype(jnp.bfloat16)
    rest = x - hi.astype(jnp.float32)
    mid = rest.astype(jnp.bfloat16)
    lo = (rest - mid.astype(jnp.float32)).astype(jnp.bfloat16)
    return hi, mid, lo


def low_half(rows):
    return lax.broadcasted_iota(jnp.int32, (rows, 128), 1) < 64


def double(x, low):
    turned = pltpu.roll(x, 64, 1)
    return jnp.where(low, x, turned), jnp.where(low, turned, x)


def load_kernel(planes, per_owner, own_blocks, pos_ref, cov, geno, samples, geno_out, samples_out, table, listed, sems):
    copies = [
        pltpu.make_async_copy(cov, listed, sems.at[0]),
        pltpu.make_async_copy(samples, samples_out, sems.at[1]),
        pltpu.make_async_copy(geno, geno_out, sems.at[2]),
    ]
    for copy in copies:
        copy.start()
    copies[0].wait()
    for mate in range(PLANE):
        batch = lax.bitwise_xor(pos_ref[0], mate)
        for turn in range(planes):
            owner = lax.bitwise_xor(pos_ref[0], turn * PLANE)
            for p in range(per_owner):
                table[mate * planes + turn, p] = listed[batch, owner * per_owner + p] - owner * own_blocks
    for copy in copies[1:]:
        copy.wait()


def steps_kernel(scale, own_blocks, pos_ref, cov, steps):
    def step_of(block):
        seen = (cov[...] == pos_ref[0] * own_blocks + block).astype(jnp.float32)
        return scale / jnp.sum(jnp.sum(seen, axis=1, keepdims=True), axis=0, keepdims=True)

    low = low_half(steps.shape[0])
    for j in range(own_blocks // 2):
        steps[:, 128 * j:128 * (j + 1)] = jnp.where(low, step_of(2 * j), step_of(2 * j + 1))


def pick_kernel(planes, turns, per_owner, own_blocks, table, *refs):
    held, packets, blocks = refs[:len(turns)], refs[len(turns):-1], refs[-1]
    low = low_half(held[0].shape[0])
    for i in range(len(turns)):
        for j in range(own_blocks // 2):
            x = held[i][:, 128 * j:128 * (j + 1)].astype(jnp.float32)
            blocks[i, 2 * j], blocks[i, 2 * j + 1] = double(x, low)
    for mate in range(PLANE):
        for i, turn in enumerate(turns):
            for q in range(per_owner // 2):
                first = table[mate * planes + turn, 2 * q]
                second = table[mate * planes + turn, 2 * q + 1]
                pair = jnp.where(low, blocks[i, first], blocks[i, second])
                packets[mate][i, :, 128 * q:128 * (q + 1)] = pair.astype(jnp.bfloat16)


def plane_sum_kernel(planes, per_owner, own_blocks, table, *refs):
    terms, sums, total = refs[:PLANE], refs[-1 - planes:-1], refs[-1]
    low = low_half(terms[0].shape[1])
    total[...] = jnp.zeros_like(total)
    for turn in range(planes):
        for mate in range(PLANE):
            for q in range(per_owner // 2):
                first = table[mate * planes + turn, 2 * q]
                second = table[mate * planes + turn, 2 * q + 1]
                pair = terms[mate][turn, :, 128 * q:128 * (q + 1)].astype(jnp.float32)
                total[turn, first] += jnp.where(low, pair, 0.0)
                total[turn, second] += jnp.where(low, 0.0, pair)
    for turn in range(planes):
        for j in range(own_blocks // 2):
            first, second = total[turn, 2 * j], total[turn, 2 * j + 1]
            both = jnp.where(low, first, second) + pltpu.roll(jnp.where(low, second, first), 64, 1)
            sums[turn][:, 128 * j:128 * (j + 1)] = both.astype(sums[turn].dtype)


def columns_of(pos, turn, mate, width):
    owner = lax.bitwise_xor(pos, turn * PLANE + mate)
    return pl.ds(pl.multiple_of(owner * width, width), width)


def product_kernel(turns, mates, first, rows, pos_ref, geno, *refs):
    packets, before, (gradient, gram) = refs[:len(mates)], refs[len(mates):-2], refs[-2:]
    pos = pos_ref[0]
    width = packets[0].shape[2]
    places = [(i, turn, m, mate) for m, mate in enumerate(mates) for i, turn in enumerate(turns)]
    total = None if first else before[1][...]
    for i, turn, m, mate in places:
        term = dot(packets[m][i], packets[m][i], NT)
        total = term if total is None else total + term
    gram[...] = total
    for r in range(geno.shape[0] // rows):
        here = slice(r * rows, (r + 1) * rows)
        total = None if first else before[0][:, here]
        for i, turn, m, mate in places:
            term = dot(packets[m][i], geno[here, columns_of(pos, turn, mate, width)], NT)
            total = term if total is None else total + term
        gradient[:, here] = total


def sample_kernel(sample_step, samples, gradient, gram, *outs):
    old = samples[...]
    old_bf16 = old.astype(jnp.bfloat16)
    total = gradient[...]
    for part in split3(gram[...]):
        total -= dot(part, old_bf16, NN)
    new = (1.0 - weight_decay) * old + sample_step * total
    *full, last = outs
    rounded = new.astype(jnp.bfloat16)
    for out in full:
        out[...] = new if out.dtype == jnp.float32 else rounded
    if last.shape[0] == last.shape[1]:
        last[...] = dot(rounded, rounded, NT)
    else:
        last[...] = jnp.zeros_like(last)


def term_kernel(groups, mate, pos_ref, geno, samples, gram, *refs):
    packets, terms = refs[:len(groups)], refs[-1]
    pos = pos_ref[0]
    width = terms.shape[2]
    parts = split3(gram[...])
    for turns, packet in zip(groups, packets):
        for i, turn in enumerate(turns):
            term = dot(samples[...], geno[:, columns_of(pos, turn, mate, width)], NN)
            for part in parts:
                term -= dot(part, packet[i], NN)
            terms[turn] = term.astype(jnp.bfloat16)


def on_device(genotypes, sample_factors, snp_factors, coverage):
    devices = lax.axis_size("rows")
    planes = devices // PLANE
    position = lax.axis_index("rows").astype(jnp.int32)
    samples_here, snps_here = genotypes.shape
    rank = sample_factors.shape[1]
    covered = coverage.shape[1]
    tile_size = snps_here // covered
    per_owner = covered // devices
    own_snps = snp_factors.shape[0]
    own_blocks = own_snps // tile_size
    width = per_owner * tile_size
    assert tile_size == 64 and per_owner % 2 == 0 and own_blocks % 2 == 0
    assert devices % PLANE == 0 and planes % 2 == 0 and planes & (planes - 1) == 0

    sample_step = 0.5 * math.sqrt(rank) / (covered * tile_size)

    smem = pl.BlockSpec(memory_space=pltpu.SMEM)
    vmem = pl.BlockSpec(memory_space=pltpu.VMEM)
    hbm = pl.BlockSpec(memory_space=pltpu.HBM)
    anywhere = pl.BlockSpec(memory_space=pl.ANY)
    params = pltpu.CompilerParams(vmem_limit_bytes=VMEM_LIMIT)
    pos = position.reshape(1)
    half = planes // 2
    near, far = groups = tuple(range(half)), tuple(range(half, planes))
    packet = jax.ShapeDtypeStruct((half, rank, width), jnp.bfloat16)
    dense_blocks = pltpu.VMEM((half, own_blocks, rank, 128), jnp.float32)
    by_samples = jax.ShapeDtypeStruct((rank, samples_here), jnp.float32)
    square = jax.ShapeDtypeStruct((rank, rank), jnp.float32)

    def cost(flops, bytes_accessed):
        return pl.CostEstimate(flops=flops, bytes_accessed=bytes_accessed, transcendentals=0)

    geno, samples, table = pl.pallas_call(
        functools.partial(load_kernel, planes, per_owner, own_blocks),
        out_shape=(
            pltpu.VMEM((samples_here, snps_here), jnp.bfloat16),
            pltpu.VMEM((rank, samples_here), jnp.float32),
            pltpu.SMEM((PLANE * planes, per_owner), jnp.int32),
        ),
        in_specs=[smem, hbm, hbm, hbm],
        out_specs=(vmem, vmem, smem),
        scratch_shapes=[pltpu.SMEM(coverage.shape, jnp.int32), pltpu.SemaphoreType.DMA((3,))],
        compiler_params=pltpu.CompilerParams(
            vmem_limit_bytes=58 * 1024 * 1024 - 2 * samples_here * snps_here
        ),
        cost_estimate=cost(0, 2 * samples_here * snps_here),
        name="load_batch",
    )(pos, coverage, genotypes, sample_factors.T)

    snp_step = pl.pallas_call(
        functools.partial(steps_kernel, 0.5 * math.sqrt(rank) / samples_here, own_blocks),
        out_shape=jax.ShapeDtypeStruct((rank, own_snps), jnp.float32),
        in_specs=[smem, vmem],
        out_specs=vmem,
        compiler_params=params,
        name="snp_steps",
    )(pos, coverage)
    small = cost(0, 2 * 1024 * 1024)

    def pick(turns, held):
        return pl.pallas_call(
            functools.partial(pick_kernel, planes, turns, per_owner, own_blocks),
            out_shape=(packet,) * PLANE,
            in_specs=[smem] + [vmem] * half,
            out_specs=(vmem,) * PLANE,
            scratch_shapes=[dense_blocks],
            compiler_params=params,
            cost_estimate=small,
            name="pick_blocks",
        )(table, *[held[turn] for turn in turns])

    def plane_sum(terms, after):
        sums = pl.pallas_call(
            functools.partial(plane_sum_kernel, planes, per_owner, own_blocks),
            out_shape=tuple(
                jax.ShapeDtypeStruct((rank, own_snps), jnp.bfloat16 if turn % 2 else jnp.float32)
                for turn in range(planes)
            ),
            in_specs=[smem] + [vmem] * PLANE + [anywhere] * len(after),
            out_specs=(vmem,) * planes,
            scratch_shapes=[pltpu.VMEM((planes, own_blocks, rank, 128), jnp.float32)],
            compiler_params=params,
            cost_estimate=small,
            name="plane_sum",
        )(table, *terms, *after)
        return list(sums)

    def product(turns, mates, panels, before):
        share = len(turns) * len(mates) * samples_here * snps_here // devices
        return pl.pallas_call(
            functools.partial(product_kernel, turns, mates, not before, 256),
            out_shape=(by_samples, square),
            in_specs=[smem] + [vmem] * (1 + len(mates) + len(before)),
            out_specs=(vmem, vmem),
            compiler_params=params,
            cost_estimate=cost(8 * rank * share, 2 * share),
            name="panel_product",
        )(pos, geno, *[panels[turns][mate] for mate in mates], *before)

    def sample_update(samples, gradient, gram, outs):
        return pl.pallas_call(
            functools.partial(sample_kernel, sample_step),
            out_shape=outs,
            in_specs=[vmem] * 3,
            out_specs=(vmem,) * len(outs),
            compiler_params=params,
            cost_estimate=small,
            name="sample_update",
        )(samples, gradient, gram)

    def terms_for(mate, samples_bf16, gram, panels, after):
        share = samples_here * snps_here // PLANE
        return pl.pallas_call(
            functools.partial(term_kernel, groups, mate),
            out_shape=jax.ShapeDtypeStruct((planes, rank, width), jnp.bfloat16),
            in_specs=[smem] + [vmem] * (3 + len(groups)) + [anywhere] * len(after),
            out_specs=vmem,
            compiler_params=params,
            cost_estimate=cost(8 * rank * share, 2 * share),
            name="mate_terms",
        )(pos, geno, samples_bf16, gram, *[panels[turns][mate] for turns in groups], *after)

    def swap(x, turn):
        return lax.ppermute(x, "rows", [(r, r ^ turn) for r in range(devices)])

    def to_mate(x, mate):
        return swap(x, mate) if mate else x

    snps = snp_factors.T
    for iteration in range(ROUNDS):
        held = {0: snps.astype(jnp.bfloat16)}
        for turn in sorted(range(1, planes), key=lambda turn: (turn & (turn - 1), -turn)):
            bit = turn & -turn
            source = held[turn ^ bit]
            if iteration == 0 and turn != bit:
                source, _ = lax.optimization_barrier((source, samples))
            held[turn] = swap(source, bit * PLANE)
        panels = {}
        for turns in (near, far):
            packets = pick(turns, held)
            panels[turns] = [to_mate(packets[mate], mate) for mate in range(PLANE)]
        partial = ()
        for turns, mates in (
            (near, (0,)), (far, (0,)), (near, (1,)), (near, (2, 3)), (far, (1,)), (far, (2,)), (far, (3,))
        ):
            partial = product(turns, mates, panels, partial)
        rounded = (jax.ShapeDtypeStruct((rank, samples_here), jnp.bfloat16), square)
        if iteration < ROUNDS - 1:
            samples, *current = sample_update(samples, *partial, (by_samples,) + rounded)
            after = []
        else:
            current = sample_update(samples, *partial, rounded)
            samples, token = sample_update(
                samples, *partial, (by_samples, jax.ShapeDtypeStruct((8, 128), jnp.float32))
            )
            after = [token]
        terms = {mate: terms_for(mate, *current, panels, []) for mate in (2, 3, 1, 0)}
        sums = plane_sum([to_mate(terms[mate], mate) for mate in range(PLANE)], after)
        for turn in range(planes - 1, 0, -1):
            bit = turn & -turn
            arrived = swap(sums[turn].astype(jnp.bfloat16), bit * PLANE)
            sums[turn ^ bit] = sums[turn ^ bit] + arrived.astype(jnp.float32)
        snps = (1.0 - weight_decay) * snps + snp_step * sums[0]
    return (samples.T, snps.T)


def solution(mesh):
    placed = (
        P(("groups", "rows"), None),
        P(("groups", "rows"), None),
        P(("groups", "rows"), None),
        P("groups", None),
    )
    return jax.shard_map(
        on_device,
        mesh=mesh,
        in_specs=placed,
        out_specs=(P(("groups", "rows"), None), P(("groups", "rows"), None)),
        check_vma=False,
    )
```

```python
import functools
import math

import jax
import jax.numpy as jnp
from jax import lax
from jax.experimental import pallas as pl
from jax.experimental.pallas import tpu as pltpu
from jax.sharding import PartitionSpec as P

ROUNDS = 2

weight_decay = 0.02

PLANE = 8
NT = (((1,), (1,)), ((), ()))
NN = (((1,), (0,)), ((), ()))
VMEM_LIMIT = 24 * 1024 * 1024


def dot(a, b, dims):
    return lax.dot_general(a, b, dims, preferred_element_type=jnp.float32)


def split3(x):
    hi = x.astype(jnp.bfloat16)
    rest = x - hi.astype(jnp.float32)
    mid = rest.astype(jnp.bfloat16)
    lo = (rest - mid.astype(jnp.float32)).astype(jnp.bfloat16)
    return hi, mid, lo


def low_half(rows):
    return lax.broadcasted_iota(jnp.int32, (rows, 128), 1) < 64


def double(x, low):
    turned = pltpu.roll(x, 64, 1)
    return jnp.where(low, x, turned), jnp.where(low, turned, x)


def load_kernel(planes, per_owner, own_blocks, pos_ref, cov, geno, samples, geno_out, samples_out, table, listed, sems):
    copies = [
        pltpu.make_async_copy(cov, listed, sems.at[0]),
        pltpu.make_async_copy(samples, samples_out, sems.at[1]),
        pltpu.make_async_copy(geno, geno_out, sems.at[2]),
    ]
    for copy in copies:
        copy.start()
    copies[0].wait()
    for mate in range(PLANE):
        batch = lax.bitwise_xor(pos_ref[0], mate)
        for turn in range(planes):
            owner = lax.bitwise_xor(pos_ref[0], turn * PLANE)
            for p in range(per_owner):
                table[mate * planes + turn, p] = listed[batch, owner * per_owner + p] - owner * own_blocks
    for copy in copies[1:]:
        copy.wait()


def steps_kernel(scale, own_blocks, pos_ref, cov, steps):
    def step_of(block):
        seen = (cov[...] == pos_ref[0] * own_blocks + block).astype(jnp.float32)
        return scale / jnp.sum(jnp.sum(seen, axis=1, keepdims=True), axis=0, keepdims=True)

    low = low_half(steps.shape[0])
    for j in range(own_blocks // 2):
        steps[:, 128 * j:128 * (j + 1)] = jnp.where(low, step_of(2 * j), step_of(2 * j + 1))


def pick_kernel(planes, per_owner, own_blocks, table, *refs):
    held, packets, blocks = refs[:planes], refs[planes:-1], refs[-1]
    low = low_half(held[0].shape[0])
    for turn in range(planes):
        for j in range(own_blocks // 2):
            x = held[turn][:, 128 * j:128 * (j + 1)].astype(jnp.float32)
            blocks[turn, 2 * j], blocks[turn, 2 * j + 1] = double(x, low)
    for mate in range(PLANE):
        for turn in range(planes):
            for q in range(per_owner // 2):
                first = table[mate * planes + turn, 2 * q]
                second = table[mate * planes + turn, 2 * q + 1]
                pair = jnp.where(low, blocks[turn, first], blocks[turn, second])
                packets[mate][turn, :, 128 * q:128 * (q + 1)] = pair.astype(jnp.bfloat16)


def plane_sum_kernel(planes, per_owner, own_blocks, table, *refs):
    terms, sums, total = refs[:PLANE], refs[-1 - planes:-1], refs[-1]
    low = low_half(terms[0].shape[1])
    total[...] = jnp.zeros_like(total)
    for turn in range(planes):
        for mate in range(PLANE):
            for q in range(per_owner // 2):
                first = table[mate * planes + turn, 2 * q]
                second = table[mate * planes + turn, 2 * q + 1]
                pair = terms[mate][turn, :, 128 * q:128 * (q + 1)].astype(jnp.float32)
                total[turn, first] += jnp.where(low, pair, 0.0)
                total[turn, second] += jnp.where(low, 0.0, pair)
    for turn in range(planes):
        for j in range(own_blocks // 2):
            first, second = total[turn, 2 * j], total[turn, 2 * j + 1]
            both = jnp.where(low, first, second) + pltpu.roll(jnp.where(low, second, first), 64, 1)
            sums[turn][:, 128 * j:128 * (j + 1)] = both.astype(sums[turn].dtype)


def columns_of(pos, turn, mate, width):
    owner = lax.bitwise_xor(pos, turn * PLANE + mate)
    return pl.ds(pl.multiple_of(owner * width, width), width)


def product_kernel(mate, first, rows, pos_ref, geno, packet, *refs):
    before, (gradient, gram) = refs[:-2], refs[-2:]
    pos = pos_ref[0]
    planes, width = packet.shape[0], packet.shape[2]
    total = None if first else before[1][...]
    for turn in range(planes):
        term = dot(packet[turn], packet[turn], NT)
        total = term if total is None else total + term
    gram[...] = total
    for r in range(geno.shape[0] // rows):
        here = slice(r * rows, (r + 1) * rows)
        total = None if first else before[0][:, here]
        for turn in range(planes):
            term = dot(packet[turn], geno[here, columns_of(pos, turn, mate, width)], NT)
            total = term if total is None else total + term
        gradient[:, here] = total


def sample_kernel(sample_step, samples, gradient, gram, *outs):
    old = samples[...]
    old_bf16 = old.astype(jnp.bfloat16)
    total = gradient[...]
    for part in split3(gram[...]):
        total -= dot(part, old_bf16, NN)
    new = (1.0 - weight_decay) * old + sample_step * total
    *full, last = outs
    rounded = new.astype(jnp.bfloat16)
    for out in full:
        out[...] = new if out.dtype == jnp.float32 else rounded
    if last.shape[0] == last.shape[1]:
        last[...] = dot(rounded, rounded, NT)
    else:
        last[...] = jnp.zeros_like(last)


def term_kernel(mate, pos_ref, geno, samples, gram, packet, terms):
    pos = pos_ref[0]
    planes, width = packet.shape[0], packet.shape[2]
    parts = split3(gram[...])
    for turn in range(planes):
        term = dot(samples[...], geno[:, columns_of(pos, turn, mate, width)], NN)
        for part in parts:
            term -= dot(part, packet[turn], NN)
        terms[turn] = term.astype(jnp.bfloat16)


def on_device(genotypes, sample_factors, snp_factors, coverage):
    devices = lax.axis_size("rows")
    planes = devices // PLANE
    position = lax.axis_index("rows").astype(jnp.int32)
    samples_here, snps_here = genotypes.shape
    rank = sample_factors.shape[1]
    covered = coverage.shape[1]
    tile_size = snps_here // covered
    per_owner = covered // devices
    own_snps = snp_factors.shape[0]
    own_blocks = own_snps // tile_size
    width = per_owner * tile_size
    assert tile_size == 64 and per_owner % 2 == 0 and own_blocks % 2 == 0
    assert devices % PLANE == 0 and planes & (planes - 1) == 0

    sample_step = 0.5 * math.sqrt(rank) / (covered * tile_size)

    smem = pl.BlockSpec(memory_space=pltpu.SMEM)
    vmem = pl.BlockSpec(memory_space=pltpu.VMEM)
    hbm = pl.BlockSpec(memory_space=pltpu.HBM)
    anywhere = pl.BlockSpec(memory_space=pl.ANY)
    params = pltpu.CompilerParams(vmem_limit_bytes=VMEM_LIMIT)
    pos = position.reshape(1)
    packet = jax.ShapeDtypeStruct((planes, rank, width), jnp.bfloat16)
    dense_blocks = pltpu.VMEM((planes, own_blocks, rank, 128), jnp.float32)
    by_samples = jax.ShapeDtypeStruct((rank, samples_here), jnp.float32)
    square = jax.ShapeDtypeStruct((rank, rank), jnp.float32)

    def cost(flops, bytes_accessed):
        return pl.CostEstimate(flops=flops, bytes_accessed=bytes_accessed, transcendentals=0)

    geno, samples, table = pl.pallas_call(
        functools.partial(load_kernel, planes, per_owner, own_blocks),
        out_shape=(
            pltpu.VMEM((samples_here, snps_here), jnp.bfloat16),
            pltpu.VMEM((rank, samples_here), jnp.float32),
            pltpu.SMEM((PLANE * planes, per_owner), jnp.int32),
        ),
        in_specs=[smem, hbm, hbm, hbm],
        out_specs=(vmem, vmem, smem),
        scratch_shapes=[pltpu.SMEM(coverage.shape, jnp.int32), pltpu.SemaphoreType.DMA((3,))],
        compiler_params=pltpu.CompilerParams(
            vmem_limit_bytes=58 * 1024 * 1024 - 2 * samples_here * snps_here
        ),
        cost_estimate=cost(0, 2 * samples_here * snps_here),
        name="load_batch",
    )(pos, coverage, genotypes, sample_factors.T)

    snp_step = pl.pallas_call(
        functools.partial(steps_kernel, 0.5 * math.sqrt(rank) / samples_here, own_blocks),
        out_shape=jax.ShapeDtypeStruct((rank, own_snps), jnp.float32),
        in_specs=[smem, vmem],
        out_specs=vmem,
        compiler_params=params,
        name="snp_steps",
    )(pos, coverage)
    small = cost(0, 2 * 1024 * 1024)

    def pick(held):
        return pl.pallas_call(
            functools.partial(pick_kernel, planes, per_owner, own_blocks),
            out_shape=(packet,) * PLANE,
            in_specs=[smem] + [vmem] * planes,
            out_specs=(vmem,) * PLANE,
            scratch_shapes=[dense_blocks],
            compiler_params=params,
            cost_estimate=small,
            name="pick_blocks",
        )(table, *held)

    def plane_sum(terms, after):
        sums = pl.pallas_call(
            functools.partial(plane_sum_kernel, planes, per_owner, own_blocks),
            out_shape=tuple(
                jax.ShapeDtypeStruct((rank, own_snps), jnp.bfloat16 if turn % 2 else jnp.float32)
                for turn in range(planes)
            ),
            in_specs=[smem] + [vmem] * PLANE + [anywhere] * len(after),
            out_specs=(vmem,) * planes,
            scratch_shapes=[dense_blocks],
            compiler_params=params,
            cost_estimate=small,
            name="plane_sum",
        )(table, *terms, *after)
        return list(sums)

    def product(mate, panel, before):
        share = samples_here * snps_here // PLANE
        return pl.pallas_call(
            functools.partial(product_kernel, mate, not before, 256),
            out_shape=(by_samples, square),
            in_specs=[smem] + [vmem] * (2 + len(before)),
            out_specs=(vmem, vmem),
            compiler_params=params,
            cost_estimate=cost(8 * rank * share, 2 * share),
            name="panel_product",
        )(pos, geno, panel, *before)

    def sample_update(samples, gradient, gram, outs):
        return pl.pallas_call(
            functools.partial(sample_kernel, sample_step),
            out_shape=outs,
            in_specs=[vmem] * 3,
            out_specs=(vmem,) * len(outs),
            compiler_params=params,
            cost_estimate=small,
            name="sample_update",
        )(samples, gradient, gram)

    def terms_for(mate, samples_bf16, gram, panel):
        share = samples_here * snps_here // PLANE
        return pl.pallas_call(
            functools.partial(term_kernel, mate),
            out_shape=packet,
            in_specs=[smem] + [vmem] * 4,
            out_specs=vmem,
            compiler_params=params,
            cost_estimate=cost(8 * rank * share, 2 * share),
            name="mate_terms",
        )(pos, geno, samples_bf16, gram, panel)

    def swap(x, turn):
        return lax.ppermute(x, "rows", [(r, r ^ turn) for r in range(devices)])

    def to_mate(x, mate):
        return swap(x, mate) if mate else x

    snps = snp_factors.T
    for iteration in range(ROUNDS):
        held = {0: snps.astype(jnp.bfloat16)}
        for turn in sorted(range(1, planes), key=lambda turn: (turn & (turn - 1), -turn)):
            bit = turn & -turn
            source = held[turn ^ bit]
            if iteration == 0 and turn != bit:
                source, _ = lax.optimization_barrier((source, samples))
            held[turn] = swap(source, bit * PLANE)
        packets = pick([held[turn] for turn in range(planes)])
        panels = [to_mate(packets[mate], mate) for mate in range(PLANE)]
        partial = ()
        for mate in (0, 7, 6, 5, 4, 3, 2, 1):
            partial = product(mate, panels[mate], partial)
        rounded = (jax.ShapeDtypeStruct((rank, samples_here), jnp.bfloat16), square)
        if iteration < ROUNDS - 1:
            samples, *current = sample_update(samples, *partial, (by_samples,) + rounded)
            after = []
        else:
            current = sample_update(samples, *partial, rounded)
            samples, token = sample_update(
                samples, *partial, (by_samples, jax.ShapeDtypeStruct((8, 128), jnp.float32))
            )
            after = [token]
        sums = plane_sum(
            [to_mate(terms_for(mate, *current, panels[mate]), mate) for mate in range(PLANE)], after
        )
        for turn in range(planes - 1, 0, -1):
            bit = turn & -turn
            arrived = swap(sums[turn].astype(jnp.bfloat16), bit * PLANE)
            sums[turn ^ bit] = sums[turn ^ bit] + arrived.astype(jnp.float32)
        snps = (1.0 - weight_decay) * snps + snp_step * sums[0]
    return (samples.T, snps.T)


def solution(mesh):
    placed = (
        P(("groups", "rows"), None),
        P(("groups", "rows"), None),
        P(("groups", "rows"), None),
        P("groups", None),
    )
    return jax.shard_map(
        on_device,
        mesh=mesh,
        in_specs=placed,
        out_specs=(P(("groups", "rows"), None), P(("groups", "rows"), None)),
        check_vma=False,
    )
```

```python
import functools
import math

import jax
import jax.numpy as jnp
from jax import lax
from jax.experimental import pallas as pl
from jax.experimental.pallas import tpu as pltpu
from jax.sharding import PartitionSpec as P

ROUNDS = 2

weight_decay = 0.02

PLANE = 8
NT = (((1,), (1,)), ((), ()))
NN = (((1,), (0,)), ((), ()))
VMEM_LIMIT = 24 * 1024 * 1024


def dot(a, b, dims):
    return lax.dot_general(a, b, dims, preferred_element_type=jnp.float32)


def split3(x):
    hi = x.astype(jnp.bfloat16)
    rest = x - hi.astype(jnp.float32)
    mid = rest.astype(jnp.bfloat16)
    lo = (rest - mid.astype(jnp.float32)).astype(jnp.bfloat16)
    return hi, mid, lo


def low_half(rows):
    return lax.broadcasted_iota(jnp.int32, (rows, 128), 1) < 64


def double(x, low):
    turned = pltpu.roll(x, 64, 1)
    return jnp.where(low, x, turned), jnp.where(low, turned, x)


def load_kernel(planes, per_owner, own_blocks, pos_ref, cov, geno, samples, geno_out, samples_out, table, listed, sems):
    copies = [
        pltpu.make_async_copy(cov, listed, sems.at[0]),
        pltpu.make_async_copy(samples, samples_out, sems.at[1]),
        pltpu.make_async_copy(geno, geno_out, sems.at[2]),
    ]
    for copy in copies:
        copy.start()
    copies[0].wait()
    for mate in range(PLANE):
        batch = lax.bitwise_xor(pos_ref[0], mate)
        for turn in range(planes):
            owner = lax.bitwise_xor(pos_ref[0], turn * PLANE)
            for p in range(per_owner):
                table[mate * planes + turn, p] = listed[batch, owner * per_owner + p] - owner * own_blocks
    for copy in copies[1:]:
        copy.wait()


def steps_kernel(scale, own_blocks, pos_ref, cov, *steps):
    low = low_half(steps[0].shape[0])
    for turn, out in enumerate(steps):
        owner = lax.bitwise_xor(pos_ref[0], turn * PLANE)

        def step_of(block):
            seen = (cov[...] == owner * own_blocks + block).astype(jnp.float32)
            return scale / jnp.sum(jnp.sum(seen, axis=1, keepdims=True), axis=0, keepdims=True)

        for j in range(own_blocks // 2):
            out[:, 128 * j:128 * (j + 1)] = jnp.where(low, step_of(2 * j), step_of(2 * j + 1))


def pick_kernel(planes, per_owner, own_blocks, table, *refs):
    held, packets, blocks = refs[:planes], refs[planes:-1], refs[-1]
    low = low_half(held[0].shape[0])
    for turn in range(planes):
        for j in range(own_blocks // 2):
            x = held[turn][:, 128 * j:128 * (j + 1)].astype(jnp.float32)
            blocks[turn, 2 * j], blocks[turn, 2 * j + 1] = double(x, low)
    for mate in range(PLANE):
        for turn in range(planes):
            for q in range(per_owner // 2):
                first = table[mate * planes + turn, 2 * q]
                second = table[mate * planes + turn, 2 * q + 1]
                pair = jnp.where(low, blocks[turn, first], blocks[turn, second])
                packets[mate][turn, :, 128 * q:128 * (q + 1)] = pair.astype(jnp.bfloat16)


def plane_sum_kernel(planes, n_outs, per_owner, own_blocks, table, *refs):
    terms, sums, total = refs[:PLANE], refs[-1 - n_outs:-1], refs[-1]
    low = low_half(terms[0].shape[1])
    total[...] = jnp.zeros_like(total)
    for turn in range(planes):
        for mate in range(PLANE):
            for q in range(per_owner // 2):
                first = table[mate * planes + turn, 2 * q]
                second = table[mate * planes + turn, 2 * q + 1]
                pair = terms[mate][turn, :, 128 * q:128 * (q + 1)].astype(jnp.float32)
                total[turn, first] += jnp.where(low, pair, 0.0)
                total[turn, second] += jnp.where(low, 0.0, pair)
    for turn in range(planes):
        for j in range(own_blocks // 2):
            first, second = total[turn, 2 * j], total[turn, 2 * j + 1]
            both = jnp.where(low, first, second) + pltpu.roll(jnp.where(low, second, first), 64, 1)
            columns = slice(128 * j, 128 * (j + 1))
            sums[turn][:, columns] = both.astype(sums[turn].dtype)
            if n_outs > planes:
                sums[planes][planes - 1 - turn, :, columns] = both.astype(jnp.bfloat16)


def columns_of(pos, turn, mate, width):
    owner = lax.bitwise_xor(pos, turn * PLANE + mate)
    return pl.ds(pl.multiple_of(owner * width, width), width)


def product_kernel(mate, first, rows, pos_ref, geno, packet, *refs):
    before, (gradient, gram) = refs[:-2], refs[-2:]
    pos = pos_ref[0]
    planes, width = packet.shape[0], packet.shape[2]
    total = None if first else before[1][...]
    for turn in range(planes):
        term = dot(packet[turn], packet[turn], NT)
        total = term if total is None else total + term
    gram[...] = total
    for r in range(geno.shape[0] // rows):
        here = slice(r * rows, (r + 1) * rows)
        total = None if first else before[0][:, here]
        for turn in range(planes):
            term = dot(packet[turn], geno[here, columns_of(pos, turn, mate, width)], NT)
            total = term if total is None else total + term
        gradient[:, here] = total


def sample_kernel(sample_step, samples, gradient, gram, *outs):
    old = samples[...]
    old_bf16 = old.astype(jnp.bfloat16)
    total = gradient[...]
    for part in split3(gram[...]):
        total -= dot(part, old_bf16, NN)
    new = (1.0 - weight_decay) * old + sample_step * total
    *full, last = outs
    rounded = new.astype(jnp.bfloat16)
    for out in full:
        out[...] = new if out.dtype == jnp.float32 else rounded
    if last.shape[0] == last.shape[1]:
        last[...] = dot(rounded, rounded, NT)
    else:
        last[...] = jnp.zeros_like(last)


def term_kernel(mate, pos_ref, geno, samples, gram, packet, terms):
    pos = pos_ref[0]
    planes, width = packet.shape[0], packet.shape[2]
    parts = split3(gram[...])
    for turn in range(planes):
        term = dot(samples[...], geno[:, columns_of(pos, turn, mate, width)], NN)
        for part in parts:
            term -= dot(part, packet[turn], NN)
        terms[turn] = term.astype(jnp.bfloat16)


def on_device(genotypes, sample_factors, snp_factors, coverage):
    devices = lax.axis_size("rows")
    planes = devices // PLANE
    position = lax.axis_index("rows").astype(jnp.int32)
    samples_here, snps_here = genotypes.shape
    rank = sample_factors.shape[1]
    covered = coverage.shape[1]
    tile_size = snps_here // covered
    per_owner = covered // devices
    own_snps = snp_factors.shape[0]
    own_blocks = own_snps // tile_size
    width = per_owner * tile_size
    assert tile_size == 64 and per_owner % 2 == 0 and own_blocks % 2 == 0
    assert devices % PLANE == 0 and planes & (planes - 1) == 0

    sample_step = 0.5 * math.sqrt(rank) / (covered * tile_size)

    smem = pl.BlockSpec(memory_space=pltpu.SMEM)
    vmem = pl.BlockSpec(memory_space=pltpu.VMEM)
    hbm = pl.BlockSpec(memory_space=pltpu.HBM)
    anywhere = pl.BlockSpec(memory_space=pl.ANY)
    params = pltpu.CompilerParams(vmem_limit_bytes=VMEM_LIMIT)
    pos = position.reshape(1)
    packet = jax.ShapeDtypeStruct((planes, rank, width), jnp.bfloat16)
    dense_blocks = pltpu.VMEM((planes, own_blocks, rank, 128), jnp.float32)
    by_samples = jax.ShapeDtypeStruct((rank, samples_here), jnp.float32)
    square = jax.ShapeDtypeStruct((rank, rank), jnp.float32)

    def cost(flops, bytes_accessed):
        return pl.CostEstimate(flops=flops, bytes_accessed=bytes_accessed, transcendentals=0)

    geno, samples, table = pl.pallas_call(
        functools.partial(load_kernel, planes, per_owner, own_blocks),
        out_shape=(
            pltpu.VMEM((samples_here, snps_here), jnp.bfloat16),
            pltpu.VMEM((rank, samples_here), jnp.float32),
            pltpu.SMEM((PLANE * planes, per_owner), jnp.int32),
        ),
        in_specs=[smem, hbm, hbm, hbm],
        out_specs=(vmem, vmem, smem),
        scratch_shapes=[pltpu.SMEM(coverage.shape, jnp.int32), pltpu.SemaphoreType.DMA((3,))],
        compiler_params=pltpu.CompilerParams(
            vmem_limit_bytes=58 * 1024 * 1024 - 2 * samples_here * snps_here
        ),
        cost_estimate=cost(0, 2 * samples_here * snps_here),
        name="load_batch",
    )(pos, coverage, genotypes, sample_factors.T)

    by_snps = jax.ShapeDtypeStruct((rank, own_snps), jnp.float32)
    pairwise = planes == 2
    n_steps = 2 if pairwise else 1
    snp_steps = pl.pallas_call(
        functools.partial(steps_kernel, 0.5 * math.sqrt(rank) / samples_here, own_blocks),
        out_shape=(by_snps,) * n_steps,
        in_specs=[smem, vmem],
        out_specs=(vmem,) * n_steps,
        compiler_params=params,
        name="snp_steps",
    )(pos, coverage)
    small = cost(0, 2 * 1024 * 1024)

    def pick(held):
        return pl.pallas_call(
            functools.partial(pick_kernel, planes, per_owner, own_blocks),
            out_shape=(packet,) * PLANE,
            in_specs=[smem] + [vmem] * planes,
            out_specs=(vmem,) * PLANE,
            scratch_shapes=[dense_blocks],
            compiler_params=params,
            cost_estimate=small,
            name="pick_blocks",
        )(table, *held)

    def plane_sum(terms, after, both):
        outs = tuple(
            jax.ShapeDtypeStruct((rank, own_snps), jnp.bfloat16 if turn % 2 and not both else jnp.float32)
            for turn in range(planes)
        )
        if both:
            outs += (jax.ShapeDtypeStruct((planes, rank, own_snps), jnp.bfloat16),)
        sums = pl.pallas_call(
            functools.partial(plane_sum_kernel, planes, len(outs), per_owner, own_blocks),
            out_shape=outs,
            in_specs=[smem] + [vmem] * PLANE + [anywhere] * len(after),
            out_specs=(vmem,) * len(outs),
            scratch_shapes=[dense_blocks],
            compiler_params=params,
            cost_estimate=small,
            name="plane_sum",
        )(table, *terms, *after)
        return list(sums)

    def product(mate, panel, before):
        share = samples_here * snps_here // PLANE
        return pl.pallas_call(
            functools.partial(product_kernel, mate, not before, 256),
            out_shape=(by_samples, square),
            in_specs=[smem] + [vmem] * (2 + len(before)),
            out_specs=(vmem, vmem),
            compiler_params=params,
            cost_estimate=cost(8 * rank * share, 2 * share),
            name="panel_product",
        )(pos, geno, panel, *before)

    def sample_update(samples, gradient, gram, outs):
        return pl.pallas_call(
            functools.partial(sample_kernel, sample_step),
            out_shape=outs,
            in_specs=[vmem] * 3,
            out_specs=(vmem,) * len(outs),
            compiler_params=params,
            cost_estimate=small,
            name="sample_update",
        )(samples, gradient, gram)

    def terms_for(mate, samples_bf16, gram, panel):
        share = samples_here * snps_here // PLANE
        return pl.pallas_call(
            functools.partial(term_kernel, mate),
            out_shape=packet,
            in_specs=[smem] + [vmem] * 4,
            out_specs=vmem,
            compiler_params=params,
            cost_estimate=cost(8 * rank * share, 2 * share),
            name="mate_terms",
        )(pos, geno, samples_bf16, gram, panel)

    def swap(x, turn):
        return lax.ppermute(x, "rows", [(r, r ^ turn) for r in range(devices)])

    def to_mate(x, mate):
        return swap(x, mate) if mate else x

    def updated(old, step, total):
        return (1.0 - weight_decay) * old.astype(jnp.float32) + step * total

    snps = snp_factors.T
    held = None
    for iteration in range(ROUNDS):
        last = iteration == ROUNDS - 1
        if held is None:
            held = {0: snps.astype(jnp.bfloat16)}
            for turn in sorted(range(1, planes), key=lambda turn: (turn & (turn - 1), -turn)):
                bit = turn & -turn
                source = held[turn ^ bit]
                if iteration == 0 and turn != bit:
                    source, _ = lax.optimization_barrier((source, samples))
                held[turn] = swap(source, bit * PLANE)
        packets = pick([held[turn] for turn in range(planes)])
        panels = [to_mate(packets[mate], mate) for mate in range(PLANE)]
        partial = ()
        for mate in (0, 7, 6, 5, 4, 3, 2, 1):
            partial = product(mate, panels[mate], partial)
        rounded = (jax.ShapeDtypeStruct((rank, samples_here), jnp.bfloat16), square)
        if not last:
            samples, *current = sample_update(samples, *partial, (by_samples,) + rounded)
            after = []
        else:
            current = sample_update(samples, *partial, rounded)
            samples, token = sample_update(
                samples, *partial, (by_samples, jax.ShapeDtypeStruct((8, 128), jnp.float32))
            )
            after = [token]
        both = pairwise and not last
        sums = plane_sum(
            [to_mate(terms_for(mate, *current, panels[mate]), mate) for mate in range(PLANE)], after, both
        )
        if both:
            arrived = swap(sums[2], PLANE)
            snps = updated(snps, snp_steps[0], sums[0] + arrived[0].astype(jnp.float32))
            other = updated(held[1], snp_steps[1], sums[1] + arrived[1].astype(jnp.float32))
            held = {0: snps.astype(jnp.bfloat16), 1: other.astype(jnp.bfloat16)}
            continue
        for turn in range(planes - 1, 0, -1):
            bit = turn & -turn
            arrived = swap(sums[turn].astype(jnp.bfloat16), bit * PLANE)
            sums[turn ^ bit] = sums[turn ^ bit] + arrived.astype(jnp.float32)
        snps = updated(snps, snp_steps[0], sums[0])
        held = None
    return (samples.T, snps.T)


def solution(mesh):
    placed = (
        P(("groups", "rows"), None),
        P(("groups", "rows"), None),
        P(("groups", "rows"), None),
        P("groups", None),
    )
    return jax.shard_map(
        on_device,
        mesh=mesh,
        in_specs=placed,
        out_specs=(P(("groups", "rows"), None), P(("groups", "rows"), None)),
        check_vma=False,
    )
```

```python
import functools
import math

import jax
import jax.numpy as jnp
from jax import lax
from jax.experimental import pallas as pl
from jax.experimental.pallas import tpu as pltpu
from jax.sharding import PartitionSpec as P

ROUNDS = 2

weight_decay = 0.02

MATES = (0, 2, 4, 6)
REST = 8
NT = (((1,), (1,)), ((), ()))
NN = (((1,), (0,)), ((), ()))
VMEM_LIMIT = 24 * 1024 * 1024


def dot(a, b, dims):
    return lax.dot_general(a, b, dims, preferred_element_type=jnp.float32)


def split3(x):
    hi = x.astype(jnp.bfloat16)
    rest = x - hi.astype(jnp.float32)
    mid = rest.astype(jnp.bfloat16)
    lo = (rest - mid.astype(jnp.float32)).astype(jnp.bfloat16)
    return hi, mid, lo


def low_half(rows):
    return lax.broadcasted_iota(jnp.int32, (rows, 128), 1) < 64


def double(x, low):
    turned = pltpu.roll(x, 64, 1)
    return jnp.where(low, x, turned), jnp.where(low, turned, x)


def load_kernel(turns, per_owner, own_blocks, pos_ref, cov, geno, samples, geno_out, samples_out, table, listed, sems):
    copies = [
        pltpu.make_async_copy(cov, listed, sems.at[0]),
        pltpu.make_async_copy(samples, samples_out, sems.at[1]),
        pltpu.make_async_copy(geno, geno_out, sems.at[2]),
    ]
    for copy in copies:
        copy.start()
    copies[0].wait()
    for m, mate in enumerate(MATES):
        batch = lax.bitwise_xor(pos_ref[0], mate)
        for t, turn in enumerate(turns):
            owner = lax.bitwise_xor(pos_ref[0], turn)
            for p in range(per_owner):
                table[m * len(turns) + t, p] = listed[batch, owner * per_owner + p] - owner * own_blocks
    for copy in copies[1:]:
        copy.wait()


def steps_kernel(scale, own_blocks, pos_ref, cov, *steps):
    low = low_half(steps[0].shape[0])
    for turn, out in enumerate(steps):
        owner = lax.bitwise_xor(pos_ref[0], turn * REST)

        def step_of(block):
            seen = (cov[...] == owner * own_blocks + block).astype(jnp.float32)
            return scale / jnp.sum(jnp.sum(seen, axis=1, keepdims=True), axis=0, keepdims=True)

        for j in range(own_blocks // 2):
            out[:, 128 * j:128 * (j + 1)] = jnp.where(low, step_of(2 * j), step_of(2 * j + 1))


def pick_kernel(places, per_owner, own_blocks, table, *refs):
    packets, blocks = refs[-1 - len(MATES):-1], refs[-1]
    turns = len(places)
    low = low_half(blocks.shape[2])
    for t, (ref, at) in enumerate(places):
        for j in range(own_blocks // 2):
            columns = slice(128 * j, 128 * (j + 1))
            x = (refs[ref][:, columns] if at is None else refs[ref][at, :, columns]).astype(jnp.float32)
            blocks[t, 2 * j], blocks[t, 2 * j + 1] = double(x, low)
    for m in range(len(MATES)):
        for t in range(turns):
            for q in range(per_owner // 2):
                first, second = table[m * turns + t, 2 * q], table[m * turns + t, 2 * q + 1]
                pair = jnp.where(low, blocks[t, first], blocks[t, second])
                packets[m][t, :, 128 * q:128 * (q + 1)] = pair.astype(jnp.bfloat16)


def mates_sum_kernel(turns, per_owner, own_blocks, table, *refs):
    terms, sums, total = refs[:len(MATES)], refs[-2 - turns // 2:-1], refs[-1]
    low = low_half(terms[0].shape[1])
    total[...] = jnp.zeros_like(total)
    for t in range(turns):
        for m in range(len(MATES)):
            for q in range(per_owner // 2):
                first, second = table[m * turns + t, 2 * q], table[m * turns + t, 2 * q + 1]
                pair = terms[m][t, :, 128 * q:128 * (q + 1)].astype(jnp.float32)
                total[t, first] += jnp.where(low, pair, 0.0)
                total[t, second] += jnp.where(low, 0.0, pair)
    for t in range(turns):
        for j in range(own_blocks // 2):
            first, second = total[t, 2 * j], total[t, 2 * j + 1]
            both = jnp.where(low, first, second) + pltpu.roll(jnp.where(low, second, first), 64, 1)
            columns = slice(128 * j, 128 * (j + 1))
            if t % 2:
                sums[-1][t // 2, :, columns] = both.astype(jnp.bfloat16)
            else:
                sums[t // 2][:, columns] = both


def add_kernel(own, other, arrived, own_sum, other_sum, swapped):
    own_sum[...] = own[...] + arrived[0].astype(jnp.float32)
    other_sum[...] = other[...] + arrived[1].astype(jnp.float32)
    swapped[0] = other_sum[...].astype(jnp.bfloat16)
    swapped[1] = own_sum[...].astype(jnp.bfloat16)


def update_kernel(own_sum, other_sum, arrived, own_step, other_step, snps, other_snps, new_snps, held):
    kept = 1.0 - weight_decay
    own_total = own_sum[...] + arrived[0].astype(jnp.float32)
    other_total = other_sum[...] + arrived[1].astype(jnp.float32)
    new_snps[...] = kept * snps[...] + own_step[...] * own_total
    held[0] = new_snps[...].astype(jnp.bfloat16)
    other = kept * other_snps[...].astype(jnp.float32) + other_step[...] * other_total
    held[1] = other.astype(jnp.bfloat16)


def turns_of(devices):
    return [high + core for high in range(0, devices, REST) for core in (0, 1)]


def columns_of(pos, turn, mate, width):
    owner = lax.bitwise_xor(pos, turn ^ mate)
    return pl.ds(pl.multiple_of(owner * width, width), width)


def product_kernel(turns, mate, first, rows, pos_ref, geno, packet, *refs):
    before, (gradient, gram) = refs[:-2], refs[-2:]
    pos = pos_ref[0]
    width = packet.shape[2]
    total = None if first else before[1][...]
    for t in range(len(turns)):
        term = dot(packet[t], packet[t], NT)
        total = term if total is None else total + term
    gram[...] = total
    for r in range(geno.shape[0] // rows):
        here = slice(r * rows, (r + 1) * rows)
        total = None if first else before[0][:, here]
        for t, turn in enumerate(turns):
            term = dot(packet[t], geno[here, columns_of(pos, turn, mate, width)], NT)
            total = term if total is None else total + term
        gradient[:, here] = total


def sample_kernel(sample_step, samples, gradient, gram, *outs):
    old = samples[...]
    old_bf16 = old.astype(jnp.bfloat16)
    total = gradient[...]
    for part in split3(gram[...]):
        total -= dot(part, old_bf16, NN)
    new = (1.0 - weight_decay) * old + sample_step * total
    *full, last = outs
    rounded = new.astype(jnp.bfloat16)
    for out in full:
        out[...] = new if out.dtype == jnp.float32 else rounded
    if last.shape[0] == last.shape[1]:
        last[...] = dot(rounded, rounded, NT)
    else:
        last[...] = jnp.zeros_like(last)


def term_kernel(turns, mate, pos_ref, geno, samples, gram, packet, terms):
    pos = pos_ref[0]
    width = packet.shape[2]
    parts = split3(gram[...])
    for t, turn in enumerate(turns):
        term = dot(samples[...], geno[:, columns_of(pos, turn, mate, width)], NN)
        for part in parts:
            term -= dot(part, packet[t], NN)
        terms[t] = term.astype(jnp.bfloat16)


def on_device(genotypes, sample_factors, snp_factors, coverage):
    devices = lax.axis_size("rows")
    turns = turns_of(devices)
    highs = len(turns) // 2
    position = lax.axis_index("rows").astype(jnp.int32)
    samples_here, snps_here = genotypes.shape
    rank = sample_factors.shape[1]
    covered = coverage.shape[1]
    tile_size = snps_here // covered
    per_owner = covered // devices
    own_snps = snp_factors.shape[0]
    own_blocks = own_snps // tile_size
    width = per_owner * tile_size
    assert tile_size == 64 and per_owner % 2 == 0 and own_blocks % 2 == 0
    assert devices % REST == 0 and devices & (devices - 1) == 0

    sample_step = 0.5 * math.sqrt(rank) / (covered * tile_size)

    smem = pl.BlockSpec(memory_space=pltpu.SMEM)
    vmem = pl.BlockSpec(memory_space=pltpu.VMEM)
    hbm = pl.BlockSpec(memory_space=pltpu.HBM)
    anywhere = pl.BlockSpec(memory_space=pl.ANY)
    params = pltpu.CompilerParams(vmem_limit_bytes=VMEM_LIMIT)
    pos = position.reshape(1)
    packet = jax.ShapeDtypeStruct((len(turns), rank, width), jnp.bfloat16)
    dense_blocks = pltpu.VMEM((len(turns), own_blocks, rank, 128), jnp.float32)
    by_samples = jax.ShapeDtypeStruct((rank, samples_here), jnp.float32)
    square = jax.ShapeDtypeStruct((rank, rank), jnp.float32)

    def cost(flops, bytes_accessed):
        return pl.CostEstimate(flops=flops, bytes_accessed=bytes_accessed, transcendentals=0)

    geno, samples, table = pl.pallas_call(
        functools.partial(load_kernel, turns, per_owner, own_blocks),
        out_shape=(
            pltpu.VMEM((samples_here, snps_here), jnp.bfloat16),
            pltpu.VMEM((rank, samples_here), jnp.float32),
            pltpu.SMEM((len(MATES) * len(turns), per_owner), jnp.int32),
        ),
        in_specs=[smem, hbm, hbm, hbm],
        out_specs=(vmem, vmem, smem),
        scratch_shapes=[pltpu.SMEM(coverage.shape, jnp.int32), pltpu.SemaphoreType.DMA((3,))],
        compiler_params=pltpu.CompilerParams(
            vmem_limit_bytes=58 * 1024 * 1024 - 2 * samples_here * snps_here
        ),
        cost_estimate=cost(0, 2 * samples_here * snps_here),
        name="load_batch",
    )(pos, coverage, genotypes, sample_factors.T)

    by_snps = jax.ShapeDtypeStruct((rank, own_snps), jnp.float32)
    pairwise = highs == 2
    n_steps = 2 if pairwise else 1
    snp_steps = pl.pallas_call(
        functools.partial(steps_kernel, 0.5 * math.sqrt(rank) / samples_here, own_blocks),
        out_shape=(by_snps,) * n_steps,
        in_specs=[smem, vmem],
        out_specs=(vmem,) * n_steps,
        compiler_params=params,
        name="snp_steps",
    )(pos, coverage)
    small = cost(0, 2 * 1024 * 1024)

    def pick(arrays, places):
        return pl.pallas_call(
            functools.partial(pick_kernel, places, per_owner, own_blocks),
            out_shape=(packet,) * len(MATES),
            in_specs=[smem] + [vmem] * len(arrays),
            out_specs=(vmem,) * len(MATES),
            scratch_shapes=[dense_blocks],
            compiler_params=params,
            cost_estimate=small,
            name="pick_blocks",
        )(table, *arrays)

    def mates_sum(terms, after):
        *sums, for_core = pl.pallas_call(
            functools.partial(mates_sum_kernel, len(turns), per_owner, own_blocks),
            out_shape=(by_snps,) * highs + (jax.ShapeDtypeStruct((highs, rank, own_snps), jnp.bfloat16),),
            in_specs=[smem] + [vmem] * len(MATES) + [anywhere] * len(after),
            out_specs=(vmem,) * (highs + 1),
            scratch_shapes=[dense_blocks],
            compiler_params=params,
            cost_estimate=small,
            name="mates_sum",
        )(table, *terms, *after)
        return sums, for_core

    two_snps = jax.ShapeDtypeStruct((2, rank, own_snps), jnp.bfloat16)
    add_core = pl.pallas_call(
        add_kernel,
        out_shape=(by_snps, by_snps, two_snps),
        in_specs=[vmem] * 3,
        out_specs=(vmem,) * 3,
        compiler_params=params,
        name="add_core",
    )
    owners_update = pl.pallas_call(
        update_kernel,
        out_shape=(by_snps, two_snps),
        in_specs=[vmem] * 7,
        out_specs=(vmem,) * 2,
        compiler_params=params,
        name="owners_update",
    )

    def product(mate, panel, before):
        share = samples_here * snps_here // len(MATES)
        return pl.pallas_call(
            functools.partial(product_kernel, turns, mate, not before, 256),
            out_shape=(by_samples, square),
            in_specs=[smem] + [vmem] * (2 + len(before)),
            out_specs=(vmem, vmem),
            compiler_params=params,
            cost_estimate=cost(8 * rank * share, 2 * share),
            name="panel_product",
        )(pos, geno, panel, *before)

    def sample_update(samples, gradient, gram, outs):
        return pl.pallas_call(
            functools.partial(sample_kernel, sample_step),
            out_shape=outs,
            in_specs=[vmem] * 3,
            out_specs=(vmem,) * len(outs),
            compiler_params=params,
            cost_estimate=small,
            name="sample_update",
        )(samples, gradient, gram)

    def terms_for(mate, samples_bf16, gram, panel):
        share = samples_here * snps_here // len(MATES)
        return pl.pallas_call(
            functools.partial(term_kernel, turns, mate),
            out_shape=packet,
            in_specs=[smem] + [vmem] * 4,
            out_specs=vmem,
            compiler_params=params,
            cost_estimate=cost(8 * rank * share, 2 * share),
            name="mate_terms",
        )(pos, geno, samples_bf16, gram, panel)

    def swap(x, turn):
        return lax.ppermute(x, "rows", [(r, r ^ turn) for r in range(devices)])

    def to_mate(x, mate):
        return swap(x, mate) if mate else x

    snps = snp_factors.T
    held = None
    for iteration in range(ROUNDS):
        last = iteration == ROUNDS - 1
        if held is None:
            held = {0: snps.astype(jnp.bfloat16)}
            for high in sorted(range(1, highs), key=lambda high: (high & (high - 1), -high)):
                bit = high & -high
                held[high] = swap(held[high ^ bit], bit * REST)
            arrays = []
            for high in range(highs):
                source = held[high]
                if iteration == 0 and high:
                    source, _ = lax.optimization_barrier((source, samples))
                arrays += [held[high], swap(source, 1)]
            places = [(i, None) for i in range(len(turns))]
        else:
            arrays = [held, swap(held, 1)]
            places = [(t % 2, t // 2) for t in range(len(turns))]
        packets = pick(arrays, places)
        panels = [to_mate(x, mate) for x, mate in zip(packets, MATES)]
        partial = ()
        for m in (0, 3, 2, 1):
            partial = product(MATES[m], panels[m], partial)
        rounded = (jax.ShapeDtypeStruct((rank, samples_here), jnp.bfloat16), square)
        if not last:
            samples, *current = sample_update(samples, *partial, (by_samples,) + rounded)
            after = []
        else:
            current = sample_update(samples, *partial, rounded)
            samples, token = sample_update(
                samples, *partial, (by_samples, jax.ShapeDtypeStruct((8, 128), jnp.float32))
            )
            after = [token]
        sums, for_core = mates_sum(
            [to_mate(terms_for(mate, *current, x), mate) for x, mate in zip(panels, MATES)], after
        )
        arrived = swap(for_core, 1)
        if pairwise and not last:
            own_sum, other_sum, swapped = add_core(*sums, arrived)
            snps, held = owners_update(
                own_sum, other_sum, swap(swapped, REST), *snp_steps, snps, held[1]
            )
            continue
        sums = [x + arrived[high].astype(jnp.float32) for high, x in enumerate(sums)]
        for high in range(highs - 1, 0, -1):
            bit = high & -high
            sums[high ^ bit] += swap(sums[high].astype(jnp.bfloat16), bit * REST).astype(jnp.float32)
        snps = (1.0 - weight_decay) * snps + snp_steps[0] * sums[0]
        held = None
    return (samples.T, snps.T)


def solution(mesh):
    placed = (
        P(("groups", "rows"), None),
        P(("groups", "rows"), None),
        P(("groups", "rows"), None),
        P("groups", None),
    )
    return jax.shard_map(
        on_device,
        mesh=mesh,
        in_specs=placed,
        out_specs=(P(("groups", "rows"), None), P(("groups", "rows"), None)),
        check_vma=False,
    )
```

```python
import functools
import math

import jax
import jax.numpy as jnp
from jax import lax
from jax.experimental import pallas as pl
from jax.experimental.pallas import tpu as pltpu
from jax.sharding import PartitionSpec as P

ROUNDS = 2

weight_decay = 0.02

MATES = (0, 2, 4, 6)
REST = 8
NT = (((1,), (1,)), ((), ()))
NN = (((1,), (0,)), ((), ()))
VMEM_LIMIT = 24 * 1024 * 1024


def dot(a, b, dims):
    return lax.dot_general(a, b, dims, preferred_element_type=jnp.float32)


def split3(x):
    hi = x.astype(jnp.bfloat16)
    rest = x - hi.astype(jnp.float32)
    mid = rest.astype(jnp.bfloat16)
    lo = (rest - mid.astype(jnp.float32)).astype(jnp.bfloat16)
    return hi, mid, lo


def low_half(rows):
    return lax.broadcasted_iota(jnp.int32, (rows, 128), 1) < 64


def double(x, low):
    turned = pltpu.roll(x, 64, 1)
    return jnp.where(low, x, turned), jnp.where(low, turned, x)


def load_kernel(turns, per_owner, own_blocks, pos_ref, cov, geno, samples, geno_out, samples_out, table, listed, sems):
    copies = [
        pltpu.make_async_copy(cov, listed, sems.at[0]),
        pltpu.make_async_copy(samples, samples_out, sems.at[1]),
        pltpu.make_async_copy(geno, geno_out, sems.at[2]),
    ]
    for copy in copies:
        copy.start()
    copies[0].wait()
    for m, mate in enumerate(MATES):
        batch = lax.bitwise_xor(pos_ref[0], mate)
        for t, turn in enumerate(turns):
            owner = lax.bitwise_xor(pos_ref[0], turn)
            for p in range(per_owner):
                table[m * len(turns) + t, p] = listed[batch, owner * per_owner + p] - owner * own_blocks
    for copy in copies[1:]:
        copy.wait()


def steps_kernel(scale, own_blocks, pos_ref, cov, *steps):
    low = low_half(steps[0].shape[0])
    for turn, out in enumerate(steps):
        owner = lax.bitwise_xor(pos_ref[0], turn * REST)

        def step_of(block):
            seen = (cov[...] == owner * own_blocks + block).astype(jnp.float32)
            return scale / jnp.sum(jnp.sum(seen, axis=1, keepdims=True), axis=0, keepdims=True)

        for j in range(own_blocks // 2):
            out[:, 128 * j:128 * (j + 1)] = jnp.where(low, step_of(2 * j), step_of(2 * j + 1))


def pick_kernel(turns, group, places, per_owner, own_blocks, table, *refs):
    packets, blocks = refs[-1 - len(MATES):-1], refs[-1]
    low = low_half(blocks.shape[2])
    for i, (ref, at) in enumerate(places):
        for j in range(own_blocks // 2):
            columns = slice(128 * j, 128 * (j + 1))
            x = (refs[ref][:, columns] if at is None else refs[ref][at, :, columns]).astype(jnp.float32)
            blocks[i, 2 * j], blocks[i, 2 * j + 1] = double(x, low)
    for m in range(len(MATES)):
        for i, t in enumerate(group):
            for q in range(per_owner // 2):
                first, second = table[m * turns + t, 2 * q], table[m * turns + t, 2 * q + 1]
                pair = jnp.where(low, blocks[i, first], blocks[i, second])
                packets[m][i, :, 128 * q:128 * (q + 1)] = pair.astype(jnp.bfloat16)


def mates_sum_kernel(turns, per_owner, own_blocks, table, *refs):
    terms, sums, total = refs[:len(MATES)], refs[-2 - turns // 2:-1], refs[-1]
    low = low_half(terms[0].shape[1])
    total[...] = jnp.zeros_like(total)
    for t in range(turns):
        for m in range(len(MATES)):
            for q in range(per_owner // 2):
                first, second = table[m * turns + t, 2 * q], table[m * turns + t, 2 * q + 1]
                pair = terms[m][t, :, 128 * q:128 * (q + 1)].astype(jnp.float32)
                total[t, first] += jnp.where(low, pair, 0.0)
                total[t, second] += jnp.where(low, 0.0, pair)
    for t in range(turns):
        for j in range(own_blocks // 2):
            first, second = total[t, 2 * j], total[t, 2 * j + 1]
            both = jnp.where(low, first, second) + pltpu.roll(jnp.where(low, second, first), 64, 1)
            columns = slice(128 * j, 128 * (j + 1))
            if t % 2:
                sums[-1][t // 2, :, columns] = both.astype(jnp.bfloat16)
            else:
                sums[t // 2][:, columns] = both


def add_kernel(own, other, arrived, own_sum, other_sum, swapped):
    own_sum[...] = own[...] + arrived[0].astype(jnp.float32)
    other_sum[...] = other[...] + arrived[1].astype(jnp.float32)
    swapped[0] = other_sum[...].astype(jnp.bfloat16)
    swapped[1] = own_sum[...].astype(jnp.bfloat16)


def update_kernel(own_sum, other_sum, arrived, own_step, other_step, snps, other_snps, new_snps, held):
    kept = 1.0 - weight_decay
    own_total = own_sum[...] + arrived[0].astype(jnp.float32)
    other_total = other_sum[...] + arrived[1].astype(jnp.float32)
    new_snps[...] = kept * snps[...] + own_step[...] * own_total
    held[0] = new_snps[...].astype(jnp.bfloat16)
    other = kept * other_snps[...].astype(jnp.float32) + other_step[...] * other_total
    held[1] = other.astype(jnp.bfloat16)


def turns_of(devices):
    return [high + core for high in range(0, devices, REST) for core in (0, 1)]


def columns_of(pos, turn, mate, width):
    owner = lax.bitwise_xor(pos, turn ^ mate)
    return pl.ds(pl.multiple_of(owner * width, width), width)


def product_kernel(turns, mate, first, rows, pos_ref, geno, packet, *refs):
    before, (gradient, gram) = refs[:-2], refs[-2:]
    pos = pos_ref[0]
    width = packet.shape[2]
    total = None if first else before[1][...]
    for t in range(len(turns)):
        term = dot(packet[t], packet[t], NT)
        total = term if total is None else total + term
    gram[...] = total
    for r in range(geno.shape[0] // rows):
        here = slice(r * rows, (r + 1) * rows)
        total = None if first else before[0][:, here]
        for t, turn in enumerate(turns):
            term = dot(packet[t], geno[here, columns_of(pos, turn, mate, width)], NT)
            total = term if total is None else total + term
        gradient[:, here] = total


def sample_kernel(sample_step, samples, gradient, gram, *outs):
    old = samples[...]
    old_bf16 = old.astype(jnp.bfloat16)
    total = gradient[...]
    for part in split3(gram[...]):
        total -= dot(part, old_bf16, NN)
    new = (1.0 - weight_decay) * old + sample_step * total
    *full, last = outs
    rounded = new.astype(jnp.bfloat16)
    for out in full:
        out[...] = new if out.dtype == jnp.float32 else rounded
    if last.shape[0] == last.shape[1]:
        last[...] = dot(rounded, rounded, NT)
    else:
        last[...] = jnp.zeros_like(last)


def term_kernel(turns, groups, mate, pos_ref, geno, samples, gram, *refs):
    packets, terms = refs[:-1], refs[-1]
    pos = pos_ref[0]
    width = terms.shape[2]
    parts = split3(gram[...])
    for packet, group in zip(packets, groups):
        for i, t in enumerate(group):
            term = dot(samples[...], geno[:, columns_of(pos, turns[t], mate, width)], NN)
            for part in parts:
                term -= dot(part, packet[i], NN)
            terms[t] = term.astype(jnp.bfloat16)


def on_device(genotypes, sample_factors, snp_factors, coverage):
    devices = lax.axis_size("rows")
    turns = turns_of(devices)
    highs = len(turns) // 2
    position = lax.axis_index("rows").astype(jnp.int32)
    samples_here, snps_here = genotypes.shape
    rank = sample_factors.shape[1]
    covered = coverage.shape[1]
    tile_size = snps_here // covered
    per_owner = covered // devices
    own_snps = snp_factors.shape[0]
    own_blocks = own_snps // tile_size
    width = per_owner * tile_size
    assert tile_size == 64 and per_owner % 2 == 0 and own_blocks % 2 == 0
    assert devices % REST == 0 and devices & (devices - 1) == 0

    sample_step = 0.5 * math.sqrt(rank) / (covered * tile_size)

    smem = pl.BlockSpec(memory_space=pltpu.SMEM)
    vmem = pl.BlockSpec(memory_space=pltpu.VMEM)
    hbm = pl.BlockSpec(memory_space=pltpu.HBM)
    anywhere = pl.BlockSpec(memory_space=pl.ANY)
    params = pltpu.CompilerParams(vmem_limit_bytes=VMEM_LIMIT)
    pos = position.reshape(1)
    packet = jax.ShapeDtypeStruct((len(turns), rank, width), jnp.bfloat16)
    dense_blocks = pltpu.VMEM((len(turns), own_blocks, rank, 128), jnp.float32)
    by_samples = jax.ShapeDtypeStruct((rank, samples_here), jnp.float32)
    square = jax.ShapeDtypeStruct((rank, rank), jnp.float32)

    def cost(flops, bytes_accessed):
        return pl.CostEstimate(flops=flops, bytes_accessed=bytes_accessed, transcendentals=0)

    geno, samples, table = pl.pallas_call(
        functools.partial(load_kernel, turns, per_owner, own_blocks),
        out_shape=(
            pltpu.VMEM((samples_here, snps_here), jnp.bfloat16),
            pltpu.VMEM((rank, samples_here), jnp.float32),
            pltpu.SMEM((len(MATES) * len(turns), per_owner), jnp.int32),
        ),
        in_specs=[smem, hbm, hbm, hbm],
        out_specs=(vmem, vmem, smem),
        scratch_shapes=[pltpu.SMEM(coverage.shape, jnp.int32), pltpu.SemaphoreType.DMA((3,))],
        compiler_params=pltpu.CompilerParams(
            vmem_limit_bytes=58 * 1024 * 1024 - 2 * samples_here * snps_here
        ),
        cost_estimate=cost(0, 2 * samples_here * snps_here),
        name="load_batch",
    )(pos, coverage, genotypes, sample_factors.T)

    by_snps = jax.ShapeDtypeStruct((rank, own_snps), jnp.float32)
    pairwise = highs == 2
    n_steps = 2 if pairwise else 1
    snp_steps = pl.pallas_call(
        functools.partial(steps_kernel, 0.5 * math.sqrt(rank) / samples_here, own_blocks),
        out_shape=(by_snps,) * n_steps,
        in_specs=[smem, vmem],
        out_specs=(vmem,) * n_steps,
        compiler_params=params,
        name="snp_steps",
    )(pos, coverage)
    small = cost(0, 2 * 1024 * 1024)

    half_packet = jax.ShapeDtypeStruct((highs, rank, width), jnp.bfloat16)

    def pick(arrays, group, places):
        return pl.pallas_call(
            functools.partial(pick_kernel, len(turns), group, places, per_owner, own_blocks),
            out_shape=(half_packet,) * len(MATES),
            in_specs=[smem] + [vmem] * len(arrays),
            out_specs=(vmem,) * len(MATES),
            scratch_shapes=[pltpu.VMEM((highs, own_blocks, rank, 128), jnp.float32)],
            compiler_params=params,
            cost_estimate=small,
            name="pick_blocks",
        )(table, *arrays)

    def mates_sum(terms, after):
        *sums, for_core = pl.pallas_call(
            functools.partial(mates_sum_kernel, len(turns), per_owner, own_blocks),
            out_shape=(by_snps,) * highs + (jax.ShapeDtypeStruct((highs, rank, own_snps), jnp.bfloat16),),
            in_specs=[smem] + [vmem] * len(MATES) + [anywhere] * len(after),
            out_specs=(vmem,) * (highs + 1),
            scratch_shapes=[dense_blocks],
            compiler_params=params,
            cost_estimate=small,
            name="mates_sum",
        )(table, *terms, *after)
        return sums, for_core

    two_snps = jax.ShapeDtypeStruct((2, rank, own_snps), jnp.bfloat16)
    add_core = pl.pallas_call(
        add_kernel,
        out_shape=(by_snps, by_snps, two_snps),
        in_specs=[vmem] * 3,
        out_specs=(vmem,) * 3,
        compiler_params=params,
        name="add_core",
    )
    owners_update = pl.pallas_call(
        update_kernel,
        out_shape=(by_snps, two_snps),
        in_specs=[vmem] * 7,
        out_specs=(vmem,) * 2,
        compiler_params=params,
        name="owners_update",
    )

    def product(mate, group, panel, before):
        share = samples_here * snps_here // len(MATES) // 2
        return pl.pallas_call(
            functools.partial(product_kernel, [turns[t] for t in group], mate, not before, 256),
            out_shape=(by_samples, square),
            in_specs=[smem] + [vmem] * (2 + len(before)),
            out_specs=(vmem, vmem),
            compiler_params=params,
            cost_estimate=cost(8 * rank * share, 2 * share),
            name="panel_product",
        )(pos, geno, panel, *before)

    def sample_update(samples, gradient, gram, outs):
        return pl.pallas_call(
            functools.partial(sample_kernel, sample_step),
            out_shape=outs,
            in_specs=[vmem] * 3,
            out_specs=(vmem,) * len(outs),
            compiler_params=params,
            cost_estimate=small,
            name="sample_update",
        )(samples, gradient, gram)

    def terms_for(mate, samples_bf16, gram, groups, panels):
        share = samples_here * snps_here // len(MATES)
        return pl.pallas_call(
            functools.partial(term_kernel, turns, groups, mate),
            out_shape=packet,
            in_specs=[smem] + [vmem] * (3 + len(panels)),
            out_specs=vmem,
            compiler_params=params,
            cost_estimate=cost(8 * rank * share, 2 * share),
            name="mate_terms",
        )(pos, geno, samples_bf16, gram, *panels)

    def swap(x, turn):
        return lax.ppermute(x, "rows", [(r, r ^ turn) for r in range(devices)])

    def to_mate(x, mate):
        return swap(x, mate) if mate else x

    snps = snp_factors.T
    held = None
    for iteration in range(ROUNDS):
        last = iteration == ROUNDS - 1
        if held is None:
            held = {0: snps.astype(jnp.bfloat16)}
            for high in sorted(range(1, highs), key=lambda high: (high & (high - 1), -high)):
                bit = high & -high
                held[high] = swap(held[high ^ bit], bit * REST)
            groups = [list(range(highs)), list(range(highs, 2 * highs))]
            sources = {}
            for high in range(highs):
                source = held[high]
                if iteration == 0 and high:
                    source, _ = lax.optimization_barrier((source, samples))
                sources[2 * high], sources[2 * high + 1] = held[high], swap(source, 1)
            picked = [
                pick([sources[t] for t in group], group, [(i, None) for i in range(highs)]) for group in groups
            ]
        else:
            groups = [[2 * high + core for high in range(highs)] for core in (0, 1)]
            picked = [
                pick([x], group, [(0, high) for high in range(highs)])
                for x, group in zip((held, swap(held, 1)), groups)
            ]
        panels = [[to_mate(x, mate) for x, mate in zip(packets, MATES)] for packets in picked]
        partial = ()
        for g, m in ((0, 0), (1, 0), (0, 3), (0, 2), (0, 1), (1, 3), (1, 2), (1, 1)):
            partial = product(MATES[m], groups[g], panels[g][m], partial)
        rounded = (jax.ShapeDtypeStruct((rank, samples_here), jnp.bfloat16), square)
        if not last:
            samples, *current = sample_update(samples, *partial, (by_samples,) + rounded)
            after = []
        else:
            current = sample_update(samples, *partial, rounded)
            samples, token = sample_update(
                samples, *partial, (by_samples, jax.ShapeDtypeStruct((8, 128), jnp.float32))
            )
            after = [token]
        sums, for_core = mates_sum(
            [
                to_mate(terms_for(mate, *current, groups, [x[m] for x in panels]), mate)
                for m, mate in enumerate(MATES)
            ],
            after,
        )
        arrived = swap(for_core, 1)
        if pairwise and not last:
            own_sum, other_sum, swapped = add_core(*sums, arrived)
            snps, held = owners_update(
                own_sum, other_sum, swap(swapped, REST), *snp_steps, snps, held[1]
            )
            continue
        sums = [x + arrived[high].astype(jnp.float32) for high, x in enumerate(sums)]
        for high in range(highs - 1, 0, -1):
            bit = high & -high
            sums[high ^ bit] += swap(sums[high].astype(jnp.bfloat16), bit * REST).astype(jnp.float32)
        snps = (1.0 - weight_decay) * snps + snp_steps[0] * sums[0]
        held = None
    return (samples.T, snps.T)


def solution(mesh):
    placed = (
        P(("groups", "rows"), None),
        P(("groups", "rows"), None),
        P(("groups", "rows"), None),
        P("groups", None),
    )
    return jax.shard_map(
        on_device,
        mesh=mesh,
        in_specs=placed,
        out_specs=(P(("groups", "rows"), None), P(("groups", "rows"), None)),
        check_vma=False,
    )
```

```python
import functools
import math

import jax
import jax.numpy as jnp
from jax import lax
from jax.experimental import pallas as pl
from jax.experimental.pallas import tpu as pltpu
from jax.sharding import PartitionSpec as P

ROUNDS = 2

weight_decay = 0.02

MATES = (0, 2, 4, 6)
REST = 8
NT = (((1,), (1,)), ((), ()))
NN = (((1,), (0,)), ((), ()))
VMEM_LIMIT = 24 * 1024 * 1024


def dot(a, b, dims):
    return lax.dot_general(a, b, dims, preferred_element_type=jnp.float32)


def split3(x):
    hi = x.astype(jnp.bfloat16)
    rest = x - hi.astype(jnp.float32)
    mid = rest.astype(jnp.bfloat16)
    lo = (rest - mid.astype(jnp.float32)).astype(jnp.bfloat16)
    return hi, mid, lo


def low_half(rows):
    return lax.broadcasted_iota(jnp.int32, (rows, 128), 1) < 64


def double(x, low):
    turned = pltpu.roll(x, 64, 1)
    return jnp.where(low, x, turned), jnp.where(low, turned, x)


def load_kernel(turns, per_owner, own_blocks, pos_ref, cov, geno, samples, geno_out, samples_out, table, listed, sems):
    copies = [
        pltpu.make_async_copy(cov, listed, sems.at[0]),
        pltpu.make_async_copy(samples, samples_out, sems.at[1]),
        pltpu.make_async_copy(geno, geno_out, sems.at[2]),
    ]
    for copy in copies:
        copy.start()
    copies[0].wait()
    for m, mate in enumerate(MATES):
        batch = lax.bitwise_xor(pos_ref[0], mate)
        for t, turn in enumerate(turns):
            owner = lax.bitwise_xor(pos_ref[0], turn)
            for p in range(per_owner):
                table[m * len(turns) + t, p] = listed[batch, owner * per_owner + p] - owner * own_blocks
    for copy in copies[1:]:
        copy.wait()


def steps_kernel(scale, own_blocks, pos_ref, cov, *steps):
    low = low_half(steps[0].shape[0])
    for turn, out in enumerate(steps):
        owner = lax.bitwise_xor(pos_ref[0], turn * REST)

        def step_of(block):
            seen = (cov[...] == owner * own_blocks + block).astype(jnp.float32)
            return scale / jnp.sum(jnp.sum(seen, axis=1, keepdims=True), axis=0, keepdims=True)

        for j in range(own_blocks // 2):
            out[:, 128 * j:128 * (j + 1)] = jnp.where(low, step_of(2 * j), step_of(2 * j + 1))


def pick_kernel(turns, group, places, per_owner, own_blocks, table, *refs):
    packets, blocks = refs[-1 - len(MATES):-1], refs[-1]
    low = low_half(blocks.shape[2])
    for i, (ref, at) in enumerate(places):
        for j in range(own_blocks // 2):
            columns = slice(128 * j, 128 * (j + 1))
            x = (refs[ref][:, columns] if at is None else refs[ref][at, :, columns]).astype(jnp.float32)
            blocks[i, 2 * j], blocks[i, 2 * j + 1] = double(x, low)
    for m in range(len(MATES)):
        for i, t in enumerate(group):
            for q in range(per_owner // 2):
                first, second = table[m * turns + t, 2 * q], table[m * turns + t, 2 * q + 1]
                pair = jnp.where(low, blocks[i, first], blocks[i, second])
                packets[m][i, :, 128 * q:128 * (q + 1)] = pair.astype(jnp.bfloat16)


def mates_sum_kernel(turns, group, per_owner, own_blocks, table, *refs):
    terms, sums, total = refs[:len(MATES)], refs[-2], refs[-1]
    low = low_half(terms[0].shape[1])
    total[...] = jnp.zeros_like(total)
    for i, t in enumerate(group):
        for m in range(len(MATES)):
            for q in range(per_owner // 2):
                first, second = table[m * turns + t, 2 * q], table[m * turns + t, 2 * q + 1]
                pair = terms[m][t, :, 128 * q:128 * (q + 1)].astype(jnp.float32)
                total[i, first] += jnp.where(low, pair, 0.0)
                total[i, second] += jnp.where(low, 0.0, pair)
    for i in range(len(group)):
        for j in range(own_blocks // 2):
            first, second = total[i, 2 * j], total[i, 2 * j + 1]
            both = jnp.where(low, first, second) + pltpu.roll(jnp.where(low, second, first), 64, 1)
            sums[i, :, 128 * j:128 * (j + 1)] = both.astype(sums.dtype)


def add_kernel(sums, arrived, own_sum, other_sum, swapped):
    own_sum[...] = sums[0] + arrived[0].astype(jnp.float32)
    other_sum[...] = sums[1] + arrived[1].astype(jnp.float32)
    swapped[0] = other_sum[...].astype(jnp.bfloat16)
    swapped[1] = own_sum[...].astype(jnp.bfloat16)


def update_kernel(own_sum, other_sum, arrived, own_step, other_step, snps, other_snps, new_snps, held):
    kept = 1.0 - weight_decay
    own_total = own_sum[...] + arrived[0].astype(jnp.float32)
    other_total = other_sum[...] + arrived[1].astype(jnp.float32)
    new_snps[...] = kept * snps[...] + own_step[...] * own_total
    held[0] = new_snps[...].astype(jnp.bfloat16)
    other = kept * other_snps[...].astype(jnp.float32) + other_step[...] * other_total
    held[1] = other.astype(jnp.bfloat16)


def turns_of(devices):
    return [high + core for high in range(0, devices, REST) for core in (0, 1)]


def columns_of(pos, turn, mate, width):
    owner = lax.bitwise_xor(pos, turn ^ mate)
    return pl.ds(pl.multiple_of(owner * width, width), width)


def product_kernel(turns, mate, first, rows, pos_ref, geno, packet, *refs):
    before, (gradient, gram) = refs[:-2], refs[-2:]
    pos = pos_ref[0]
    width = packet.shape[2]
    total = None if first else before[1][...]
    for t in range(len(turns)):
        term = dot(packet[t], packet[t], NT)
        total = term if total is None else total + term
    gram[...] = total
    for r in range(geno.shape[0] // rows):
        here = slice(r * rows, (r + 1) * rows)
        total = None if first else before[0][:, here]
        for t, turn in enumerate(turns):
            term = dot(packet[t], geno[here, columns_of(pos, turn, mate, width)], NT)
            total = term if total is None else total + term
        gradient[:, here] = total


def sample_kernel(sample_step, samples, gradient, gram, *outs):
    old = samples[...]
    old_bf16 = old.astype(jnp.bfloat16)
    total = gradient[...]
    for part in split3(gram[...]):
        total -= dot(part, old_bf16, NN)
    new = (1.0 - weight_decay) * old + sample_step * total
    *full, last = outs
    rounded = new.astype(jnp.bfloat16)
    for out in full:
        out[...] = new if out.dtype == jnp.float32 else rounded
    if last.shape[0] == last.shape[1]:
        last[...] = dot(rounded, rounded, NT)
    else:
        last[...] = jnp.zeros_like(last)


def term_kernel(turns, groups, mate, pos_ref, geno, samples, gram, *refs):
    packets, terms = refs[:-1], refs[-1]
    pos = pos_ref[0]
    width = terms.shape[2]
    parts = split3(gram[...])
    for packet, group in zip(packets, groups):
        for i, t in enumerate(group):
            term = dot(samples[...], geno[:, columns_of(pos, turns[t], mate, width)], NN)
            for part in parts:
                term -= dot(part, packet[i], NN)
            terms[t] = term.astype(jnp.bfloat16)


def on_device(genotypes, sample_factors, snp_factors, coverage):
    devices = lax.axis_size("rows")
    turns = turns_of(devices)
    highs = len(turns) // 2
    position = lax.axis_index("rows").astype(jnp.int32)
    samples_here, snps_here = genotypes.shape
    rank = sample_factors.shape[1]
    covered = coverage.shape[1]
    tile_size = snps_here // covered
    per_owner = covered // devices
    own_snps = snp_factors.shape[0]
    own_blocks = own_snps // tile_size
    width = per_owner * tile_size
    assert tile_size == 64 and per_owner % 2 == 0 and own_blocks % 2 == 0
    assert devices % REST == 0 and devices & (devices - 1) == 0

    sample_step = 0.5 * math.sqrt(rank) / (covered * tile_size)

    smem = pl.BlockSpec(memory_space=pltpu.SMEM)
    vmem = pl.BlockSpec(memory_space=pltpu.VMEM)
    hbm = pl.BlockSpec(memory_space=pltpu.HBM)
    anywhere = pl.BlockSpec(memory_space=pl.ANY)
    params = pltpu.CompilerParams(vmem_limit_bytes=VMEM_LIMIT)
    pos = position.reshape(1)
    packet = jax.ShapeDtypeStruct((len(turns), rank, width), jnp.bfloat16)
    dense_blocks = pltpu.VMEM((len(turns), own_blocks, rank, 128), jnp.float32)
    by_samples = jax.ShapeDtypeStruct((rank, samples_here), jnp.float32)
    square = jax.ShapeDtypeStruct((rank, rank), jnp.float32)

    def cost(flops, bytes_accessed):
        return pl.CostEstimate(flops=flops, bytes_accessed=bytes_accessed, transcendentals=0)

    geno, samples, table = pl.pallas_call(
        functools.partial(load_kernel, turns, per_owner, own_blocks),
        out_shape=(
            pltpu.VMEM((samples_here, snps_here), jnp.bfloat16),
            pltpu.VMEM((rank, samples_here), jnp.float32),
            pltpu.SMEM((len(MATES) * len(turns), per_owner), jnp.int32),
        ),
        in_specs=[smem, hbm, hbm, hbm],
        out_specs=(vmem, vmem, smem),
        scratch_shapes=[pltpu.SMEM(coverage.shape, jnp.int32), pltpu.SemaphoreType.DMA((3,))],
        compiler_params=pltpu.CompilerParams(
            vmem_limit_bytes=58 * 1024 * 1024 - 2 * samples_here * snps_here
        ),
        cost_estimate=cost(0, 2 * samples_here * snps_here),
        name="load_batch",
    )(pos, coverage, genotypes, sample_factors.T)

    by_snps = jax.ShapeDtypeStruct((rank, own_snps), jnp.float32)
    pairwise = highs == 2
    n_steps = 2 if pairwise else 1
    snp_steps = pl.pallas_call(
        functools.partial(steps_kernel, 0.5 * math.sqrt(rank) / samples_here, own_blocks),
        out_shape=(by_snps,) * n_steps,
        in_specs=[smem, vmem],
        out_specs=(vmem,) * n_steps,
        compiler_params=params,
        name="snp_steps",
    )(pos, coverage)
    small = cost(0, 2 * 1024 * 1024)

    half_packet = jax.ShapeDtypeStruct((highs, rank, width), jnp.bfloat16)

    def pick(arrays, group, places):
        return pl.pallas_call(
            functools.partial(pick_kernel, len(turns), group, places, per_owner, own_blocks),
            out_shape=(half_packet,) * len(MATES),
            in_specs=[smem] + [vmem] * len(arrays),
            out_specs=(vmem,) * len(MATES),
            scratch_shapes=[pltpu.VMEM((highs, own_blocks, rank, 128), jnp.float32)],
            compiler_params=params,
            cost_estimate=small,
            name="pick_blocks",
        )(table, *arrays)

    def mates_sum(terms, group, dtype, after):
        return pl.pallas_call(
            functools.partial(mates_sum_kernel, len(turns), group, per_owner, own_blocks),
            out_shape=jax.ShapeDtypeStruct((len(group), rank, own_snps), dtype),
            in_specs=[smem] + [vmem] * len(MATES) + [anywhere] * len(after),
            out_specs=vmem,
            scratch_shapes=[pltpu.VMEM((len(group), own_blocks, rank, 128), jnp.float32)],
            compiler_params=params,
            cost_estimate=small,
            name="mates_sum",
        )(table, *terms, *after)

    two_snps = jax.ShapeDtypeStruct((2, rank, own_snps), jnp.bfloat16)
    add_core = pl.pallas_call(
        add_kernel,
        out_shape=(by_snps, by_snps, two_snps),
        in_specs=[vmem] * 2,
        out_specs=(vmem,) * 3,
        compiler_params=params,
        name="add_core",
    )
    owners_update = pl.pallas_call(
        update_kernel,
        out_shape=(by_snps, two_snps),
        in_specs=[vmem] * 7,
        out_specs=(vmem,) * 2,
        compiler_params=params,
        name="owners_update",
    )

    def product(mate, group, panel, before):
        share = samples_here * snps_here // len(MATES) // 2
        return pl.pallas_call(
            functools.partial(product_kernel, [turns[t] for t in group], mate, not before, 256),
            out_shape=(by_samples, square),
            in_specs=[smem] + [vmem] * (2 + len(before)),
            out_specs=(vmem, vmem),
            compiler_params=params,
            cost_estimate=cost(8 * rank * share, 2 * share),
            name="panel_product",
        )(pos, geno, panel, *before)

    def sample_update(samples, gradient, gram, outs):
        return pl.pallas_call(
            functools.partial(sample_kernel, sample_step),
            out_shape=outs,
            in_specs=[vmem] * 3,
            out_specs=(vmem,) * len(outs),
            compiler_params=params,
            cost_estimate=small,
            name="sample_update",
        )(samples, gradient, gram)

    def terms_for(mate, samples_bf16, gram, groups, panels):
        share = samples_here * snps_here // len(MATES)
        return pl.pallas_call(
            functools.partial(term_kernel, turns, groups, mate),
            out_shape=packet,
            in_specs=[smem] + [vmem] * (3 + len(panels)),
            out_specs=vmem,
            compiler_params=params,
            cost_estimate=cost(8 * rank * share, 2 * share),
            name="mate_terms",
        )(pos, geno, samples_bf16, gram, *panels)

    def swap(x, turn):
        return lax.ppermute(x, "rows", [(r, r ^ turn) for r in range(devices)])

    def to_mate(x, mate):
        return swap(x, mate) if mate else x

    snps = snp_factors.T
    held = None
    for iteration in range(ROUNDS):
        last = iteration == ROUNDS - 1
        if held is None:
            held = {0: snps.astype(jnp.bfloat16)}
            for high in sorted(range(1, highs), key=lambda high: (high & (high - 1), -high)):
                bit = high & -high
                held[high] = swap(held[high ^ bit], bit * REST)
            groups = [list(range(highs)), list(range(highs, 2 * highs))]
            sources = {}
            for high in range(highs):
                source = held[high]
                if iteration == 0 and high:
                    source, _ = lax.optimization_barrier((source, samples))
                sources[2 * high], sources[2 * high + 1] = held[high], swap(source, 1)
            picked = [
                pick([sources[t] for t in group], group, [(i, None) for i in range(highs)]) for group in groups
            ]
        else:
            groups = [[2 * high + core for high in range(highs)] for core in (0, 1)]
            picked = [
                pick([x], group, [(0, high) for high in range(highs)])
                for x, group in zip((held, swap(held, 1)), groups)
            ]
        panels = [[to_mate(x, mate) for x, mate in zip(packets, MATES)] for packets in picked]
        partial = ()
        for g, m in ((0, 0), (1, 0), (0, 3), (0, 2), (0, 1), (1, 3), (1, 2), (1, 1)):
            partial = product(MATES[m], groups[g], panels[g][m], partial)
        rounded = (jax.ShapeDtypeStruct((rank, samples_here), jnp.bfloat16), square)
        if not last:
            samples, *current = sample_update(samples, *partial, (by_samples,) + rounded)
            after = []
        else:
            current = sample_update(samples, *partial, rounded)
            samples, token = sample_update(
                samples, *partial, (by_samples, jax.ShapeDtypeStruct((8, 128), jnp.float32))
            )
            after = [token]
        sent = [
            to_mate(terms_for(mate, *current, groups, [x[m] for x in panels]), mate)
            for m, mate in enumerate(MATES)
        ]
        for_core = mates_sum(sent, list(range(1, len(turns), 2)), jnp.bfloat16, after)
        arrived = swap(for_core, 1)
        sums = mates_sum(sent, list(range(0, len(turns), 2)), jnp.float32, [for_core])
        if pairwise and not last:
            own_sum, other_sum, swapped = add_core(sums, arrived)
            snps, held = owners_update(
                own_sum, other_sum, swap(swapped, REST), *snp_steps, snps, held[1]
            )
            continue
        sums = [sums[high] + arrived[high].astype(jnp.float32) for high in range(highs)]
        for high in range(highs - 1, 0, -1):
            bit = high & -high
            sums[high ^ bit] += swap(sums[high].astype(jnp.bfloat16), bit * REST).astype(jnp.float32)
        snps = (1.0 - weight_decay) * snps + snp_steps[0] * sums[0]
        held = None
    return (samples.T, snps.T)


def solution(mesh):
    placed = (
        P(("groups", "rows"), None),
        P(("groups", "rows"), None),
        P(("groups", "rows"), None),
        P("groups", None),
    )
    return jax.shard_map(
        on_device,
        mesh=mesh,
        in_specs=placed,
        out_specs=(P(("groups", "rows"), None), P(("groups", "rows"), None)),
        check_vma=False,
    )
```

```python
import functools
import math

import jax
import jax.numpy as jnp
from jax import lax
from jax.experimental import pallas as pl
from jax.experimental.pallas import tpu as pltpu
from jax.sharding import PartitionSpec as P

ROUNDS = 2

weight_decay = 0.02

MATES = (0, 2, 4, 6)
REST = 8
NT = (((1,), (1,)), ((), ()))
NN = (((1,), (0,)), ((), ()))
VMEM_LIMIT = 24 * 1024 * 1024


def dot(a, b, dims):
    return lax.dot_general(a, b, dims, preferred_element_type=jnp.float32)


def split3(x):
    hi = x.astype(jnp.bfloat16)
    rest = x - hi.astype(jnp.float32)
    mid = rest.astype(jnp.bfloat16)
    lo = (rest - mid.astype(jnp.float32)).astype(jnp.bfloat16)
    return hi, mid, lo


def low_half(rows):
    return lax.broadcasted_iota(jnp.int32, (rows, 128), 1) < 64


def double(x, low):
    turned = pltpu.roll(x, 64, 1)
    return jnp.where(low, x, turned), jnp.where(low, turned, x)


def load_kernel(turns, per_owner, own_blocks, pos_ref, cov, geno, samples, geno_out, samples_out, table, listed, sems):
    copies = [
        pltpu.make_async_copy(cov, listed, sems.at[0]),
        pltpu.make_async_copy(samples, samples_out, sems.at[1]),
        pltpu.make_async_copy(geno, geno_out, sems.at[2]),
    ]
    for copy in copies:
        copy.start()
    copies[0].wait()
    for m, mate in enumerate(MATES):
        batch = lax.bitwise_xor(pos_ref[0], mate)
        for t, turn in enumerate(turns):
            owner = lax.bitwise_xor(pos_ref[0], turn)
            for p in range(per_owner):
                table[m * len(turns) + t, p] = listed[batch, owner * per_owner + p] - owner * own_blocks
    for copy in copies[1:]:
        copy.wait()


def steps_kernel(scale, own_blocks, pos_ref, cov, *steps):
    low = low_half(steps[0].shape[0])
    for turn, out in enumerate(steps):
        owner = lax.bitwise_xor(pos_ref[0], turn * REST)

        def step_of(block):
            seen = (cov[...] == owner * own_blocks + block).astype(jnp.float32)
            return scale / jnp.sum(jnp.sum(seen, axis=1, keepdims=True), axis=0, keepdims=True)

        for j in range(own_blocks // 2):
            out[:, 128 * j:128 * (j + 1)] = jnp.where(low, step_of(2 * j), step_of(2 * j + 1))


def pick_kernel(turns, group, places, per_owner, own_blocks, table, *refs):
    packets, blocks = refs[-1 - len(MATES):-1], refs[-1]
    low = low_half(blocks.shape[2])
    for i, (ref, at) in enumerate(places):
        for j in range(own_blocks // 2):
            columns = slice(128 * j, 128 * (j + 1))
            x = (refs[ref][:, columns] if at is None else refs[ref][at, :, columns]).astype(jnp.float32)
            blocks[i, 2 * j], blocks[i, 2 * j + 1] = double(x, low)
    for m in range(len(MATES)):
        for i, t in enumerate(group):
            for q in range(per_owner // 2):
                first, second = table[m * turns + t, 2 * q], table[m * turns + t, 2 * q + 1]
                pair = jnp.where(low, blocks[i, first], blocks[i, second])
                packets[m][i, :, 128 * q:128 * (q + 1)] = pair.astype(jnp.bfloat16)


def mates_sum_kernel(turns, group, per_owner, own_blocks, table, *refs):
    terms, sums, total = refs[:len(MATES)], refs[-2], refs[-1]
    low = low_half(terms[0].shape[1])
    total[...] = jnp.zeros_like(total)
    for i, t in enumerate(group):
        for m in range(len(MATES)):
            for q in range(per_owner // 2):
                first, second = table[m * turns + t, 2 * q], table[m * turns + t, 2 * q + 1]
                pair = terms[m][t, :, 128 * q:128 * (q + 1)].astype(jnp.float32)
                total[i, first] += jnp.where(low, pair, 0.0)
                total[i, second] += jnp.where(low, 0.0, pair)
    for i in range(len(group)):
        for j in range(own_blocks // 2):
            first, second = total[i, 2 * j], total[i, 2 * j + 1]
            both = jnp.where(low, first, second) + pltpu.roll(jnp.where(low, second, first), 64, 1)
            sums[i, :, 128 * j:128 * (j + 1)] = both.astype(sums.dtype)


def add_kernel(sums, arrived, own_sum, other_sum, swapped):
    own_sum[...] = sums[0] + arrived[0].astype(jnp.float32)
    other_sum[...] = sums[1] + arrived[1].astype(jnp.float32)
    swapped[0] = other_sum[...].astype(jnp.bfloat16)
    swapped[1] = own_sum[...].astype(jnp.bfloat16)


def update_kernel(own_sum, other_sum, arrived, own_step, other_step, snps, other_snps, new_snps, held):
    kept = 1.0 - weight_decay
    own_total = own_sum[...] + arrived[0].astype(jnp.float32)
    other_total = other_sum[...] + arrived[1].astype(jnp.float32)
    new_snps[...] = kept * snps[...] + own_step[...] * own_total
    held[0] = new_snps[...].astype(jnp.bfloat16)
    other = kept * other_snps[...].astype(jnp.float32) + other_step[...] * other_total
    held[1] = other.astype(jnp.bfloat16)


def turns_of(devices):
    return [high + core for high in range(0, devices, REST) for core in (0, 1)]


def columns_of(pos, turn, mate, width):
    owner = lax.bitwise_xor(pos, turn ^ mate)
    return pl.ds(pl.multiple_of(owner * width, width), width)


def product_kernel(turns, mate, first, rows, pos_ref, geno, packet, *refs):
    before, (gradient, gram) = refs[:2], refs[-2:]
    pos = pos_ref[0]
    width = packet.shape[2]
    total = None if first else before[1][...]
    for t in range(len(turns)):
        term = dot(packet[t], packet[t], NT)
        total = term if total is None else total + term
    gram[...] = total
    for r in range(geno.shape[0] // rows):
        here = slice(r * rows, (r + 1) * rows)
        total = None if first else before[0][:, here]
        for t, turn in enumerate(turns):
            term = dot(packet[t], geno[here, columns_of(pos, turn, mate, width)], NT)
            total = term if total is None else total + term
        gradient[:, here] = total


def sample_kernel(sample_step, samples, gradient, gram, *outs):
    old = samples[...]
    old_bf16 = old.astype(jnp.bfloat16)
    total = gradient[...]
    for part in split3(gram[...]):
        total -= dot(part, old_bf16, NN)
    new = (1.0 - weight_decay) * old + sample_step * total
    *full, last = outs
    rounded = new.astype(jnp.bfloat16)
    for out in full:
        out[...] = new if out.dtype == jnp.float32 else rounded
    if last.shape[0] == last.shape[1]:
        last[...] = dot(rounded, rounded, NT)
    else:
        last[...] = jnp.zeros_like(last)


def term_kernel(turns, groups, mate, pos_ref, geno, samples, gram, *refs):
    packets, terms = refs[:-1], refs[-1]
    pos = pos_ref[0]
    width = terms.shape[2]
    parts = split3(gram[...])
    for packet, group in zip(packets, groups):
        for i, t in enumerate(group):
            term = dot(samples[...], geno[:, columns_of(pos, turns[t], mate, width)], NN)
            for part in parts:
                term -= dot(part, packet[i], NN)
            terms[t] = term.astype(jnp.bfloat16)


def on_device(genotypes, sample_factors, snp_factors, coverage):
    devices = lax.axis_size("rows")
    turns = turns_of(devices)
    highs = len(turns) // 2
    position = lax.axis_index("rows").astype(jnp.int32)
    samples_here, snps_here = genotypes.shape
    rank = sample_factors.shape[1]
    covered = coverage.shape[1]
    tile_size = snps_here // covered
    per_owner = covered // devices
    own_snps = snp_factors.shape[0]
    own_blocks = own_snps // tile_size
    width = per_owner * tile_size
    assert tile_size == 64 and per_owner % 2 == 0 and own_blocks % 2 == 0
    assert devices % REST == 0 and devices & (devices - 1) == 0

    sample_step = 0.5 * math.sqrt(rank) / (covered * tile_size)

    smem = pl.BlockSpec(memory_space=pltpu.SMEM)
    vmem = pl.BlockSpec(memory_space=pltpu.VMEM)
    hbm = pl.BlockSpec(memory_space=pltpu.HBM)
    anywhere = pl.BlockSpec(memory_space=pl.ANY)
    params = pltpu.CompilerParams(vmem_limit_bytes=VMEM_LIMIT)
    pos = position.reshape(1)
    packet = jax.ShapeDtypeStruct((len(turns), rank, width), jnp.bfloat16)
    dense_blocks = pltpu.VMEM((len(turns), own_blocks, rank, 128), jnp.float32)
    by_samples = jax.ShapeDtypeStruct((rank, samples_here), jnp.float32)
    square = jax.ShapeDtypeStruct((rank, rank), jnp.float32)

    def cost(flops, bytes_accessed):
        return pl.CostEstimate(flops=flops, bytes_accessed=bytes_accessed, transcendentals=0)

    geno, samples, table = pl.pallas_call(
        functools.partial(load_kernel, turns, per_owner, own_blocks),
        out_shape=(
            pltpu.VMEM((samples_here, snps_here), jnp.bfloat16),
            pltpu.VMEM((rank, samples_here), jnp.float32),
            pltpu.SMEM((len(MATES) * len(turns), per_owner), jnp.int32),
        ),
        in_specs=[smem, hbm, hbm, hbm],
        out_specs=(vmem, vmem, smem),
        scratch_shapes=[pltpu.SMEM(coverage.shape, jnp.int32), pltpu.SemaphoreType.DMA((3,))],
        compiler_params=pltpu.CompilerParams(
            vmem_limit_bytes=58 * 1024 * 1024 - 2 * samples_here * snps_here
        ),
        cost_estimate=cost(0, 2 * samples_here * snps_here),
        name="load_batch",
    )(pos, coverage, genotypes, sample_factors.T)

    by_snps = jax.ShapeDtypeStruct((rank, own_snps), jnp.float32)
    pairwise = highs == 2
    n_steps = 2 if pairwise else 1
    snp_steps = pl.pallas_call(
        functools.partial(steps_kernel, 0.5 * math.sqrt(rank) / samples_here, own_blocks),
        out_shape=(by_snps,) * n_steps,
        in_specs=[smem, vmem],
        out_specs=(vmem,) * n_steps,
        compiler_params=params,
        name="snp_steps",
    )(pos, coverage)
    small = cost(0, 2 * 1024 * 1024)

    half_packet = jax.ShapeDtypeStruct((highs, rank, width), jnp.bfloat16)

    def pick(arrays, group, places):
        return pl.pallas_call(
            functools.partial(pick_kernel, len(turns), group, places, per_owner, own_blocks),
            out_shape=(half_packet,) * len(MATES),
            in_specs=[smem] + [vmem] * len(arrays),
            out_specs=(vmem,) * len(MATES),
            scratch_shapes=[pltpu.VMEM((highs, own_blocks, rank, 128), jnp.float32)],
            compiler_params=params,
            cost_estimate=small,
            name="pick_blocks",
        )(table, *arrays)

    def mates_sum(terms, group, dtype, after):
        return pl.pallas_call(
            functools.partial(mates_sum_kernel, len(turns), group, per_owner, own_blocks),
            out_shape=jax.ShapeDtypeStruct((len(group), rank, own_snps), dtype),
            in_specs=[smem] + [vmem] * len(MATES) + [anywhere] * len(after),
            out_specs=vmem,
            scratch_shapes=[pltpu.VMEM((len(group), own_blocks, rank, 128), jnp.float32)],
            compiler_params=params,
            cost_estimate=small,
            name="mates_sum",
        )(table, *terms, *after)

    two_snps = jax.ShapeDtypeStruct((2, rank, own_snps), jnp.bfloat16)
    add_core = pl.pallas_call(
        add_kernel,
        out_shape=(by_snps, by_snps, two_snps),
        in_specs=[vmem] * 2,
        out_specs=(vmem,) * 3,
        compiler_params=params,
        name="add_core",
    )
    owners_update = pl.pallas_call(
        update_kernel,
        out_shape=(by_snps, two_snps),
        in_specs=[vmem] * 7,
        out_specs=(vmem,) * 2,
        compiler_params=params,
        name="owners_update",
    )

    def product(mate, group, panel, before, after):
        share = samples_here * snps_here // len(MATES) // 2
        return pl.pallas_call(
            functools.partial(product_kernel, [turns[t] for t in group], mate, not before, 256),
            out_shape=(by_samples, square),
            in_specs=[smem] + [vmem] * (2 + len(before)) + [anywhere] * len(after),
            out_specs=(vmem, vmem),
            compiler_params=params,
            cost_estimate=cost(8 * rank * share, 2 * share),
            name="panel_product",
        )(pos, geno, panel, *before, *after)

    def sample_update(samples, gradient, gram, outs):
        return pl.pallas_call(
            functools.partial(sample_kernel, sample_step),
            out_shape=outs,
            in_specs=[vmem] * 3,
            out_specs=(vmem,) * len(outs),
            compiler_params=params,
            cost_estimate=small,
            name="sample_update",
        )(samples, gradient, gram)

    def terms_for(mate, samples_bf16, gram, groups, panels):
        share = samples_here * snps_here // len(MATES)
        return pl.pallas_call(
            functools.partial(term_kernel, turns, groups, mate),
            out_shape=packet,
            in_specs=[smem] + [vmem] * (3 + len(panels)),
            out_specs=vmem,
            compiler_params=params,
            cost_estimate=cost(8 * rank * share, 2 * share),
            name="mate_terms",
        )(pos, geno, samples_bf16, gram, *panels)

    def swap(x, turn):
        return lax.ppermute(x, "rows", [(r, r ^ turn) for r in range(devices)])

    def to_mate(x, mate):
        return swap(x, mate) if mate else x

    snps = snp_factors.T
    held = None
    for iteration in range(ROUNDS):
        last = iteration == ROUNDS - 1
        if held is None:
            held = {0: snps.astype(jnp.bfloat16)}
            for high in sorted(range(1, highs), key=lambda high: (high & (high - 1), -high)):
                bit = high & -high
                held[high] = swap(held[high ^ bit], bit * REST)
            groups = [list(range(highs)), list(range(highs, 2 * highs))]
            sources = {}
            for high in range(highs):
                source = held[high]
                if iteration == 0 and high:
                    source, _ = lax.optimization_barrier((source, samples))
                sources[2 * high], sources[2 * high + 1] = held[high], swap(source, 1)
            picked = [
                pick([sources[t] for t in group], group, [(i, None) for i in range(highs)]) for group in groups
            ]
        else:
            groups = [[2 * high + core for high in range(highs)] for core in (0, 1)]
            picked = [
                pick([x], group, [(0, high) for high in range(highs)])
                for x, group in zip((held, swap(held, 1)), groups)
            ]
        panels = [[to_mate(x, mate) for x, mate in zip(packets, MATES)] for packets in picked]
        partial = ()
        for g, m in ((0, 0), (0, 3), (0, 2), (0, 1), (1, 0), (1, 3), (1, 2), (1, 1)):
            after = [panels[1][0]] if (g, m) == (0, 3) else []
            partial = product(MATES[m], groups[g], panels[g][m], partial, after)
        rounded = (jax.ShapeDtypeStruct((rank, samples_here), jnp.bfloat16), square)
        if not last:
            samples, *current = sample_update(samples, *partial, (by_samples,) + rounded)
            after = []
        else:
            current = sample_update(samples, *partial, rounded)
            samples, token = sample_update(
                samples, *partial, (by_samples, jax.ShapeDtypeStruct((8, 128), jnp.float32))
            )
            after = [token]
        sent = [
            to_mate(terms_for(mate, *current, groups, [x[m] for x in panels]), mate)
            for m, mate in enumerate(MATES)
        ]
        for_core = mates_sum(sent, list(range(1, len(turns), 2)), jnp.bfloat16, after)
        arrived = swap(for_core, 1)
        sums = mates_sum(sent, list(range(0, len(turns), 2)), jnp.float32, [for_core])
        if pairwise and not last:
            own_sum, other_sum, swapped = add_core(sums, arrived)
            snps, held = owners_update(
                own_sum, other_sum, swap(swapped, REST), *snp_steps, snps, held[1]
            )
            continue
        sums = [sums[high] + arrived[high].astype(jnp.float32) for high in range(highs)]
        for high in range(highs - 1, 0, -1):
            bit = high & -high
            sums[high ^ bit] += swap(sums[high].astype(jnp.bfloat16), bit * REST).astype(jnp.float32)
        snps = (1.0 - weight_decay) * snps + snp_steps[0] * sums[0]
        held = None
    return (samples.T, snps.T)


def solution(mesh):
    placed = (
        P(("groups", "rows"), None),
        P(("groups", "rows"), None),
        P(("groups", "rows"), None),
        P("groups", None),
    )
    return jax.shard_map(
        on_device,
        mesh=mesh,
        in_specs=placed,
        out_specs=(P(("groups", "rows"), None), P(("groups", "rows"), None)),
        check_vma=False,
    )
```

```python
import functools
import math

import jax
import jax.numpy as jnp
from jax import lax
from jax.experimental import pallas as pl
from jax.experimental.pallas import tpu as pltpu
from jax.sharding import PartitionSpec as P

ROUNDS = 2

weight_decay = 0.02

MATES = (0, 2, 4, 6)
REST = 8
NT = (((1,), (1,)), ((), ()))
NN = (((1,), (0,)), ((), ()))
VMEM_LIMIT = 24 * 1024 * 1024


def dot(a, b, dims):
    return lax.dot_general(a, b, dims, preferred_element_type=jnp.float32)


def stacked3(x):
    hi = x.astype(jnp.bfloat16)
    rest = x - hi.astype(jnp.float32)
    mid = rest.astype(jnp.bfloat16)
    lo = (rest - mid.astype(jnp.float32)).astype(jnp.bfloat16)
    return jnp.concatenate([hi, mid, lo], axis=0)


def dot3(parts, b):
    products = dot(parts, b, NN)
    rows = parts.shape[0] // 3
    return products[:rows] + (products[rows:2 * rows] + products[2 * rows:])


def low_half(rows):
    return lax.broadcasted_iota(jnp.int32, (rows, 128), 1) < 64


def double(x, low):
    turned = pltpu.roll(x, 64, 1)
    return jnp.where(low, x, turned), jnp.where(low, turned, x)


def load_kernel(turns, per_owner, own_blocks, pos_ref, cov, geno, samples, geno_out, samples_out, table, listed, sems):
    copies = [
        pltpu.make_async_copy(cov, listed, sems.at[0]),
        pltpu.make_async_copy(samples, samples_out, sems.at[1]),
        pltpu.make_async_copy(geno, geno_out, sems.at[2]),
    ]
    for copy in copies:
        copy.start()
    copies[0].wait()
    for m, mate in enumerate(MATES):
        batch = lax.bitwise_xor(pos_ref[0], mate)
        for t, turn in enumerate(turns):
            owner = lax.bitwise_xor(pos_ref[0], turn)
            for p in range(per_owner):
                table[m * len(turns) + t, p] = listed[batch, owner * per_owner + p] - owner * own_blocks
    for copy in copies[1:]:
        copy.wait()


def steps_kernel(scale, own_blocks, pos_ref, cov, *steps):
    low = low_half(steps[0].shape[0])
    for turn, out in enumerate(steps):
        owner = lax.bitwise_xor(pos_ref[0], turn * REST)

        def step_of(block):
            seen = (cov[...] == owner * own_blocks + block).astype(jnp.float32)
            return scale / jnp.sum(jnp.sum(seen, axis=1, keepdims=True), axis=0, keepdims=True)

        for j in range(own_blocks // 2):
            out[:, 128 * j:128 * (j + 1)] = jnp.where(low, step_of(2 * j), step_of(2 * j + 1))


def pick_kernel(turns, group, places, per_owner, own_blocks, table, *refs):
    packets, blocks = refs[-1 - len(MATES):-1], refs[-1]
    low = low_half(blocks.shape[2])
    for i, (ref, at) in enumerate(places):
        for j in range(own_blocks // 2):
            columns = slice(128 * j, 128 * (j + 1))
            x = (refs[ref][:, columns] if at is None else refs[ref][at, :, columns]).astype(jnp.float32)
            blocks[i, 2 * j], blocks[i, 2 * j + 1] = double(x, low)
    for m in range(len(MATES)):
        for i, t in enumerate(group):
            for q in range(per_owner // 2):
                first, second = table[m * turns + t, 2 * q], table[m * turns + t, 2 * q + 1]
                pair = jnp.where(low, blocks[i, first], blocks[i, second])
                packets[m][i, :, 128 * q:128 * (q + 1)] = pair.astype(jnp.bfloat16)


def mates_sum_kernel(turns, group, per_owner, own_blocks, table, *refs):
    terms, sums, total = refs[:len(MATES)], refs[-2], refs[-1]
    low = low_half(terms[0].shape[1])
    total[...] = jnp.zeros_like(total)
    for i, t in enumerate(group):
        for m in range(len(MATES)):
            for q in range(per_owner // 2):
                first, second = table[m * turns + t, 2 * q], table[m * turns + t, 2 * q + 1]
                pair = terms[m][t, :, 128 * q:128 * (q + 1)].astype(jnp.float32)
                total[i, first] += jnp.where(low, pair, 0.0)
                total[i, second] += jnp.where(low, 0.0, pair)
    for i in range(len(group)):
        for j in range(own_blocks // 2):
            first, second = total[i, 2 * j], total[i, 2 * j + 1]
            both = jnp.where(low, first, second) + pltpu.roll(jnp.where(low, second, first), 64, 1)
            sums[i, :, 128 * j:128 * (j + 1)] = both.astype(sums.dtype)


def add_kernel(sums, arrived, own_sum, other_sum, swapped):
    own_sum[...] = sums[0] + arrived[0].astype(jnp.float32)
    other_sum[...] = sums[1] + arrived[1].astype(jnp.float32)
    swapped[0] = other_sum[...].astype(jnp.bfloat16)
    swapped[1] = own_sum[...].astype(jnp.bfloat16)


def update_kernel(own_sum, other_sum, arrived, own_step, other_step, snps, other_snps, new_snps, held):
    kept = 1.0 - weight_decay
    own_total = own_sum[...] + arrived[0].astype(jnp.float32)
    other_total = other_sum[...] + arrived[1].astype(jnp.float32)
    new_snps[...] = kept * snps[...] + own_step[...] * own_total
    held[0] = new_snps[...].astype(jnp.bfloat16)
    other = kept * other_snps[...].astype(jnp.float32) + other_step[...] * other_total
    held[1] = other.astype(jnp.bfloat16)


def turns_of(devices):
    return [high + core for high in range(0, devices, REST) for core in (0, 1)]


def columns_of(pos, turn, mate, width):
    owner = lax.bitwise_xor(pos, turn ^ mate)
    return pl.ds(pl.multiple_of(owner * width, width), width)


def product_kernel(turns, mate, first, rows, pos_ref, geno, packet, *refs):
    before, (gradient, gram) = refs[:2], refs[-2:]
    pos = pos_ref[0]
    width = packet.shape[2]
    total = None if first else before[1][...]
    for t in range(len(turns)):
        term = dot(packet[t], packet[t], NT)
        total = term if total is None else total + term
    gram[...] = total
    for r in range(geno.shape[0] // rows):
        here = slice(r * rows, (r + 1) * rows)
        total = None if first else before[0][:, here]
        for t, turn in enumerate(turns):
            term = dot(packet[t], geno[here, columns_of(pos, turn, mate, width)], NT)
            total = term if total is None else total + term
        gradient[:, here] = total


def sample_kernel(sample_step, samples, gradient, gram, *outs):
    old = samples[...]
    old_bf16 = old.astype(jnp.bfloat16)
    total = gradient[...]
    total -= dot3(stacked3(gram[...]), old_bf16)
    new = (1.0 - weight_decay) * old + sample_step * total
    *full, last = outs
    rounded = new.astype(jnp.bfloat16)
    for out in full:
        out[...] = new if out.dtype == jnp.float32 else rounded
    if last.shape[0] == last.shape[1]:
        last[...] = dot(rounded, rounded, NT)
    else:
        last[...] = jnp.zeros_like(last)


def term_kernel(turns, groups, mate, pos_ref, geno, samples, gram, *refs):
    packets, terms = refs[:-1], refs[-1]
    pos = pos_ref[0]
    width = terms.shape[2]
    parts = stacked3(gram[...])
    for packet, group in zip(packets, groups):
        for i, t in enumerate(group):
            term = dot(samples[...], geno[:, columns_of(pos, turns[t], mate, width)], NN)
            term -= dot3(parts, packet[i])
            terms[t] = term.astype(jnp.bfloat16)


def on_device(genotypes, sample_factors, snp_factors, coverage):
    devices = lax.axis_size("rows")
    turns = turns_of(devices)
    highs = len(turns) // 2
    position = lax.axis_index("rows").astype(jnp.int32)
    samples_here, snps_here = genotypes.shape
    rank = sample_factors.shape[1]
    covered = coverage.shape[1]
    tile_size = snps_here // covered
    per_owner = covered // devices
    own_snps = snp_factors.shape[0]
    own_blocks = own_snps // tile_size
    width = per_owner * tile_size
    assert tile_size == 64 and per_owner % 2 == 0 and own_blocks % 2 == 0
    assert devices % REST == 0 and devices & (devices - 1) == 0

    sample_step = 0.5 * math.sqrt(rank) / (covered * tile_size)

    smem = pl.BlockSpec(memory_space=pltpu.SMEM)
    vmem = pl.BlockSpec(memory_space=pltpu.VMEM)
    hbm = pl.BlockSpec(memory_space=pltpu.HBM)
    anywhere = pl.BlockSpec(memory_space=pl.ANY)
    params = pltpu.CompilerParams(vmem_limit_bytes=VMEM_LIMIT)
    pos = position.reshape(1)
    packet = jax.ShapeDtypeStruct((len(turns), rank, width), jnp.bfloat16)
    dense_blocks = pltpu.VMEM((len(turns), own_blocks, rank, 128), jnp.float32)
    by_samples = jax.ShapeDtypeStruct((rank, samples_here), jnp.float32)
    square = jax.ShapeDtypeStruct((rank, rank), jnp.float32)

    def cost(flops, bytes_accessed):
        return pl.CostEstimate(flops=flops, bytes_accessed=bytes_accessed, transcendentals=0)

    geno, samples, table = pl.pallas_call(
        functools.partial(load_kernel, turns, per_owner, own_blocks),
        out_shape=(
            pltpu.VMEM((samples_here, snps_here), jnp.bfloat16),
            pltpu.VMEM((rank, samples_here), jnp.float32),
            pltpu.SMEM((len(MATES) * len(turns), per_owner), jnp.int32),
        ),
        in_specs=[smem, hbm, hbm, hbm],
        out_specs=(vmem, vmem, smem),
        scratch_shapes=[pltpu.SMEM(coverage.shape, jnp.int32), pltpu.SemaphoreType.DMA((3,))],
        compiler_params=pltpu.CompilerParams(
            vmem_limit_bytes=58 * 1024 * 1024 - 2 * samples_here * snps_here
        ),
        cost_estimate=cost(0, 2 * samples_here * snps_here),
        name="load_batch",
    )(pos, coverage, genotypes, sample_factors.T)

    by_snps = jax.ShapeDtypeStruct((rank, own_snps), jnp.float32)
    pairwise = highs == 2
    n_steps = 2 if pairwise else 1
    snp_steps = pl.pallas_call(
        functools.partial(steps_kernel, 0.5 * math.sqrt(rank) / samples_here, own_blocks),
        out_shape=(by_snps,) * n_steps,
        in_specs=[smem, vmem],
        out_specs=(vmem,) * n_steps,
        compiler_params=params,
        name="snp_steps",
    )(pos, coverage)
    small = cost(0, 2 * 1024 * 1024)

    half_packet = jax.ShapeDtypeStruct((highs, rank, width), jnp.bfloat16)

    def pick(arrays, group, places):
        return pl.pallas_call(
            functools.partial(pick_kernel, len(turns), group, places, per_owner, own_blocks),
            out_shape=(half_packet,) * len(MATES),
            in_specs=[smem] + [vmem] * len(arrays),
            out_specs=(vmem,) * len(MATES),
            scratch_shapes=[pltpu.VMEM((highs, own_blocks, rank, 128), jnp.float32)],
            compiler_params=params,
            cost_estimate=small,
            name="pick_blocks",
        )(table, *arrays)

    def mates_sum(terms, group, dtype, after):
        return pl.pallas_call(
            functools.partial(mates_sum_kernel, len(turns), group, per_owner, own_blocks),
            out_shape=jax.ShapeDtypeStruct((len(group), rank, own_snps), dtype),
            in_specs=[smem] + [vmem] * len(MATES) + [anywhere] * len(after),
            out_specs=vmem,
            scratch_shapes=[pltpu.VMEM((len(group), own_blocks, rank, 128), jnp.float32)],
            compiler_params=params,
            cost_estimate=small,
            name="mates_sum",
        )(table, *terms, *after)

    two_snps = jax.ShapeDtypeStruct((2, rank, own_snps), jnp.bfloat16)
    add_core = pl.pallas_call(
        add_kernel,
        out_shape=(by_snps, by_snps, two_snps),
        in_specs=[vmem] * 2,
        out_specs=(vmem,) * 3,
        compiler_params=params,
        name="add_core",
    )
    owners_update = pl.pallas_call(
        update_kernel,
        out_shape=(by_snps, two_snps),
        in_specs=[vmem] * 7,
        out_specs=(vmem,) * 2,
        compiler_params=params,
        name="owners_update",
    )

    def product(mate, group, panel, before, after):
        share = samples_here * snps_here // len(MATES) // 2
        return pl.pallas_call(
            functools.partial(product_kernel, [turns[t] for t in group], mate, not before, 256),
            out_shape=(by_samples, square),
            in_specs=[smem] + [vmem] * (2 + len(before)) + [anywhere] * len(after),
            out_specs=(vmem, vmem),
            compiler_params=params,
            cost_estimate=cost(8 * rank * share, 2 * share),
            name="panel_product",
        )(pos, geno, panel, *before, *after)

    def sample_update(samples, gradient, gram, outs):
        return pl.pallas_call(
            functools.partial(sample_kernel, sample_step),
            out_shape=outs,
            in_specs=[vmem] * 3,
            out_specs=(vmem,) * len(outs),
            compiler_params=params,
            cost_estimate=small,
            name="sample_update",
        )(samples, gradient, gram)

    def terms_for(mate, samples_bf16, gram, groups, panels):
        share = samples_here * snps_here // len(MATES)
        return pl.pallas_call(
            functools.partial(term_kernel, turns, groups, mate),
            out_shape=packet,
            in_specs=[smem] + [vmem] * (3 + len(panels)),
            out_specs=vmem,
            compiler_params=params,
            cost_estimate=cost(8 * rank * share, 2 * share),
            name="mate_terms",
        )(pos, geno, samples_bf16, gram, *panels)

    def swap(x, turn):
        return lax.ppermute(x, "rows", [(r, r ^ turn) for r in range(devices)])

    def to_mate(x, mate):
        return swap(x, mate) if mate else x

    snps = snp_factors.T
    held = None
    for iteration in range(ROUNDS):
        last = iteration == ROUNDS - 1
        if held is None:
            held = {0: snps.astype(jnp.bfloat16)}
            for high in sorted(range(1, highs), key=lambda high: (high & (high - 1), -high)):
                bit = high & -high
                held[high] = swap(held[high ^ bit], bit * REST)
            groups = [list(range(highs)), list(range(highs, 2 * highs))]
            sources = {}
            for high in range(highs):
                source = held[high]
                if iteration == 0 and high:
                    source, _ = lax.optimization_barrier((source, samples))
                sources[2 * high], sources[2 * high + 1] = held[high], swap(source, 1)
            picked = [
                pick([sources[t] for t in group], group, [(i, None) for i in range(highs)]) for group in groups
            ]
        else:
            groups = [[2 * high + core for high in range(highs)] for core in (0, 1)]
            picked = [
                pick([x], group, [(0, high) for high in range(highs)])
                for x, group in zip((held, swap(held, 1)), groups)
            ]
        panels = [[to_mate(x, mate) for x, mate in zip(packets, MATES)] for packets in picked]
        partial = ()
        for g, m in ((0, 0), (0, 3), (0, 2), (0, 1), (1, 0), (1, 3), (1, 2), (1, 1)):
            after = [panels[1][0]] if (g, m) == (0, 3) else []
            partial = product(MATES[m], groups[g], panels[g][m], partial, after)
        rounded = (jax.ShapeDtypeStruct((rank, samples_here), jnp.bfloat16), square)
        if not last:
            samples, *current = sample_update(samples, *partial, (by_samples,) + rounded)
            after = []
        else:
            current = sample_update(samples, *partial, rounded)
            samples, token = sample_update(
                samples, *partial, (by_samples, jax.ShapeDtypeStruct((8, 128), jnp.float32))
            )
            after = [token]
        sent = [
            to_mate(terms_for(mate, *current, groups, [x[m] for x in panels]), mate)
            for m, mate in enumerate(MATES)
        ]
        for_core = mates_sum(sent, list(range(1, len(turns), 2)), jnp.bfloat16, after)
        arrived = swap(for_core, 1)
        sums = mates_sum(sent, list(range(0, len(turns), 2)), jnp.float32, [for_core])
        if pairwise and not last:
            own_sum, other_sum, swapped = add_core(sums, arrived)
            snps, held = owners_update(
                own_sum, other_sum, swap(swapped, REST), *snp_steps, snps, held[1]
            )
            continue
        sums = [sums[high] + arrived[high].astype(jnp.float32) for high in range(highs)]
        for high in range(highs - 1, 0, -1):
            bit = high & -high
            sums[high ^ bit] += swap(sums[high].astype(jnp.bfloat16), bit * REST).astype(jnp.float32)
        snps = (1.0 - weight_decay) * snps + snp_steps[0] * sums[0]
        held = None
    return (samples.T, snps.T)


def solution(mesh):
    placed = (
        P(("groups", "rows"), None),
        P(("groups", "rows"), None),
        P(("groups", "rows"), None),
        P("groups", None),
    )
    return jax.shard_map(
        on_device,
        mesh=mesh,
        in_specs=placed,
        out_specs=(P(("groups", "rows"), None), P(("groups", "rows"), None)),
        check_vma=False,
    )
```

```python
import functools
import math

import jax
import jax.numpy as jnp
from jax import lax
from jax.experimental import pallas as pl
from jax.experimental.pallas import tpu as pltpu
from jax.sharding import PartitionSpec as P

ROUNDS = 2

weight_decay = 0.02

MATES = (0, 2, 4, 6)
REST = 8
NT = (((1,), (1,)), ((), ()))
NN = (((1,), (0,)), ((), ()))
VMEM_LIMIT = 24 * 1024 * 1024


def dot(a, b, dims):
    return lax.dot_general(a, b, dims, preferred_element_type=jnp.float32)


def stacked3(x):
    hi = x.astype(jnp.bfloat16)
    rest = x - hi.astype(jnp.float32)
    mid = rest.astype(jnp.bfloat16)
    lo = (rest - mid.astype(jnp.float32)).astype(jnp.bfloat16)
    return jnp.concatenate([hi, mid, lo], axis=0)


def dot3(parts, b):
    products = dot(parts, b, NN)
    rows = parts.shape[0] // 3
    return products[:rows] + (products[rows:2 * rows] + products[2 * rows:])


def low_half(rows):
    return lax.broadcasted_iota(jnp.int32, (rows, 128), 1) < 64


def double(x, low):
    turned = pltpu.roll(x, 64, 1)
    return jnp.where(low, x, turned), jnp.where(low, turned, x)


def load_kernel(turns, per_owner, own_blocks, pos_ref, cov, geno, samples, geno_out, samples_out, table, listed, sems):
    copies = [
        pltpu.make_async_copy(cov, listed, sems.at[0]),
        pltpu.make_async_copy(samples, samples_out, sems.at[1]),
        pltpu.make_async_copy(geno, geno_out, sems.at[2]),
    ]
    for copy in copies:
        copy.start()
    copies[0].wait()
    for m, mate in enumerate(MATES):
        batch = lax.bitwise_xor(pos_ref[0], mate)
        for t, turn in enumerate(turns):
            owner = lax.bitwise_xor(pos_ref[0], turn)
            for p in range(per_owner):
                table[m * len(turns) + t, p] = listed[batch, owner * per_owner + p] - owner * own_blocks
    for copy in copies[1:]:
        copy.wait()


def steps_kernel(scale, own_blocks, pos_ref, cov, *steps):
    low = low_half(steps[0].shape[0])
    for turn, out in enumerate(steps):
        owner = lax.bitwise_xor(pos_ref[0], turn * REST)

        def step_of(block):
            seen = (cov[...] == owner * own_blocks + block).astype(jnp.float32)
            return scale / jnp.sum(jnp.sum(seen, axis=1, keepdims=True), axis=0, keepdims=True)

        for j in range(own_blocks // 2):
            out[:, 128 * j:128 * (j + 1)] = jnp.where(low, step_of(2 * j), step_of(2 * j + 1))


def pick_kernel(turns, group, places, per_owner, own_blocks, table, *refs):
    packets, blocks = refs[-1 - len(MATES):-1], refs[-1]
    low = low_half(blocks.shape[2])
    for i, (ref, at) in enumerate(places):
        for j in range(own_blocks // 2):
            columns = slice(128 * j, 128 * (j + 1))
            x = (refs[ref][:, columns] if at is None else refs[ref][at, :, columns]).astype(jnp.float32)
            blocks[i, 2 * j], blocks[i, 2 * j + 1] = double(x, low)
    for m in range(len(MATES)):
        for i, t in enumerate(group):
            for q in range(per_owner // 2):
                first, second = table[m * turns + t, 2 * q], table[m * turns + t, 2 * q + 1]
                pair = jnp.where(low, blocks[i, first], blocks[i, second])
                packets[m][i, :, 128 * q:128 * (q + 1)] = pair.astype(jnp.bfloat16)


def mates_sum_kernel(turns, group, per_owner, own_blocks, table, *refs):
    terms, sums, total = refs[:len(MATES)], refs[-2], refs[-1]
    low = low_half(terms[0].shape[1])
    total[...] = jnp.zeros_like(total)
    for i, t in enumerate(group):
        for m in range(len(MATES)):
            for q in range(per_owner // 2):
                first, second = table[m * turns + t, 2 * q], table[m * turns + t, 2 * q + 1]
                pair = terms[m][t, :, 128 * q:128 * (q + 1)].astype(jnp.float32)
                total[i, first] += jnp.where(low, pair, 0.0)
                total[i, second] += jnp.where(low, 0.0, pair)
    for i in range(len(group)):
        for j in range(own_blocks // 2):
            first, second = total[i, 2 * j], total[i, 2 * j + 1]
            both = jnp.where(low, first, second) + pltpu.roll(jnp.where(low, second, first), 64, 1)
            sums[i, :, 128 * j:128 * (j + 1)] = both.astype(sums.dtype)


def add_kernel(sums, arrived, own_sum, other_sum, swapped):
    own_sum[...] = sums[0] + arrived[0].astype(jnp.float32)
    other_sum[...] = sums[1] + arrived[1].astype(jnp.float32)
    swapped[0] = other_sum[...].astype(jnp.bfloat16)
    swapped[1] = own_sum[...].astype(jnp.bfloat16)


def update_kernel(own_sum, other_sum, arrived, own_step, other_step, snps, other_snps, new_snps, held):
    kept = 1.0 - weight_decay
    own_total = own_sum[...] + arrived[0].astype(jnp.float32)
    other_total = other_sum[...] + arrived[1].astype(jnp.float32)
    new_snps[...] = kept * snps[...] + own_step[...] * own_total
    held[0] = new_snps[...].astype(jnp.bfloat16)
    other = kept * other_snps[...].astype(jnp.float32) + other_step[...] * other_total
    held[1] = other.astype(jnp.bfloat16)


def turns_of(devices):
    return [high + core for high in range(0, devices, REST) for core in (0, 1)]


def columns_of(pos, turn, mate, width):
    owner = lax.bitwise_xor(pos, turn ^ mate)
    return pl.ds(pl.multiple_of(owner * width, width), width)


def product_kernel(turns, mate, first, rows, pos_ref, geno, packet, *refs):
    before, (gradient, gram) = refs[:2], refs[-2:]
    pos = pos_ref[0]
    width = packet.shape[2]
    total = None if first else before[1][...]
    for t in range(len(turns)):
        term = dot(packet[t], packet[t], NT)
        total = term if total is None else total + term
    gram[...] = total
    for r in range(geno.shape[0] // rows):
        here = slice(r * rows, (r + 1) * rows)
        total = None if first else before[0][:, here]
        for t, turn in enumerate(turns):
            term = dot(packet[t], geno[here, columns_of(pos, turn, mate, width)], NT)
            total = term if total is None else total + term
        gradient[:, here] = total


def sample_kernel(sample_step, samples, gradient, gram, *outs):
    old = samples[...]
    old_bf16 = old.astype(jnp.bfloat16)
    total = gradient[...]
    total -= dot3(stacked3(gram[...]), old_bf16)
    new = (1.0 - weight_decay) * old + sample_step * total
    *full, last = outs
    rounded = new.astype(jnp.bfloat16)
    for out in full:
        out[...] = new if out.dtype == jnp.float32 else rounded
    if last.shape[0] == last.shape[1]:
        last[...] = dot(rounded, rounded, NT)
    else:
        last[...] = jnp.zeros_like(last)


def term_kernel(turns, groups, mate, pos_ref, geno, samples, gram, *refs):
    packets, terms = refs[:-1], refs[-1]
    pos = pos_ref[0]
    width = terms.shape[2]
    parts = stacked3(gram[...])
    for packet, group in zip(packets, groups):
        for i, t in enumerate(group):
            term = dot(samples[...], geno[:, columns_of(pos, turns[t], mate, width)], NN)
            term -= dot3(parts, packet[i])
            terms[t] = term.astype(jnp.bfloat16)


def on_device(genotypes, sample_factors, snp_factors, coverage):
    devices = lax.axis_size("rows")
    turns = turns_of(devices)
    highs = len(turns) // 2
    position = lax.axis_index("rows").astype(jnp.int32)
    samples_here, snps_here = genotypes.shape
    rank = sample_factors.shape[1]
    covered = coverage.shape[1]
    tile_size = snps_here // covered
    per_owner = covered // devices
    own_snps = snp_factors.shape[0]
    own_blocks = own_snps // tile_size
    width = per_owner * tile_size
    assert tile_size == 64 and per_owner % 2 == 0 and own_blocks % 2 == 0
    assert devices % REST == 0 and devices & (devices - 1) == 0

    sample_step = 0.5 * math.sqrt(rank) / (covered * tile_size)

    smem = pl.BlockSpec(memory_space=pltpu.SMEM)
    vmem = pl.BlockSpec(memory_space=pltpu.VMEM)
    hbm = pl.BlockSpec(memory_space=pltpu.HBM)
    anywhere = pl.BlockSpec(memory_space=pl.ANY)
    params = pltpu.CompilerParams(vmem_limit_bytes=VMEM_LIMIT)
    pos = position.reshape(1)
    packet = jax.ShapeDtypeStruct((len(turns), rank, width), jnp.bfloat16)
    dense_blocks = pltpu.VMEM((len(turns), own_blocks, rank, 128), jnp.float32)
    by_samples = jax.ShapeDtypeStruct((rank, samples_here), jnp.float32)
    square = jax.ShapeDtypeStruct((rank, rank), jnp.float32)

    def cost(flops, bytes_accessed):
        return pl.CostEstimate(flops=flops, bytes_accessed=bytes_accessed, transcendentals=0)

    geno, samples, table = pl.pallas_call(
        functools.partial(load_kernel, turns, per_owner, own_blocks),
        out_shape=(
            pltpu.VMEM((samples_here, snps_here), jnp.bfloat16),
            pltpu.VMEM((rank, samples_here), jnp.float32),
            pltpu.SMEM((len(MATES) * len(turns), per_owner), jnp.int32),
        ),
        in_specs=[smem, hbm, hbm, hbm],
        out_specs=(vmem, vmem, smem),
        scratch_shapes=[pltpu.SMEM(coverage.shape, jnp.int32), pltpu.SemaphoreType.DMA((3,))],
        compiler_params=pltpu.CompilerParams(
            vmem_limit_bytes=58 * 1024 * 1024 - 2 * samples_here * snps_here
        ),
        cost_estimate=cost(0, 2 * samples_here * snps_here),
        name="load_batch",
    )(pos, coverage, genotypes, sample_factors.T)

    by_snps = jax.ShapeDtypeStruct((rank, own_snps), jnp.float32)
    pairwise = highs == 2
    n_steps = 2 if pairwise else 1
    snp_steps = pl.pallas_call(
        functools.partial(steps_kernel, 0.5 * math.sqrt(rank) / samples_here, own_blocks),
        out_shape=(by_snps,) * n_steps,
        in_specs=[smem, vmem],
        out_specs=(vmem,) * n_steps,
        compiler_params=params,
        name="snp_steps",
    )(pos, coverage)
    small = cost(0, 2 * 1024 * 1024)

    half_packet = jax.ShapeDtypeStruct((highs, rank, width), jnp.bfloat16)

    def pick(arrays, group, places):
        return pl.pallas_call(
            functools.partial(pick_kernel, len(turns), group, places, per_owner, own_blocks),
            out_shape=(half_packet,) * len(MATES),
            in_specs=[smem] + [vmem] * len(arrays),
            out_specs=(vmem,) * len(MATES),
            scratch_shapes=[pltpu.VMEM((highs, own_blocks, rank, 128), jnp.float32)],
            compiler_params=params,
            cost_estimate=small,
            name="pick_blocks",
        )(table, *arrays)

    def mates_sum(terms, group, dtype, after):
        return pl.pallas_call(
            functools.partial(mates_sum_kernel, len(turns), group, per_owner, own_blocks),
            out_shape=jax.ShapeDtypeStruct((len(group), rank, own_snps), dtype),
            in_specs=[smem] + [vmem] * len(MATES) + [anywhere] * len(after),
            out_specs=vmem,
            scratch_shapes=[pltpu.VMEM((len(group), own_blocks, rank, 128), jnp.float32)],
            compiler_params=params,
            cost_estimate=small,
            name="mates_sum",
        )(table, *terms, *after)

    two_snps = jax.ShapeDtypeStruct((2, rank, own_snps), jnp.bfloat16)
    add_core = pl.pallas_call(
        add_kernel,
        out_shape=(by_snps, by_snps, two_snps),
        in_specs=[vmem] * 2,
        out_specs=(vmem,) * 3,
        compiler_params=params,
        name="add_core",
    )
    owners_update = pl.pallas_call(
        update_kernel,
        out_shape=(by_snps, two_snps),
        in_specs=[vmem] * 7,
        out_specs=(vmem,) * 2,
        compiler_params=params,
        name="owners_update",
    )

    def product(mate, group, panel, before, after):
        share = samples_here * snps_here // len(MATES) // 2
        return pl.pallas_call(
            functools.partial(product_kernel, [turns[t] for t in group], mate, not before, 512),
            out_shape=(by_samples, square),
            in_specs=[smem] + [vmem] * (2 + len(before)) + [anywhere] * len(after),
            out_specs=(vmem, vmem),
            compiler_params=params,
            cost_estimate=cost(8 * rank * share, 2 * share),
            name="panel_product",
        )(pos, geno, panel, *before, *after)

    def sample_update(samples, gradient, gram, outs):
        return pl.pallas_call(
            functools.partial(sample_kernel, sample_step),
            out_shape=outs,
            in_specs=[vmem] * 3,
            out_specs=(vmem,) * len(outs),
            compiler_params=params,
            cost_estimate=small,
            name="sample_update",
        )(samples, gradient, gram)

    def terms_for(mate, samples_bf16, gram, groups, panels):
        share = samples_here * snps_here // len(MATES)
        return pl.pallas_call(
            functools.partial(term_kernel, turns, groups, mate),
            out_shape=packet,
            in_specs=[smem] + [vmem] * (3 + len(panels)),
            out_specs=vmem,
            compiler_params=params,
            cost_estimate=cost(8 * rank * share, 2 * share),
            name="mate_terms",
        )(pos, geno, samples_bf16, gram, *panels)

    def swap(x, turn):
        return lax.ppermute(x, "rows", [(r, r ^ turn) for r in range(devices)])

    def to_mate(x, mate):
        return swap(x, mate) if mate else x

    snps = snp_factors.T
    held = None
    for iteration in range(ROUNDS):
        last = iteration == ROUNDS - 1
        if held is None:
            held = {0: snps.astype(jnp.bfloat16)}
            for high in sorted(range(1, highs), key=lambda high: (high & (high - 1), -high)):
                bit = high & -high
                held[high] = swap(held[high ^ bit], bit * REST)
            groups = [list(range(highs)), list(range(highs, 2 * highs))]
            sources = {}
            for high in range(highs):
                source = held[high]
                if iteration == 0 and high:
                    source, _ = lax.optimization_barrier((source, samples))
                sources[2 * high], sources[2 * high + 1] = held[high], swap(source, 1)
            picked = [
                pick([sources[t] for t in group], group, [(i, None) for i in range(highs)]) for group in groups
            ]
        else:
            groups = [[2 * high + core for high in range(highs)] for core in (0, 1)]
            picked = [
                pick([x], group, [(0, high) for high in range(highs)])
                for x, group in zip((held, swap(held, 1)), groups)
            ]
        panels = [[to_mate(x, mate) for x, mate in zip(packets, MATES)] for packets in picked]
        partial = ()
        for g, m in ((0, 0), (0, 3), (0, 2), (0, 1), (1, 0), (1, 3), (1, 2), (1, 1)):
            after = [panels[1][0]] if (g, m) == (0, 3) else []
            partial = product(MATES[m], groups[g], panels[g][m], partial, after)
        rounded = (jax.ShapeDtypeStruct((rank, samples_here), jnp.bfloat16), square)
        if not last:
            samples, *current = sample_update(samples, *partial, (by_samples,) + rounded)
            after = []
        else:
            current = sample_update(samples, *partial, rounded)
            samples, token = sample_update(
                samples, *partial, (by_samples, jax.ShapeDtypeStruct((8, 128), jnp.float32))
            )
            after = [token]
        sent = [
            to_mate(terms_for(mate, *current, groups, [x[m] for x in panels]), mate)
            for m, mate in enumerate(MATES)
        ]
        for_core = mates_sum(sent, list(range(1, len(turns), 2)), jnp.bfloat16, after)
        arrived = swap(for_core, 1)
        sums = mates_sum(sent, list(range(0, len(turns), 2)), jnp.float32, [for_core])
        if pairwise and not last:
            own_sum, other_sum, swapped = add_core(sums, arrived)
            snps, held = owners_update(
                own_sum, other_sum, swap(swapped, REST), *snp_steps, snps, held[1]
            )
            continue
        sums = [sums[high] + arrived[high].astype(jnp.float32) for high in range(highs)]
        for high in range(highs - 1, 0, -1):
            bit = high & -high
            sums[high ^ bit] += swap(sums[high].astype(jnp.bfloat16), bit * REST).astype(jnp.float32)
        snps = (1.0 - weight_decay) * snps + snp_steps[0] * sums[0]
        held = None
    return (samples.T, snps.T)


def solution(mesh):
    placed = (
        P(("groups", "rows"), None),
        P(("groups", "rows"), None),
        P(("groups", "rows"), None),
        P("groups", None),
    )
    return jax.shard_map(
        on_device,
        mesh=mesh,
        in_specs=placed,
        out_specs=(P(("groups", "rows"), None), P(("groups", "rows"), None)),
        check_vma=False,
    )
```
